32 devices in a mesh: grp: 2 (over core), dp: 16 (over z, y, x).
Axes of the slice: x: 2, y: 2, z: 4, core: 2. Of those that a mesh axis runs over, the one named last changes fastest.
Arguments:
- obs_rows: bfloat16 [102400, 376], P('dp'), may hold values from -6 to 6
- next_rows: bfloat16 [102400, 376], P('dp'), may hold values from -6 to 6
- action_rows: float32 [102400, 17], P('dp'), may hold values from -0.95 to 0.95
- reward_rows: float32 [102400], P('dp'), may hold values from -5 to 5
- batch_index: int32 [102400], P('dp'), may hold values from 0 to 6399
- valid_mask: int32 [102400], P('dp'), may hold values from 0 to 1
- noise: float32 [102400, 35], P('dp'), may hold values from -5 to 5
- importance: float32 [102400], P('dp'), may hold values from 0.1 to 5
- actor_params: float32 [2, 171042], P('grp'), may hold values from -2 to 2
- critic_params: float32 [2, 167170], P('grp'), may hold values from -2 to 2
- actor_stats: float32 [1980], replicated, as said below
- critic_stats: float32 [1933], replicated, as said below
- log_alpha: float32 [1], replicated, may hold values from -2 to -0.5
Outputs:
- actor_new: float32 [2, 171042], P('grp')
- critic_new: float32 [2, 167170], P('grp')
- actor_copy: bfloat16 [2, 171042], P('grp')
- critic_copy: bfloat16 [2, 167170], P('grp')
- actor_grad: float32 [171042], replicated
- critic_grad: float32 [167170], replicated
- actor_stats_new: float32 [1980], replicated
- critic_stats_new: float32 [1933], replicated
- summary: float32 [3], replicated
- log_alpha_new: float32 [1], replicated
The draws below stay inside these ranges and needn't reach their ends.
Inputs may be any that keep to these rules, and one draw needn't show every extreme that they name: `actor_stats`: positive. `critic_stats`: positive.
All inputs are finite; a program needn't handle non-finite values.
Results may differ from the reference program's by a relative error of at most 0.001.
Values sent between devices are 32-bit elements; how exact they have to be, the bound alone decides.
No kernel may reach another device: no remote copies, remote signals or barrier semaphores. Data moves between devices by JAX's collectives and lax.ppermute only.
A program may use at most 256 MiB of HBM per device.

```python
import math
import jax
import jax.numpy as jnp
from jax import lax

OBS = 376
ACT = 17
HID = 256
BATCH_DEV = 6400
ROWS_DEV = 6400
BATCH = 102400
ROWS = 102400
SA = 1980
SC = 1933


def layered(key, layout):
    subkeys = jax.random.split(key, 2 * len(layout))
    pieces = []
    for position, shape_pair in enumerate(layout):
        height = shape_pair[0]
        breadth = shape_pair[1]
        normal_part = jnp.clip(jax.random.normal(subkeys[position], (2, height * breadth), jnp.float32), -6.0, 6.0)
        pieces.append(normal_part * height ** (-0.5))
    for position, shape_pair in enumerate(layout):
        breadth = shape_pair[1]
        normal_part = jnp.clip(jax.random.normal(subkeys[len(layout) + position], (2, breadth), jnp.float32), -6.0, 6.0)
        pieces.append(0.05 * normal_part)
    return jnp.concatenate(pieces, axis=1)


def draw_actor_params(key, part):
    key = jax.random.fold_in(key, 11)
    return layered(key, [(OBS, HID), (HID, HID), (HID, 2 * ACT)])


def draw_critic_params(key, part):
    key = jax.random.fold_in(key, 12)
    return layered(key, [(OBS + ACT, HID), (HID, HID), (HID, 2)])


def draw_actor_stats(key, part):
    key = jax.random.fold_in(key, 13)
    return jnp.exp(jax.random.uniform(key, (SA,), jnp.float32, math.log(0.03), math.log(0.15))) / BATCH


def draw_critic_stats(key, part):
    key = jax.random.fold_in(key, 14)
    return jnp.exp(jax.random.uniform(key, (SC,), jnp.float32, math.log(0.5), math.log(2.5))) / BATCH


def draw_valid_mask(key, part):
    key = jax.random.fold_in(key, 15)
    shard_of = jnp.arange(BATCH, dtype=jnp.int32) // BATCH_DEV
    shards = BATCH // BATCH_DEV
    level = 250 + 500 * shard_of // (shards - 1)
    return (jax.random.randint(key, (BATCH,), 0, 1000) < level).astype(jnp.int32)


def draw_importance(key, part):
    key = jax.random.fold_in(key, 16)
    shard_of = jnp.arange(BATCH, dtype=jnp.int32) // BATCH_DEV
    ramp = shard_of.astype(jnp.float32) / (BATCH // BATCH_DEV - 1)
    return jnp.exp(jax.random.uniform(key, (BATCH,), jnp.float32, math.log(0.1), 0.0)) * (1.0 + 2.0 * ramp)


def plant(values, stream_key, least, high):
    spot = [jax.random.randint(jax.random.fold_in(stream_key, axis), (), 0, length) for axis, length in enumerate(values.shape)]
    main_axis = values.shape.index(max(values.shape))
    neighbour = spot[:main_axis] + [(spot[main_axis] + 1) % values.shape[main_axis]] + spot[main_axis + 1:]
    return values.at[tuple(spot)].set(least).at[tuple(neighbour)].set(high)


def level_of(key, dims, cuts, least, top_value):
    def one(dim, parts):
        draws = jax.random.uniform(jax.random.fold_in(jax.random.fold_in(key, 6), dim), (parts,), jnp.float32, least / len(cuts), top_value / len(cuts))
        return jnp.repeat(jnp.exp(draws), dims[dim] // parts).reshape((-1,) + (1,) * (len(dims) - dim - 1))

    factor_of = one(*cuts[0])
    for cut in cuts[1:]:
        factor_of = factor_of * one(*cut)
    return factor_of


def centred(stream_key, shape, deviation, most, cuts=(), held_as=jnp.bfloat16):
    loudness = level_of(stream_key, shape, cuts, -0.22, 0.18) if cuts else 1.0
    drawn = jax.random.normal(stream_key, shape, jnp.float32) * deviation * loudness
    return jnp.minimum(jnp.maximum(drawn, -most), most).astype(held_as)


def setup_inputs(seed: int = 0) -> dict:
    splits = jax.random.split(jax.random.key(seed), 14)
    obs_rows = centred(splits[0], (ROWS, OBS), 1.0, 6.0, ((0, 16),))
    next_rows = centred(splits[1], (ROWS, OBS), 1.0, 6.0, ((0, 16),))
    action_rows = jnp.clip(jax.random.uniform(splits[2], (ROWS, ACT), jnp.float32, -0.95, 0.95) * level_of(splits[2], (ROWS, ACT), ((0, 16),), -0.4, 0.0), -0.95, 0.95)
    reward_rows = centred(splits[3], (ROWS,), 1.0, 5.0, ((0, 16),), jnp.float32)
    batch_index = plant(jax.random.randint(splits[4], (BATCH,), 0, ROWS_DEV), jax.random.fold_in(splits[4], 1), 0, ROWS_DEV - 1).astype(jnp.int32)
    valid_mask = draw_valid_mask(jax.random.fold_in(splits[13], 71), 0)
    noise = centred(splits[6], (BATCH, 2 * ACT + 1), 1.0, 5.0, ((0, 16),), jnp.float32)
    importance = draw_importance(jax.random.fold_in(splits[13], 71), 0)
    actor_params = draw_actor_params(jax.random.fold_in(splits[13], 71), 0)
    critic_params = draw_critic_params(jax.random.fold_in(splits[13], 71), 0)
    actor_stats = draw_actor_stats(jax.random.fold_in(splits[13], 71), 0)
    critic_stats = draw_critic_stats(jax.random.fold_in(splits[13], 71), 0)
    log_alpha = jnp.clip(jax.random.uniform(splits[12], (1,), jnp.float32, -2.0, -0.5), -2.0, -0.5)
    return dict(obs_rows=obs_rows, next_rows=next_rows, action_rows=action_rows, reward_rows=reward_rows, batch_index=batch_index, valid_mask=valid_mask, noise=noise, importance=importance, actor_params=actor_params, critic_params=critic_params, actor_stats=actor_stats, critic_stats=critic_stats, log_alpha=log_alpha)


@jax.custom_vjp
def low(v):
    return lax.optimization_barrier(v.astype(jnp.bfloat16)).astype(jnp.float32)

@jax.custom_vjp
def low_back(v):
    return v

def low_keep(v):
    return (low(v), None)

def low_pass(kept, grad):
    return (grad,)

def back_keep(v):
    return (v, None)

def back_low(kept, grad):
    return (low(grad),)
low.defvjp(low_keep, low_pass)
low_back.defvjp(back_keep, back_low)
DISCOUNT = 0.99
POLYAK_RATE = 0.1
DECAY_RATE = 0.5
LEARN_RATE = 0.1
CLIP_LEVEL = 0.1
ALPHA_STEP = 0.01
TINY_TERM = 1e-30
HALF_LOG_TWO_PI = 0.9189385332046727
LOG_TWO = 0.6931471805599453

def project(inputs, matrix):
    return jnp.dot(inputs, matrix, precision=lax.Precision.HIGHEST, preferred_element_type=jnp.float32)

def layout_of(width_in, width_out):
    return [(width_in, HID), (HID, HID), (HID, width_out)]

def unpack(flat_params, layout):
    pieces = []
    offset = 0
    for height, breadth in layout:
        pieces.append(flat_params[offset:offset + height * breadth].reshape(height, breadth))
        offset += height * breadth
    for height, breadth in layout:
        pieces.append(flat_params[offset:offset + breadth])
        offset += breadth
    return pieces

def network(pieces, inputs):
    weight_one, weight_two, weight_three, bias_one, bias_two, bias_three = pieces
    hidden = jax.nn.gelu(project(inputs, weight_one) + bias_one, approximate=False)
    hidden = jax.nn.gelu(project(hidden, weight_two) + bias_two, approximate=False)
    return project(hidden, weight_three) + bias_three

def policy(flat_params, states, shocks):
    output = network(unpack(flat_params, layout_of(OBS, 2 * ACT)), states)
    centre = output[:, :ACT]
    spread = jax.nn.softplus(output[:, ACT:]) + 0.05
    pre_tanh = centre + spread * shocks
    log_terms = -0.5 * shocks * shocks - jnp.log(spread) - HALF_LOG_TWO_PI - 2.0 * (LOG_TWO - pre_tanh - jax.nn.softplus(-2.0 * pre_tanh))
    return (jnp.tanh(pre_tanh), lax.optimization_barrier(jnp.sum(log_terms, axis=1)))

def critic(flat_params, states, action):
    output = network(unpack(flat_params, layout_of(OBS + ACT, 2)), jnp.concatenate([states, action], axis=1))
    return (output[:, 0], jax.nn.softplus(output[:, 1]) + 0.1)

def clipped(update):
    return update / jnp.maximum(1.0, jnp.sqrt(jnp.mean(update * update)) / CLIP_LEVEL)

def adafactor(flat_params, gradient, statistics, layout):
    renewed = []
    row_parts = []
    col_parts = []
    offset = 0
    row_at = 0
    col_at = sum((height for height, breadth in layout))
    for height, breadth in layout:
        extent = height * breadth
        matrix_grad = gradient[offset:offset + extent].reshape(height, breadth)
        square = matrix_grad * matrix_grad + TINY_TERM
        row_stat = DECAY_RATE * statistics[row_at:row_at + height] + (1.0 - DECAY_RATE) * lax.optimization_barrier(jnp.mean(square, axis=1))
        col_stat = DECAY_RATE * statistics[col_at:col_at + breadth] + (1.0 - DECAY_RATE) * lax.optimization_barrier(jnp.mean(square, axis=0))
        second = row_stat[:, None] * col_stat[None, :] / jnp.mean(row_stat)
        update = clipped(matrix_grad * lax.rsqrt(second))
        renewed.append(flat_params[offset:offset + extent] - LEARN_RATE * update.reshape(-1))
        row_parts.append(row_stat)
        col_parts.append(col_stat)
        offset += extent
        row_at += height
        col_at += breadth
    bias_grad = gradient[offset:]
    bias_stat = DECAY_RATE * statistics[col_at:] + (1.0 - DECAY_RATE) * (bias_grad * bias_grad + TINY_TERM)
    renewed.append(flat_params[offset:] - LEARN_RATE * clipped(bias_grad * lax.rsqrt(bias_stat)))
    return (jnp.concatenate(renewed), jnp.concatenate(row_parts + col_parts + [bias_stat]))

def reference(obs_rows, next_rows, action_rows, reward_rows, batch_index, valid_mask, noise, importance, actor_params, critic_params, actor_stats, critic_stats, log_alpha):
    shard_of = (jnp.arange(BATCH, dtype=jnp.int32) // BATCH_DEV).astype(jnp.int32)
    picked = (shard_of * ROWS_DEV + batch_index).astype(jnp.int32)
    states = obs_rows[picked].astype(jnp.float32)
    next_states = next_rows[picked].astype(jnp.float32)
    action = action_rows[picked]
    reward = reward_rows[picked]
    temper = jnp.exp(log_alpha[0])
    next_action, next_logp = policy(actor_params[0], next_states, noise[:, :ACT])
    next_mean, next_spread = critic(critic_params[0], next_states, next_action)
    target = reward + DISCOUNT * (next_mean + next_spread * noise[:, 2 * ACT] - temper * next_logp)
    online_actor = actor_params[1]
    online_critic = critic_params[1]
    fixed_mean, fixed_spread = critic(online_critic, states, action)
    bounded = fixed_mean + jnp.clip(target - fixed_mean, -3.0 * fixed_spread, 3.0 * fixed_spread)
    counted = valid_mask.astype(jnp.float32)
    counted_total = jnp.sum(counted)
    weight = counted * importance / jnp.max(importance)

    def critic_loss(flat_params):
        q_value, spread = critic(flat_params, states, action)
        neg_loglik = 0.5 * (target - q_value) ** 2 / fixed_spread ** 2 + 0.5 * (bounded - fixed_mean) ** 2 / spread ** 2 + jnp.log(spread)
        return jnp.sum(weight * neg_loglik)
    critic_sum, pull_back = jax.vjp(critic_loss, online_critic)
    critic_grad = pull_back(jnp.ones((), jnp.float32))[0] / counted_total

    def actor_loss(flat_params):
        new_action, logp = policy(flat_params, states, noise[:, ACT:2 * ACT])
        q_value, spread = critic(online_critic, states, new_action)
        return (jnp.sum(counted * (temper * logp - q_value)), jnp.sum(counted * logp))
    actor_sum, pull_actor, logp_sum = jax.vjp(actor_loss, online_actor, has_aux=True)
    actor_grad = pull_actor(jnp.ones((), jnp.float32))[0] / counted_total
    new_log_alpha = log_alpha[0] + ALPHA_STEP * (logp_sum / counted_total - ACT)
    actor_online, actor_state = adafactor(online_actor, actor_grad, actor_stats, layout_of(OBS, 2 * ACT))
    critic_online, critic_state = adafactor(online_critic, critic_grad, critic_stats, layout_of(OBS + ACT, 2))
    actor_new = jnp.stack([POLYAK_RATE * actor_online + (1.0 - POLYAK_RATE) * actor_params[0], actor_online])
    critic_new = jnp.stack([POLYAK_RATE * critic_online + (1.0 - POLYAK_RATE) * critic_params[0], critic_online])
    summary = jnp.stack([critic_sum, actor_sum, counted_total])
    return (actor_new, critic_new, actor_new.astype(jnp.bfloat16), critic_new.astype(jnp.bfloat16), actor_grad, critic_grad, actor_state, critic_state, summary, jnp.reshape(new_log_alpha, (1,)))
```

```python
import jax
import jax.numpy as jnp
from jax import lax
from jax.experimental import pallas as pl
from jax.experimental.pallas import tpu as pltpu
from jax.sharding import PartitionSpec as P

OBS = 376
ACT = 17
HID = 256
LANES = 128
TILE = 256

DISCOUNT = 0.99
POLYAK_RATE = 0.1
DECAY_RATE = 0.5
LEARN_RATE = 0.1
CLIP_LEVEL = 0.1
ALPHA_STEP = 0.01
TINY_TERM = 1e-30
HALF_LOG_TWO_PI = 0.9189385332046727
LOG_TWO = 0.6931471805599453
ROOT_HALF = 0.7071067811865476
INV_ROOT_TWO_PI = 0.3989422804014327
HALF_LOG2_E = 0.7213475204444817

F32 = jnp.float32
BF16 = jnp.bfloat16
VMEM_BYTES = 60 * 2**20

ONE_LANE = OBS
AUX_LOW = 32
AUX_REWARD = 64
AUX_ROWS = 72


def flat_rows(width_in, width_out):
    w2 = width_in * HID // LANES
    w3 = w2 + HID * HID // LANES
    b1 = w3 + HID * width_out // LANES
    return w2, w3, b1, b1 + 2, b1 + 4


A_ROWS = flat_rows(OBS, 2 * ACT)
C_ROWS = flat_rows(OBS + ACT, 2)
A_SIZE = A_ROWS[4] * LANES + 2 * ACT
C_SIZE = C_ROWS[4] * LANES + 2
A_FLAT = -(-A_SIZE // 1024) * 8
C_FLAT = -(-C_SIZE // 1024) * 8

A_W1 = (0, OBS)
A_W2 = (2 * OBS, 2 * OBS + HID)
A_W3 = (2 * OBS + 2 * HID, 2 * OBS + 2 * HID + 40)
A_B = A_W3[1] + 40
C_W1 = (A_B + 8, A_B + 8 + 400)
C_W2 = (C_W1[1] + 400, C_W1[1] + 400 + HID)
C_W3 = (C_W2[1] + HID, C_W2[1] + HID + 8)
C_B = C_W3[1] + 8
EXTRA = C_B + 8
EXTRA_SLOTS = EXTRA + 4
DATA_ROWS = EXTRA + 8


def nn(left, right):
    return lax.dot_general(
        left, right, (((1,), (0,)), ((), ())), preferred_element_type=F32
    )


def nt(left, right):
    return lax.dot_general(
        left, right, (((1,), (1,)), ((), ())), preferred_element_type=F32
    )


def exact_nn(left, right):
    return lax.dot_general(
        left,
        right,
        (((1,), (0,)), ((), ())),
        precision=lax.Precision.HIGHEST,
        preferred_element_type=F32,
    )


def split(value):
    high = value.astype(BF16)
    return high, (value - high.astype(F32)).astype(BF16)


def gelu(z):
    return ((0.5 * z) * (1.0 + lax.erf(z * ROOT_HALF))).astype(BF16)


def gelu_pair(z):
    cdf = 0.5 + 0.5 * lax.erf(z * ROOT_HALF)
    bell = jnp.exp2(z * z * (-HALF_LOG2_E))
    return (z * cdf).astype(BF16), cdf + (z * INV_ROOT_TWO_PI) * bell


def softplus(x):
    return jnp.maximum(x, 0.0) + jnp.log(1.0 + jnp.exp(-jnp.abs(x)))


def softplus_pair(x):
    decay = jnp.exp(-jnp.abs(x))
    inverse = 1.0 / (1.0 + decay)
    return jnp.maximum(x, 0.0) + jnp.log(1.0 + decay), jnp.where(x >= 0.0, inverse, decay * inverse)


def column(row):
    return jnp.broadcast_to(row, (LANES, LANES)).T


def rows_of(count):
    return lax.broadcasted_iota(jnp.int32, (count, LANES), 0)


def lanes_of(count):
    return lax.broadcasted_iota(jnp.int32, (count, LANES), 1)


def one_hot_rows(width, rows, later):
    owner = lax.broadcasted_iota(jnp.int32, (rows, HID), 1) * width // LANES + later
    return (owner == lax.broadcasted_iota(jnp.int32, (rows, HID), 0)).astype(F32)


def rotate_rows(value, shift):
    for bit in range(7):
        step = 1 << bit
        value = jnp.where((shift & step) != 0, pltpu.roll(value, step, 1), value)
    return value


def unflatten(flat, width):
    rows = flat.shape[0]
    offset = (rows_of(HID) * width) % LANES
    first = exact_nn(one_hot_rows(width, rows, 0).T, flat)
    second = exact_nn(one_hot_rows(width, rows, 1).T, flat)
    mixed = jnp.where(lanes_of(HID) >= offset, first, second)
    return rotate_rows(mixed, (LANES - offset) % LANES)


def flatten(value, width, rows):
    offset = (rows_of(HID) * width) % LANES
    turned = rotate_rows(value, offset)
    here = lanes_of(HID) >= offset
    return exact_nn(one_hot_rows(width, rows, 0), jnp.where(here, turned, 0.0)) + exact_nn(
        one_hot_rows(width, rows, 1), jnp.where(here, 0.0, turned)
    )


def gather_kernel(
    blocks, block, picks, obs, nxt, act, misc, states, nexts, aux, table, got, wide
):
    step = pl.program_id(0)
    groups = block // 8
    table3 = table.reshape(table.shape[0] // 64, 64, LANES)

    @pl.when(step == 0)
    def _():
        wide[...] = jnp.zeros_like(wide)

    @pl.when(step < blocks)
    def _():
        ones = (lax.broadcasted_iota(jnp.int32, (8, block), 0) == 0).astype(F32)
        at = pl.multiple_of(step * groups, groups)

        def put(value, first):
            for c in range(value.shape[1] // LANES):
                table3[pl.ds(at, groups), 8 * (first + c) : 8 * (first + c) + 8, :] = value[
                    :, LANES * c : LANES * (c + 1)
                ].reshape(groups, 8, LANES)

        put(jnp.concatenate([obs[...].astype(F32), ones], axis=0).T, 0)
        put(jnp.concatenate([nxt[...].astype(F32), ones], axis=0).T, 3)
        action = act[...]
        high = action.astype(BF16).astype(F32)
        wide[0:ACT, :] = high
        wide[AUX_LOW : AUX_LOW + ACT, :] = action - high
        wide[AUX_REWARD : AUX_REWARD + 8, :] = misc[...]
        put(wide[...].T, 6)

    @pl.when(step >= blocks)
    def _():
        tile = step - blocks
        batch = 32

        def fetch(b, carry):
            found = []
            for j in range(batch):
                at = picks[tile * TILE + b * batch + j]
                found.append(table[pl.ds(at, 8, stride=8), :])
            for j in range(batch):
                to = b * (batch * 8) + (j // 8) * 64 + j % 8
                got[pl.ds(to, 8, stride=8), :] = found[j]
            return carry

        lax.fori_loop(0, TILE // batch, fetch, 0)
        got3 = got.reshape(TILE // 8, 64, LANES)

        def chunk(c):
            return got3[:, 8 * c : 8 * c + 8, :].reshape(TILE, LANES)

        for c in range(3):
            states[:, LANES * c : LANES * (c + 1)] = chunk(c).astype(BF16)
            nexts[:, LANES * c : LANES * (c + 1)] = chunk(3 + c).astype(BF16)
        extra = chunk(6)
        states[:, 3 * LANES :] = extra.astype(BF16)
        aux[...] = extra.T[0:AUX_ROWS, :]


def gather(picks, obs, nxt, act, misc, padded):
    rows = obs.shape[1]
    block = 640
    blocks = rows // block

    def source(i, picks):
        return (0, jnp.minimum(i, blocks - 1))

    def target(i, picks):
        return (jnp.maximum(i - blocks, 0), 0)

    def target_t(i, picks):
        return (0, jnp.maximum(i - blocks, 0))

    def body(*refs):
        gather_kernel(blocks, block, *refs)

    return pl.pallas_call(
        body,
        out_shape=(
            jax.ShapeDtypeStruct((padded, 512), BF16),
            jax.ShapeDtypeStruct((padded, 384), BF16),
            jax.ShapeDtypeStruct((AUX_ROWS, padded), F32),
        ),
        grid_spec=pltpu.PrefetchScalarGridSpec(
            num_scalar_prefetch=1,
            grid=(blocks + padded // TILE,),
            in_specs=[
                pl.BlockSpec((OBS, block), source),
                pl.BlockSpec((OBS, block), source),
                pl.BlockSpec((ACT, block), source),
                pl.BlockSpec((8, block), source),
            ],
            out_specs=(
                pl.BlockSpec((TILE, 512), target),
                pl.BlockSpec((TILE, 384), target),
                pl.BlockSpec((AUX_ROWS, TILE), target_t),
            ),
            scratch_shapes=[
                pltpu.VMEM((rows * 8, LANES), F32),
                pltpu.VMEM((TILE * 8, LANES), F32),
                pltpu.VMEM((LANES, block), F32),
            ],
        ),
        compiler_params=pltpu.CompilerParams(
            dimension_semantics=("arbitrary",), vmem_limit_bytes=VMEM_BYTES
        ),
        name="gather_rows",
    )(picks, obs, nxt, act, misc)


def copy_flat(flat, source):
    size = source.shape[1]
    whole = size // 1024

    def body(k, carry):
        flat[pl.ds(pl.multiple_of(k * 8, 8), 8), :] = source[
            0:1, pl.ds(pl.multiple_of(k * 1024, 1024), 1024)
        ].reshape(8, LANES)
        return carry

    lax.fori_loop(0, whole, body, 0)
    flat[8 * whole : 8 * whole + 8, :] = jnp.zeros((8, LANES), F32)
    full = (size - whole * 1024) // LANES
    for k in range(full):
        flat[8 * whole + k : 8 * whole + k + 1, :] = source[
            0:1, whole * 1024 + k * LANES : whole * 1024 + (k + 1) * LANES
        ]
    rest = size - whole * 1024 - full * LANES
    flat[8 * whole + full : 8 * whole + full + 1, 0:rest] = source[0:1, size - rest : size]


def halves(flat, start, height):
    return [flat[pl.ds(start + side, height, stride=2), :] for side in (0, 1)]


def first_layer(flat, rows, dst_high, dst_low, base):
    tops = halves(flat, 0, OBS)
    for side in (0, 1):
        bias = flat[rows[2] + side : rows[2] + side + 1, :]
        pad = jnp.where(rows_of(8) == 0, jnp.broadcast_to(bias, (8, LANES)), 0.0)
        high, low = split(jnp.concatenate([tops[side], pad], axis=0).T)
        at = base + side * LANES
        dst_high[at : at + LANES, 0:384] = high
        if dst_low is not None:
            dst_low[at : at + LANES, 0:384] = low


def action_layer(flat, square, stack, in_high, in_low, back):
    lane = lanes_of(LANES)
    tops = halves(flat, 2 * OBS, ACT)
    for side in (0, 1):
        at = side * LANES
        square[...] = jnp.zeros_like(square)
        for part in range(3):
            square[32 * part : 32 * part + ACT, :] = tops[side]
        high, low = split(square[...].T)
        stack[at : at + LANES, :] = jnp.where(lane < 64, high.astype(F32), low.astype(F32)).astype(
            BF16
        )
        if in_high is not None:
            in_high[at : at + LANES, 384:512] = jnp.where(
                lane < 64, high.astype(F32), 0.0
            ).astype(BF16)
            in_low[at : at + LANES, 384:512] = jnp.where(lane < 32, low.astype(F32), 0.0).astype(
                BF16
            )
            high, low = split(square[0:32, :])
            back[0:32, at : at + LANES] = high
            back[32:64, at : at + LANES] = low


def second_layer(flat, rows, forward_high, forward_low, back_high, back_low, bias):
    tops = halves(flat, rows[0], HID)
    for side in (0, 1):
        at = side * LANES
        high, low = split(tops[side].T)
        forward_high[at : at + LANES, :] = high
        if forward_low is not None:
            forward_low[at : at + LANES, :] = low
            high, low = split(tops[side])
            back_high[:, at : at + LANES] = high
            back_low[:, at : at + LANES] = low
        bias[at : at + LANES, :] = column(flat[rows[3] + side : rows[3] + side + 1, :])


def actor_head(flat, rows, forward, bias, back, tall):
    wide = unflatten(flat[rows[1] : rows[1] + 72, :], 2 * ACT).T
    tall[...] = jnp.zeros_like(tall)
    tall[0:ACT, :] = wide[0:ACT, :]
    tall[24 : 24 + ACT, :] = wide[ACT : 2 * ACT, :]
    tall[48:96, :] = tall[0:48, :]
    tall[96:144, :] = tall[0:48, :]
    high, low = split(tall[0:48, :])
    forward[0:48, :] = high
    forward[48:96, :] = low
    if back is not None:
        high, low = split(tall[...].T)
        lane = lax.broadcasted_iota(jnp.int32, (HID, HID), 1)
        back[...] = jnp.where(lane < 96, high.astype(F32), low.astype(F32)).astype(BF16)
    heads = column(flat[rows[4] : rows[4] + 1, :])
    bias[0:24, :] = heads[0:24, :]
    bias[24:48, :] = jnp.concatenate([heads[ACT : ACT + 24, :]], axis=0)


def critic_head(flat, rows, forward, bias, back, small):
    wide = unflatten(flat[rows[1] : rows[1] + 8, :], 2).T
    small[...] = jnp.zeros_like(small)
    small[0:2, :] = wide[0:2, :]
    high, low = split(small[...])
    forward[0:16, :] = high
    forward[16:32, :] = low
    if back is not None:
        for k in (0, 1):
            for side in (0, 1):
                back[side * LANES : (side + 1) * LANES, k * LANES : (k + 1) * LANES] = column(
                    wide[k : k + 1, side * LANES : (side + 1) * LANES]
                )
    bias[...] = column(flat[rows[4] : rows[4] + 1, :])[0:8, :]


def spread_lanes(bias):
    return jnp.concatenate([bias, bias], axis=1)


def policy_parts(out, shocks):
    centre = out[0:ACT, :]
    raw = out[24 : 24 + ACT, :]
    soft, slope = softplus_pair(raw)
    spread = soft + 0.05
    pre = centre + spread * shocks
    terms = (
        -0.5 * shocks * shocks
        - jnp.log(spread)
        - HALF_LOG_TWO_PI
        - 2.0 * (LOG_TWO - pre - softplus(-2.0 * pre))
    )
    return jnp.tanh(pre), jnp.sum(terms, axis=0, keepdims=True), spread, slope


def stacked_action(value, pad):
    tall = jnp.concatenate([value, pad], axis=0)
    high, low = split(tall)
    return jnp.concatenate([high, low, high, jnp.zeros_like(high)], axis=0)


def loss_kernel(
    tiles, half, chunk,
    meta, log_alpha, states, nexts, aux, noise_l, noise_r, misc_l, misc_r,
    own_actor, other_actor, own_critic, other_critic,
    keep, send,
    flat_ta, flat_oa, flat_tc, flat_oc,
    w1_t, w1a_h, w1a_l, w1c_h, w1c_l, wa_t, wa_o, wa_back,
    w2_ta, w2_tc, w2a_h, w2a_l, w2c_h, w2c_l, w2a_bh, w2a_bl, w2c_bh, w2c_bl,
    bias2, w3_ta, w3_oa, w3_tc, w3_oc, w3a_back, w3c_back, bias3_ta, bias3_oa, bias3_tc, bias3_oc,
    square, tall, small,
    g1a, g1c, g2a, g2c, g3a, g3c, gb2a, gb2c, gb3a, gb3c, sums, total,
):
    step = pl.program_id(0)

    @pl.when(step == 0)
    def _():
        @pl.when(meta[0] == 0)
        def _():
            copy_flat(flat_ta, own_actor)
            copy_flat(flat_oa, other_actor)
            copy_flat(flat_tc, own_critic)
            copy_flat(flat_oc, other_critic)

        @pl.when(meta[0] != 0)
        def _():
            copy_flat(flat_ta, other_actor)
            copy_flat(flat_oa, own_actor)
            copy_flat(flat_tc, other_critic)
            copy_flat(flat_oc, own_critic)

        first_layer(flat_ta, A_ROWS, w1_t, None, 0)
        first_layer(flat_tc, C_ROWS, w1_t, None, HID)
        first_layer(flat_oa, A_ROWS, w1a_h, w1a_l, 0)
        first_layer(flat_oc, C_ROWS, w1c_h, w1c_l, 0)
        action_layer(flat_tc, square, wa_t, None, None, None)
        action_layer(flat_oc, square, wa_o, w1c_h, w1c_l, wa_back)
        second_layer(flat_ta, A_ROWS, w2_ta, None, None, None, bias2.at[0])
        second_layer(flat_tc, C_ROWS, w2_tc, None, None, None, bias2.at[1])
        second_layer(flat_oa, A_ROWS, w2a_h, w2a_l, w2a_bh, w2a_bl, bias2.at[2])
        second_layer(flat_oc, C_ROWS, w2c_h, w2c_l, w2c_bh, w2c_bl, bias2.at[3])
        actor_head(flat_ta, A_ROWS, w3_ta, bias3_ta, None, tall)
        actor_head(flat_oa, A_ROWS, w3_oa, bias3_oa, w3a_back, tall)
        critic_head(flat_tc, C_ROWS, w3_tc, bias3_tc, None, small)
        critic_head(flat_oc, C_ROWS, w3_oc, bias3_oc, w3c_back, small)
        for ref in (g1a, g1c, g2a, g2c, g3a, g3c, gb2a, gb2c, gb3a, gb3c, sums):
            ref[...] = jnp.zeros_like(ref)

    alpha = jnp.exp(jnp.full((1, TILE), log_alpha[0], F32))
    place = step * TILE + lax.broadcasted_iota(jnp.int32, (1, TILE), 1)
    inside = place < half
    misc = jnp.concatenate([misc_l[...], misc_r[...]], axis=1)
    noise = jnp.concatenate([noise_l[...], noise_r[...]], axis=1)
    importance = jnp.where(inside, misc[1:2, :], 0.0)
    counted = jnp.where(inside, misc[2:3, :], 0.0)
    weight = counted * importance
    pad = jnp.zeros((32 - ACT, TILE), F32)

    x = states[...]
    x3 = x[:, 0:384]
    xn = nexts[...]
    z1_t = nt(w1_t[...], xn)
    z1_c = nt(w1c_h[...], x) + nt(w1c_l[...], x)
    z1_a = nt(w1a_h[...], x3) + nt(w1a_l[...], x3)

    def head(weights, hidden, bias, size):
        both = nn(weights[...], hidden)
        return both[0:size, :] + both[size : 2 * size, :] + spread_lanes(bias)

    h1 = gelu(z1_t[0:HID, :])
    h2 = gelu(nn(w2_ta[...], h1) + spread_lanes(bias2[0]))
    out = head(w3_ta, h2, bias3_ta[...], 48)
    next_action, next_logp, _, _ = policy_parts(out, noise[0:ACT, :])

    h1c, s1c = gelu_pair(z1_c)
    z2_c = nn(w2c_h[...], h1c) + nn(w2c_l[...], h1c) + spread_lanes(bias2[3])
    h2c, s2c = gelu_pair(z2_c)
    both = nn(w3_oc[...], h2c)
    out_c = both[0:8, :] + both[16:24, :] + spread_lanes(bias3_oc[...])

    z1 = z1_t[HID:, :] + nn(wa_t[...], stacked_action(next_action, pad))
    h1 = gelu(z1)
    h2 = gelu(nn(w2_tc[...], h1) + spread_lanes(bias2[1]))
    both = nn(w3_tc[...], h2)
    out_t = both[0:8, :] + both[16:24, :] + spread_lanes(bias3_tc[...])
    next_spread = softplus(out_t[1:2, :]) + 0.1
    reward = aux[AUX_REWARD : AUX_REWARD + 1, :]
    goal = reward + DISCOUNT * (
        out_t[0:1, :] + next_spread * noise[2 * ACT : 2 * ACT + 1, :] - alpha * next_logp
    )

    q_value = out_c[0:1, :]
    soft, slope = softplus_pair(out_c[1:2, :])
    spread = soft + 0.1
    inverse = 1.0 / spread
    square_inverse = inverse * inverse
    miss = goal - q_value
    bound = jnp.minimum(jnp.maximum(miss, -3.0 * spread), 3.0 * spread)
    critic_loss = weight * (
        0.5 * miss * miss * square_inverse
        + 0.5 * bound * bound * square_inverse
        + jnp.log(spread)
    )
    mean_back = -weight * miss * square_inverse
    spread_back = weight * (1.0 - bound * bound * square_inverse) * inverse * slope
    col0 = spread_lanes(w3c_back[:, 0:LANES])
    col1 = spread_lanes(w3c_back[:, LANES : 2 * LANES])
    dz2 = (col0 * mean_back + col1 * spread_back) * s2c
    dz2b = dz2.astype(BF16)
    g2c[...] += nt(h1c, dz2b)
    gb2c[...] += dz2[:, 0:LANES] + dz2[:, LANES:]
    dz1 = (nn(w2c_bh[...], dz2b) + nn(w2c_bl[...], dz2b)) * s1c
    g1c[...] += nn(dz1.astype(BF16), x)
    row8 = lax.broadcasted_iota(jnp.int32, (16, TILE), 0)
    do_c = jnp.where(
        row8 == 0,
        jnp.broadcast_to(mean_back, (16, TILE)),
        jnp.where(row8 == 1, jnp.broadcast_to(spread_back, (16, TILE)), 0.0),
    )
    g3c[...] += nt(do_c.astype(BF16), h2c)
    gb3c[...] += do_c[:, 0:LANES] + do_c[:, LANES:]

    h1a, s1a = gelu_pair(z1_a)
    z2_a = nn(w2a_h[...], h1a) + nn(w2a_l[...], h1a) + spread_lanes(bias2[2])
    h2a, s2a = gelu_pair(z2_a)
    out = head(w3_oa, h2a, bias3_oa[...], 48)
    shocks = noise[ACT : 2 * ACT, :]
    action, logp, spread_a, slope_a = policy_parts(out, shocks)

    old_action = aux[0:ACT, :] + aux[AUX_LOW : AUX_LOW + ACT, :]
    z1 = z1_c + nn(wa_o[...], stacked_action(action - old_action, pad))
    h1q, s1q = gelu_pair(z1)
    z2_q = nn(w2c_h[...], h1q) + nn(w2c_l[...], h1q) + spread_lanes(bias2[3])
    h2q, s2q = gelu_pair(z2_q)
    both = nn(w3_oc[...], h2q)
    value_now = both[0:1, :] + both[16:17, :] + spread_lanes(bias3_oc[0:1, :])
    dz2q = (col0 * s2q).astype(BF16)
    dz1q = (nn(w2c_bh[...], dz2q) + nn(w2c_bl[...], dz2q)) * s1q
    both = nn(wa_back[...], dz1q.astype(BF16))
    value_back = both[0:ACT, :] + both[32 : 32 + ACT, :]

    counted_alpha = counted * alpha
    d_pre = counted_alpha * 2.0 * action - counted * value_back * (1.0 - action * action)
    d_raw = (d_pre * shocks - counted_alpha / spread_a) * slope_a
    gap = jnp.zeros((24 - ACT, TILE), F32)
    do_a = jnp.concatenate([d_pre, gap, d_raw, gap], axis=0)
    high, low = split(do_a)
    dz2 = nn(w3a_back[:, 0:144], jnp.concatenate([high, low, high], axis=0)) * s2a
    dz2b = dz2.astype(BF16)
    g2a[...] += nt(h1a, dz2b)
    gb2a[...] += dz2[:, 0:LANES] + dz2[:, LANES:]
    dz1 = (nn(w2a_bh[...], dz2b) + nn(w2a_bl[...], dz2b)) * s1a
    g1a[...] += nn(dz1.astype(BF16), x3)
    g3a[...] += nt(high, h2a)
    gb3a[...] += do_a[:, 0:LANES] + do_a[:, LANES:]

    def fold(row):
        return row[:, 0:LANES] + row[:, LANES:]

    sums[0:1, :] += fold(counted)
    sums[1:2, :] += fold(counted * logp)
    sums[2:3, :] += fold(critic_loss)
    sums[3:4, :] += fold(counted * (alpha * logp - value_now))
    sums[4:5, :] = jnp.maximum(
        sums[4:5, :], jnp.maximum(importance[:, 0:LANES], importance[:, LANES:])
    )

    @pl.when(step == tiles - 1)
    def _():
        total[...] = jnp.zeros_like(total)

        def sum_row(block):
            return jnp.sum(block.T, axis=0, keepdims=True)

        for side in (0, 1):
            at = side * LANES
            turned = g1a[at : at + LANES, :].T
            total[A_W1[side] : A_W1[side] + OBS, :] = turned[0:OBS, :]
            total[A_B + side : A_B + side + 1, :] = turned[ONE_LANE : ONE_LANE + 1, :]
            total[A_W2[side] : A_W2[side] + HID, :] = g2a[:, at : at + LANES]
            total[A_W3[side] : A_W3[side] + ACT, :] = g3a[0:ACT, at : at + LANES]
            total[A_W3[side] + ACT : A_W3[side] + 2 * ACT, :] = g3a[24 : 24 + ACT, at : at + LANES]
            total[A_B + 2 + side : A_B + 3 + side, :] = sum_row(gb2a[at : at + LANES, :])
            turned = g1c[at : at + LANES, :].T
            total[C_W1[side] : C_W1[side] + OBS, :] = turned[0:OBS, :]
            total[C_W1[side] + OBS : C_W1[side] + OBS + ACT, :] = (
                turned[384 : 384 + ACT, :] + turned[384 + AUX_LOW : 384 + AUX_LOW + ACT, :]
            )
            total[C_B + side : C_B + side + 1, :] = turned[ONE_LANE : ONE_LANE + 1, :]
            total[C_W2[side] : C_W2[side] + HID, :] = g2c[:, at : at + LANES]
            total[C_W3[side] : C_W3[side] + 2, :] = g3c[0:2, at : at + LANES]
            total[C_B + 2 + side : C_B + 3 + side, :] = sum_row(gb2c[at : at + LANES, :])
        square[...] = jnp.zeros_like(square)
        square[0:ACT, :] = gb3a[0:ACT, :]
        square[ACT : 2 * ACT, :] = gb3a[24 : 24 + ACT, :]
        total[A_B + 4 : A_B + 5, :] = sum_row(square[...])
        square[...] = jnp.zeros_like(square)
        square[0:2, :] = gb3c[0:2, :]
        total[C_B + 4 : C_B + 5, :] = sum_row(square[...])
        total[EXTRA : EXTRA + 4, :] = sums[0:4, :]
        peak = jnp.max(sums[4:5, :], axis=1, keepdims=True)
        for k in range(EXTRA + 8 - EXTRA_SLOTS):
            total[EXTRA_SLOTS + k : EXTRA_SLOTS + k + 1, :] = jnp.where(
                lanes_of(1) + k * LANES == meta[1], jnp.broadcast_to(peak, (1, LANES)), 0.0
            )
        count = keep.shape[0] // chunk
        for p in range(count):
            at = pl.multiple_of((meta[1] ^ p) * chunk, 8)
            keep[p * chunk : (p + 1) * chunk, :] = total[pl.ds(at, chunk), :]
            at = pl.multiple_of((meta[1] ^ (p + count)) * chunk, 8)
            send[p * chunk : (p + 1) * chunk, :] = total[pl.ds(at, chunk), :]


def losses(meta, log_alpha, states, nexts, aux, noise, misc, own_a, other_a, own_c, other_c, devices):
    padded = states.shape[0]
    half = noise.shape[1] // 2
    tiles = padded // TILE
    chunk = chunk_rows(devices)
    rows = chunk * devices
    blocks = half // LANES
    last = 2 * blocks - 1

    def fixed(i, meta):
        return (0, 0)

    def left(i, meta):
        return (0, jnp.minimum(meta[0] * blocks + 2 * i, last))

    def right(i, meta):
        return (0, jnp.minimum(meta[0] * blocks + 2 * i + 1, last))

    def body(*refs):
        loss_kernel(tiles, half, chunk, *refs)

    def bf(*shape):
        return pltpu.VMEM(shape, BF16)

    def f32(*shape):
        return pltpu.VMEM(shape, F32)

    features = noise.shape[0]
    return pl.pallas_call(
        body,
        out_shape=(
            jax.ShapeDtypeStruct((rows // 2, LANES), F32),
            jax.ShapeDtypeStruct((rows // 2, LANES), F32),
        ),
        grid_spec=pltpu.PrefetchScalarGridSpec(
            num_scalar_prefetch=1,
            grid=(tiles,),
            in_specs=[
                pl.BlockSpec(memory_space=pltpu.SMEM),
                pl.BlockSpec((TILE, 512), lambda i, meta: (i, 0)),
                pl.BlockSpec((TILE, 384), lambda i, meta: (i, 0)),
                pl.BlockSpec((AUX_ROWS, TILE), lambda i, meta: (0, i)),
                pl.BlockSpec((features, LANES), left),
                pl.BlockSpec((features, LANES), right),
                pl.BlockSpec((8, LANES), left),
                pl.BlockSpec((8, LANES), right),
                pl.BlockSpec((1, A_SIZE), fixed),
                pl.BlockSpec((1, A_SIZE), fixed),
                pl.BlockSpec((1, C_SIZE), fixed),
                pl.BlockSpec((1, C_SIZE), fixed),
            ],
            out_specs=(
                pl.BlockSpec((rows // 2, LANES), fixed),
                pl.BlockSpec((rows // 2, LANES), fixed),
            ),
            scratch_shapes=[
                f32(A_FLAT, LANES), f32(A_FLAT, LANES), f32(C_FLAT, LANES), f32(C_FLAT, LANES),
                bf(512, 384), bf(HID, 384), bf(HID, 384), bf(HID, 512), bf(HID, 512),
                bf(HID, LANES), bf(HID, LANES), bf(64, HID),
                bf(HID, HID), bf(HID, HID),
                bf(HID, HID), bf(HID, HID), bf(HID, HID), bf(HID, HID),
                bf(HID, HID), bf(HID, HID), bf(HID, HID), bf(HID, HID),
                f32(4, HID, LANES), bf(96, HID), bf(96, HID), bf(32, HID), bf(32, HID),
                bf(HID, HID), f32(HID, 2 * LANES),
                f32(48, LANES), f32(48, LANES), f32(8, LANES), f32(8, LANES),
                f32(LANES, LANES), f32(HID, HID), f32(16, HID),
                f32(HID, 384), f32(HID, 512), f32(HID, HID), f32(HID, HID),
                f32(48, HID), f32(16, HID), f32(HID, LANES), f32(HID, LANES),
                f32(48, LANES), f32(16, LANES), f32(8, LANES), f32(rows, LANES),
            ],
        ),
        compiler_params=pltpu.CompilerParams(
            dimension_semantics=("arbitrary",), vmem_limit_bytes=VMEM_BYTES
        ),
        name="losses",
    )(meta, log_alpha, states, nexts, aux, noise, noise, misc, misc, own_a, other_a, own_c, other_c)


def stat_pieces(width_in, width_out):
    sizes = [width_in, HID, HID, HID, HID, width_out, HID, HID, width_out]
    starts = [sum(sizes[:k]) for k in range(len(sizes))]
    rows = [-(-size // LANES) for size in sizes]
    return sizes, starts, [sum(rows[:k]) for k in range(len(rows))], sum(rows)


def aligned_stats(statistics, width_in, width_out):
    sizes, starts, _, rows = stat_pieces(width_in, width_out)
    pieces = [
        jnp.pad(statistics[start : start + size], (0, -size % LANES))
        for size, start in zip(sizes, starts)
    ]
    pieces.append(jnp.zeros((-rows % 8 * LANES,), F32))
    return jnp.concatenate(pieces).reshape(-1, LANES)


def store_line(out, lead, value):
    size = out.shape[-1]
    count = value.shape[0]
    whole = size // 1024
    for k in range(whole):
        part = value[8 * k : 8 * k + 8, :]
        out[pl.ds(1024 * k, 1024)] = part.reshape(1024)
    for k in range(8 * whole, count):
        width = min(LANES, size - k * LANES)
        if width > 0:
            out[pl.ds(k * LANES, width)] = value[k : k + 1, 0:width].reshape(width)


def net_update(
    total, scale, old_stats, width_in, width_out, w1, w2, w3, bias_at, rows, fg, fu, stats_out
):
    sizes, starts, first, _ = stat_pieces(width_in, width_out)
    lines = [[] for _ in sizes]

    def old_row(piece, k):
        return old_stats[first[piece] + k : first[piece] + k + 1, :]

    def blend(old, new):
        return DECAY_RATE * old + (1.0 - DECAY_RATE) * new

    def clip_scale(square_sum, number):
        root = jnp.sqrt(square_sum / number)
        return 1.0 / jnp.maximum(1.0, root / CLIP_LEVEL)

    def whole_sum(value):
        return jnp.sum(jnp.sum(value, axis=0, keepdims=True), axis=1, keepdims=True)

    for layer, (places, height, flat_at) in enumerate(
        ((w1, width_in, 0), (w2, HID, rows[0]))
    ):
        parts = [total[at : at + height, :] * scale for at in places]
        squares = [g * g + TINY_TERM for g in parts]
        blocks = -(-height // LANES)
        old = jnp.concatenate([column(old_row(layer, k)) for k in range(blocks)], axis=0)
        old = old[0:height, :]
        mean = jnp.sum(squares[0] + squares[1], axis=1, keepdims=True) * (1.0 / HID)
        row_stat = blend(old, jnp.broadcast_to(mean, (height, LANES)))
        for k in range(blocks):
            block = row_stat[k * LANES : min(height, (k + 1) * LANES), :]
            if block.shape[0] < LANES:
                block = jnp.concatenate(
                    [block, jnp.zeros((LANES - block.shape[0], LANES), F32)], axis=0
                )
            lines[layer].append(block.T[0:1, :])
        mean_row = jnp.sum(row_stat, axis=0, keepdims=True) * (1.0 / height)
        row_root = lax.rsqrt(row_stat)
        steps = []
        for side in (0, 1):
            col_stat = blend(
                old_row(3 + layer, side),
                jnp.sum(squares[side], axis=0, keepdims=True) * (1.0 / height),
            )
            lines[3 + layer].append(col_stat)
            steps.append((parts[side] * row_root) * (lax.rsqrt(col_stat) * jnp.sqrt(mean_row)))
        factor = clip_scale(
            whole_sum(steps[0] * steps[0] + steps[1] * steps[1]), float(height * HID)
        )
        for side in (0, 1):
            fg[pl.ds(flat_at + side, height, stride=2), :] = parts[side]
            fu[pl.ds(flat_at + side, height, stride=2), :] = steps[side] * factor

    tall = -(-width_out // 8) * 8
    parts = [total[at : at + tall, :] * scale for at in w3]
    real = rows_of(tall) < width_out
    squares = [jnp.where(real, g * g + TINY_TERM, 0.0) for g in parts]
    old = column(old_row(5, 0))[0:tall, :]
    mean = jnp.sum(squares[0] + squares[1], axis=1, keepdims=True) * (1.0 / HID)
    col_stat = blend(old, jnp.broadcast_to(mean, (tall, LANES)))
    lines[5].append(
        jnp.concatenate([col_stat, jnp.zeros((LANES - tall, LANES), F32)], axis=0).T[0:1, :]
    )
    row_stats = []
    for side in (0, 1):
        row_stats.append(
            blend(
                old_row(2, side),
                jnp.sum(squares[side], axis=0, keepdims=True) * (1.0 / width_out),
            )
        )
        lines[2].append(row_stats[side])
    mean_row = jnp.sum(row_stats[0] + row_stats[1], axis=1, keepdims=True) * (1.0 / HID)
    col_root = jnp.where(real, lax.rsqrt(col_stat), 0.0)
    steps = [
        (parts[side] * lax.rsqrt(row_stats[side])) * (col_root * jnp.sqrt(mean_row))
        for side in (0, 1)
    ]
    factor = clip_scale(
        whole_sum(steps[0] * steps[0] + steps[1] * steps[1]), float(HID * width_out)
    )
    pad = jnp.zeros((LANES - tall, LANES), F32)
    size = rows[2] - rows[1]
    padded = -(-size // 8) * 8
    for flat, pair in ((fg, parts), (fu, [u * factor for u in steps])):
        turned = jnp.concatenate(
            [
                jnp.concatenate([jnp.where(real, pair[side], 0.0), pad], axis=0).T
                for side in (0, 1)
            ],
            axis=0,
        )
        flat[rows[1] : rows[1] + size, :] = flatten(turned, width_out, padded)[0:size, :]

    grad = total[bias_at : bias_at + 8, :] * scale
    line = rows_of(8)
    lane = lanes_of(8)
    real = (line < 4) | ((line == 4) & (lane < width_out))
    grad = jnp.where(real, grad, 0.0)
    stat = blend(old_stats[first[6] : first[6] + 5, :], grad[0:5, :] * grad[0:5, :] + TINY_TERM)
    step = jnp.where(real[0:5, :], grad[0:5, :] * lax.rsqrt(stat), 0.0)
    factor = clip_scale(whole_sum(step * step), float(2 * HID + width_out))
    fg[rows[2] : rows[2] + 5, :] = grad[0:5, :]
    fu[rows[2] : rows[2] + 5, :] = step * factor
    for k in range(5):
        lines[6 + k // 2].append(stat[k : k + 1, :])

    size = stats_out.shape[0]
    count = -(-size // LANES)
    made = [jnp.zeros((1, LANES), F32) for _ in range(count + 1)]
    lane = lanes_of(1)
    for piece, pieces in enumerate(lines):
        for k, value in enumerate(pieces):
            start = starts[piece] + k * LANES
            width = min(LANES, sizes[piece] - k * LANES)
            value = jnp.where(lane < width, value, 0.0)
            shift = start % LANES
            at = start // LANES
            if shift:
                value = pltpu.roll(value, shift, 1)
            made[at] = made[at] + jnp.where(lane >= shift, value, 0.0)
            if shift:
                made[at + 1] = made[at + 1] + jnp.where(lane < shift, value, 0.0)
    for k in range(count):
        width = min(LANES, size - k * LANES)
        stats_out[pl.ds(k * LANES, width)] = made[k][:, 0:width].reshape(width)


def write_net(side, own, other, fg, fu, slot, copy, grad):
    size = own.shape[1]
    whole = size // 1024

    def piece(at, row, width, count):
        mine = own[0:1, pl.ds(at, width)].reshape(count, width // count)
        theirs = other[0:1, pl.ds(at, width)].reshape(count, width // count)
        wide = width // count
        step = fu[pl.ds(row, count), 0:wide]
        online = jnp.where(side == 0, theirs, mine)
        new = online - LEARN_RATE * step
        held = jnp.where(side == 0, POLYAK_RATE * new + (1.0 - POLYAK_RATE) * mine, new)
        slot[0:1, pl.ds(at, width)] = held.reshape(1, width)
        copy[0:1, pl.ds(at, width)] = held.reshape(1, width).astype(BF16)
        grad[pl.ds(at, width)] = fg[pl.ds(row, count), 0:wide].reshape(width)

    def body(k, carry):
        piece(pl.multiple_of(k * 1024, 1024), pl.multiple_of(k * 8, 8), 1024, 8)
        return carry

    lax.fori_loop(0, whole, body, 0)
    full = size // LANES
    for row in range(whole * 8, full):
        piece(row * LANES, row, LANES, 1)
    piece(full * LANES, full, size - full * LANES, 1)


def update_kernel(
    chunk, devices,
    meta, log_alpha, mine, theirs, own_a, other_a, own_c, other_c, stats_a, stats_c,
    slot_a, slot_c, copy_a, copy_c, grad_a, grad_c, new_a, new_c, summary, alpha_out,
    total, fg_a, fu_a, fg_c, fu_c,
):
    count = devices // 2
    for p in range(count):
        at = pl.multiple_of((meta[1] ^ p) * chunk, 8)
        total[pl.ds(at, chunk), :] = mine[p * chunk : (p + 1) * chunk, :]
        at = pl.multiple_of((meta[1] ^ (p + count)) * chunk, 8)
        total[pl.ds(at, chunk), :] = theirs[p * chunk : (p + 1) * chunk, :]

    sums = jnp.sum(total[EXTRA : EXTRA + 8, :], axis=1, keepdims=True)
    peak = jnp.max(total[EXTRA_SLOTS : EXTRA + 8, :], axis=1, keepdims=True)
    peak = jnp.max(peak, axis=0, keepdims=True)
    counted = sums[0:1, :]
    scale_a = 1.0 / counted
    scale_c = scale_a / peak
    lane = lanes_of(1)
    line = jnp.where(
        lane == 0,
        jnp.broadcast_to(sums[2:3, :] / peak, (1, LANES)),
        jnp.where(
            lane == 1,
            jnp.broadcast_to(sums[3:4, :], (1, LANES)),
            jnp.broadcast_to(counted, (1, LANES)),
        ),
    )
    summary[...] = line
    alpha_out[...] = log_alpha[0] + ALPHA_STEP * (
        jnp.broadcast_to(sums[1:2, :] / counted, (1, LANES)) - ACT
    )
    net_update(
        total, scale_a, stats_a, OBS, 2 * ACT, A_W1, A_W2, A_W3, A_B, A_ROWS, fg_a, fu_a, new_a
    )
    net_update(
        total, scale_c, stats_c, OBS + ACT, 2, C_W1, C_W2, C_W3, C_B, C_ROWS, fg_c, fu_c, new_c
    )
    write_net(meta[0], own_a, other_a, fg_a, fu_a, slot_a, copy_a, grad_a)
    write_net(meta[0], own_c, other_c, fg_c, fu_c, slot_c, copy_c, grad_c)


def update(meta, log_alpha, mine, theirs, own_a, other_a, own_c, other_c, stats_a, stats_c, sizes, devices):
    chunk = chunk_rows(devices)

    def body(*refs):
        update_kernel(chunk, devices, *refs)

    def f32(*shape):
        return jax.ShapeDtypeStruct(shape, F32)

    smem = pl.BlockSpec(memory_space=pltpu.SMEM)
    vmem = pl.BlockSpec(memory_space=pltpu.VMEM)
    return pl.pallas_call(
        body,
        out_shape=(
            f32(1, A_SIZE), f32(1, C_SIZE),
            jax.ShapeDtypeStruct((1, A_SIZE), BF16), jax.ShapeDtypeStruct((1, C_SIZE), BF16),
            f32(A_SIZE), f32(C_SIZE), f32(sizes[0]), f32(sizes[1]), f32(1, LANES), f32(1, LANES),
        ),
        in_specs=[smem, smem] + [vmem] * 8,
        out_specs=tuple([vmem] * 10),
        scratch_shapes=[
            pltpu.VMEM((chunk * devices, LANES), F32),
            pltpu.VMEM((A_FLAT, LANES), F32), pltpu.VMEM((A_FLAT, LANES), F32),
            pltpu.VMEM((C_FLAT, LANES), F32), pltpu.VMEM((C_FLAT, LANES), F32),
        ],
        compiler_params=pltpu.CompilerParams(vmem_limit_bytes=VMEM_BYTES),
        name="optimizer",
    )(meta, log_alpha, mine, theirs, own_a, other_a, own_c, other_c, stats_a, stats_c)


def chunk_rows(devices):
    return -(-DATA_ROWS // (8 * devices)) * 8


def radices(count):
    found = []
    while count > 1:
        found.append(4 if count % 4 == 0 else 2)
        count //= found[-1]
    return found


def swap_groups(value):
    return lax.ppermute(value, "grp", [(0, 1), (1, 0)])


def exchange(value, mask):
    count = lax.axis_size("dp")
    return lax.ppermute(value, "dp", [(i, i ^ mask) for i in range(count)])


def buffer_place(group_side, count):
    rest = lax.axis_index("dp")
    place = group_side
    for radix in radices(count):
        place = place * radix + rest % radix
        rest = rest // radix
    return place


def all_sum(keep, send):
    stages = radices(lax.axis_size("dp"))
    value = keep + swap_groups(send)
    stride = 1
    for radix in stages:
        rows = value.shape[0] // radix
        parts = [value[k * rows : (k + 1) * rows] for k in range(radix)]
        came = [exchange(parts[k], k * stride) for k in range(1, radix)]
        value = parts[0]
        for part in came:
            value = value + part
        stride *= radix
    for radix in reversed(stages):
        stride //= radix
        value = jnp.concatenate(
            [value] + [exchange(value, k * stride) for k in range(1, radix)], axis=0
        )
    return value, swap_groups(value)


def shards(
    obs_rows,
    next_rows,
    action_rows,
    reward_rows,
    batch_index,
    valid_mask,
    noise,
    importance,
    actor_params,
    critic_params,
    actor_stats,
    critic_stats,
    log_alpha,
):
    devices = lax.axis_size("dp") * lax.axis_size("grp")
    group_side = lax.axis_index("grp")
    other_a = swap_groups(actor_params)
    other_c = swap_groups(critic_params)
    half = batch_index.shape[0] // 2
    padded = -(-half // TILE) * TILE
    picks = lax.dynamic_slice_in_dim(batch_index, group_side * half, half, 0)
    picks = jnp.pad((picks // 8) * 64 + picks % 8, (0, padded - half))
    meta = jnp.stack([group_side, buffer_place(group_side, lax.axis_size("dp"))]).astype(jnp.int32)
    blank = jnp.zeros_like(importance)
    misc = jnp.stack(
        [reward_rows, importance, valid_mask.astype(F32), blank, blank, blank, blank, blank]
    )
    states, nexts, aux = gather(
        picks, obs_rows.T, next_rows.T, action_rows.T, misc, padded
    )
    keep, send = losses(
        meta, log_alpha, states, nexts, aux, noise.T, misc,
        actor_params, other_a, critic_params, other_c, devices,
    )
    mine, theirs = all_sum(keep, send)
    (
        slot_a, slot_c, copy_a, copy_c, grad_a, grad_c, new_a, new_c, summary, alpha
    ) = update(
        meta, log_alpha, mine, theirs, actor_params, other_a, critic_params, other_c,
        aligned_stats(actor_stats, OBS, 2 * ACT), aligned_stats(critic_stats, OBS + ACT, 2),
        (actor_stats.shape[0], critic_stats.shape[0]), devices,
    )
    return (
        slot_a, slot_c, copy_a, copy_c, grad_a, grad_c, new_a, new_c,
        summary[0, 0:3], alpha[0, 0:1],
    )


def solution(mesh):
    return jax.shard_map(
        shards,
        mesh=mesh,
        in_specs=(
            P("dp", None),
            P("dp", None),
            P("dp", None),
            P("dp"),
            P("dp"),
            P("dp"),
            P("dp", None),
            P("dp"),
            P("grp", None),
            P("grp", None),
            P(),
            P(),
            P(),
        ),
        out_specs=(
            P("grp", None),
            P("grp", None),
            P("grp", None),
            P("grp", None),
            P(),
            P(),
            P(),
            P(),
            P(),
            P(),
        ),
        check_vma=False,
    )
```

```python
import jax
import jax.numpy as jnp
from jax import lax
from jax.experimental import pallas as pl
from jax.experimental.pallas import tpu as pltpu
from jax.sharding import PartitionSpec as P

OBS = 376
ACT = 17
HID = 256
LANES = 128
TILE = 512
SUB = 256

DISCOUNT = 0.99
POLYAK_RATE = 0.1
DECAY_RATE = 0.5
LEARN_RATE = 0.1
CLIP_LEVEL = 0.1
ALPHA_STEP = 0.01
TINY_TERM = 1e-30
HALF_LOG_TWO_PI = 0.9189385332046727
LOG_TWO = 0.6931471805599453
ROOT_HALF = 0.7071067811865476
ROOT_TWO = 1.4142135623730951
LOG2_E = 1.4426950408889634
LOG2_TWO_OVER_ROOT_PI = 0.17425193548825

F32 = jnp.float32
BF16 = jnp.bfloat16
VMEM_BYTES = 62 * 2**20

ONE_LANE = OBS
AUX_LOW = 32
AUX_REWARD = 64
AUX_AGAIN = 96
AUX_ROWS = 72
OWN_WEIGHT = 40
OWN_ROWS = 48
MISC_VALID = 2
MISC_SPOT = 3


def flat_rows(width_in, width_out):
    w2 = width_in * HID // LANES
    w3 = w2 + HID * HID // LANES
    b1 = w3 + HID * width_out // LANES
    return w2, w3, b1, b1 + 2, b1 + 4


A_ROWS = flat_rows(OBS, 2 * ACT)
C_ROWS = flat_rows(OBS + ACT, 2)
A_SIZE = A_ROWS[4] * LANES + 2 * ACT
C_SIZE = C_ROWS[4] * LANES + 2
A_FLAT = -(-A_SIZE // 1024) * 8
C_FLAT = -(-C_SIZE // 1024) * 8

A_W1 = (0, OBS)
A_W2 = (2 * OBS, 2 * OBS + HID)
A_W3 = (2 * OBS + 2 * HID, 2 * OBS + 2 * HID + 40)
A_B = A_W3[1] + 40
C_W1 = (A_B + 8, A_B + 8 + 400)
C_W2 = (C_W1[1] + 400, C_W1[1] + 400 + HID)
C_W3 = (C_W2[1] + HID, C_W2[1] + HID + 8)
C_B = C_W3[1] + 8
EXTRA = C_B + 8
EXTRA_SLOTS = EXTRA + 4
DATA_ROWS = EXTRA + 8


def nn(left, right):
    return lax.dot_general(
        left, right, (((1,), (0,)), ((), ())), preferred_element_type=F32
    )


def nt(left, right):
    return lax.dot_general(
        left, right, (((1,), (1,)), ((), ())), preferred_element_type=F32
    )


def split(value):
    high = value.astype(BF16)
    return high, (value - high.astype(F32)).astype(BF16)


def twice(value):
    return jnp.concatenate([value, value], axis=0)


def gelu(t):
    return (t * (1.0 + lax.erf(t))).astype(BF16)


def gelu_pair(t):
    double_cdf = 1.0 + lax.erf(t)
    bell = jnp.exp2(LOG2_TWO_OVER_ROOT_PI - LOG2_E * (t * t))
    return (t * double_cdf).astype(BF16), double_cdf + t * bell


def softplus(x):
    return jnp.maximum(x, 0.0) + jnp.log(1.0 + jnp.exp(-jnp.abs(x)))


def softplus_pair(x):
    decay = jnp.exp(-jnp.abs(x))
    inverse = 1.0 / (1.0 + decay)
    return jnp.maximum(x, 0.0) + jnp.log(1.0 + decay), jnp.where(x >= 0.0, inverse, decay * inverse)


def column(row):
    return jnp.broadcast_to(row, (LANES, LANES)).T


def rows_of(count):
    return lax.broadcasted_iota(jnp.int32, (count, LANES), 0)


def lanes_of(count):
    return lax.broadcasted_iota(jnp.int32, (count, LANES), 1)


def square_eye(reverse=False):
    row = lax.broadcasted_iota(jnp.int32, (HID, HID), 0)
    lane = lax.broadcasted_iota(jnp.int32, (HID, HID), 1)
    return (row == (HID - 1 - lane if reverse else lane)).astype(F32).astype(BF16)


def two_pieces(value):
    return jnp.concatenate(split(value), axis=1)


def strided_roll(value, shift, stride):
    turn = (rows_of(HID) * stride + shift) % LANES
    for step in (2, 4, 8, 16, 32, 64):
        value = jnp.where((turn & step) != 0, pltpu.roll(value, step, 1), value)
    return value


def unflatten(flat, width):
    rows = flat.shape[0]
    first = (HID - 1 - rows_of(HID)) * width
    lane = lanes_of(HID)
    owner = first // LANES
    picks = jnp.concatenate([(owner == lane), (owner + 1 == lane)], axis=0).astype(F32).astype(BF16)
    found = nn(picks[:, 0:rows], two_pieces(flat))
    found = found[:, 0:LANES] + found[:, LANES:]
    mixed = jnp.where(lane >= first % LANES, found[0:HID, :], found[HID:, :])
    turned = strided_roll(mixed, -(HID - 1) * width % LANES, width)
    return nn(square_eye(True), two_pieces(turned)).astype(BF16)


def flatten(value, width, rows):
    first = rows_of(HID) * width
    turned = strided_roll(value, 0, width)
    here = lanes_of(HID) >= first % LANES
    both = jnp.concatenate([jnp.where(here, turned, 0.0), jnp.where(here, 0.0, turned)], axis=0)
    high, low = split(both)
    least = (both - high.astype(F32) - low.astype(F32)).astype(BF16)
    owner = lax.broadcasted_iota(jnp.int32, (rows, HID), 1) * width // LANES
    row = lax.broadcasted_iota(jnp.int32, (rows, HID), 0)
    places = jnp.concatenate([owner == row, owner + 1 == row], axis=1).astype(F32).astype(BF16)
    found = nn(places, jnp.concatenate([high, low, least], axis=1))
    return found[:, 0:LANES] + found[:, LANES : 2 * LANES] + found[:, 2 * LANES :]


def build_table(step, block, obs, nxt, act, misc, table, wide):
    groups = block // 8
    table3 = table.reshape(table.shape[0] // 64, 64, LANES)
    at = pl.multiple_of(step * groups, groups)

    def put(value, first):
        for c in range(value.shape[1] // LANES):
            table3[pl.ds(at, groups), 8 * (first + c) : 8 * (first + c) + 8, :] = value[
                :, LANES * c : LANES * (c + 1)
            ].reshape(groups, 8, LANES)

    ones = (lax.broadcasted_iota(jnp.int32, (8, block), 0) == 0).astype(F32)
    whole = OBS // 16 * 16

    def padded(source):
        value = source[...]
        rest = jnp.concatenate([value[whole:, :].astype(F32), ones], axis=0).astype(BF16)
        return jnp.concatenate([value[0:whole, :], rest], axis=0)

    value = padded(obs)
    eye = square_eye()
    turned = [nt(eye, value[:, k : k + HID]) for k in range(0, block, HID)]
    put(jnp.concatenate(turned, axis=0), 0)
    put(padded(nxt).T.astype(F32), 3)
    action = act[...]
    high = action.astype(BF16).astype(F32)
    wide[0:ACT, :] = high
    wide[AUX_LOW : AUX_LOW + ACT, :] = action - high
    wide[AUX_AGAIN : AUX_AGAIN + ACT, :] = high
    wide[AUX_REWARD : AUX_REWARD + 8, :] = misc[...]
    put(wide[...].T, 6)


def build_own(step, size, noise, misc, own_table, tall):
    tall[0 : 2 * ACT + 1, :] = noise[...]
    tall[OWN_WEIGHT : OWN_WEIGHT + 8, :] = misc[...]
    own_table[pl.ds(pl.multiple_of(step * size, size), size), :] = tall[...].T


def choose(step, size, misc, chosen, count):
    lane = lanes_of(1)
    parts = size // LANES
    counted = misc[MISC_VALID : MISC_VALID + 1, :]
    flags = [counted[:, LANES * k : LANES * (k + 1)] for k in range(parts)]
    stacked = jnp.concatenate(flags + [jnp.zeros((-parts % 16, LANES), F32)], axis=0).astype(BF16)
    before = nn(stacked, (rows_of(LANES) < lanes_of(LANES)).astype(F32).astype(BF16))
    before = before.astype(jnp.int32)
    spot = misc[MISC_SPOT : MISC_SPOT + 1, :].astype(jnp.int32)
    place = count[0]
    none = jnp.zeros((1, LANES), jnp.int32)
    for k in range(parts):
        where = (before[k : k + 1, :] + place) & (LANES - 1)
        where = jnp.where(flags[k] > 0.0, where, -1)
        hit = (jnp.broadcast_to(where, (LANES, LANES)) == rows_of(LANES)).astype(F32).astype(BF16)
        here = spot[:, LANES * k : LANES * (k + 1)]
        index = lane + (step * size + LANES * k)
        digits = jnp.concatenate(
            [here >> 8, here & 255, index >> 8, index & 255] + [none] * 12, axis=0
        )
        moved = nt(digits.astype(F32).astype(BF16), hit).astype(jnp.int32)
        row = place >> 7
        first = lane >= (place & (LANES - 1))
        for which in (0, 1):
            value = (moved[2 * which : 2 * which + 1, :] << 8) + moved[2 * which + 1 : 2 * which + 2, :]
            chosen[which, pl.ds(row, 1), :] += jnp.where(first, value, 0)
            chosen[which, pl.ds(row + 1, 1), :] += jnp.where(first, 0, value)
        place = place + jnp.sum(flags[k]).astype(jnp.int32)
    count[0] = place


def fetch_rows(chosen, first, table, own_table, got, start, stop, batch=16):
    for base in range(start, stop, batch):
        spots = [(first + j // LANES, j % LANES) for j in range(base, base + batch)]
        found = [table[pl.ds(chosen[0, row, lane], 8, stride=8), :] for row, lane in spots]
        own = [own_table[pl.ds(chosen[1, row, lane], 1), :] for row, lane in spots]
        for j in range(base, base + batch):
            at = (j // 8) * 64 + j % 8
            got[pl.ds(at, 8, stride=8), :] = found[j - base]
            got[at + 56 : at + 57, :] = own[j - base]


def turn_rows(got, states, nexts, aux):
    got3 = got.reshape(TILE // 8, 64, LANES)

    def chunk(c):
        return got3[:, 8 * c : 8 * c + 8, :].reshape(TILE, LANES)

    for c in range(3):
        states[:, LANES * c : LANES * (c + 1)] = chunk(c).astype(BF16)
        nexts[:, LANES * c : LANES * (c + 1)] = chunk(3 + c).astype(BF16)
    extra = chunk(6)
    states[:, 3 * LANES :] = extra.astype(BF16)
    aux[0:AUX_ROWS, :] = extra.T[0:AUX_ROWS, :]
    aux[AUX_ROWS:, :] = chunk(7).T[0:OWN_ROWS, :]


def copy_flat(flat, source):
    size = source.shape[1]
    whole = size // 1024

    for k in range(whole):
        flat[8 * k : 8 * k + 8, :] = source[0:1, 1024 * k : 1024 * (k + 1)].reshape(8, LANES)
    flat[8 * whole : 8 * whole + 8, :] = jnp.zeros((8, LANES), F32)
    full = (size - whole * 1024) // LANES
    for k in range(full):
        flat[8 * whole + k : 8 * whole + k + 1, :] = source[
            0:1, whole * 1024 + k * LANES : whole * 1024 + (k + 1) * LANES
        ]
    rest = size - whole * 1024 - full * LANES
    flat[8 * whole + full : 8 * whole + full + 1, 0:rest] = source[0:1, size - rest : size]


def halves(flat, start, height):
    return [flat[pl.ds(start + side, height, stride=2), :] for side in (0, 1)]


def natural(flat, start, height):
    return jnp.concatenate([flat[pl.ds(start + side, height, stride=2), :] for side in (0, 1)], axis=1)


def bias_row(flat, at):
    return jnp.concatenate([flat[at : at + 1, :], flat[at + 1 : at + 2, :]], axis=1)


def first_layer(flat, rows, eye, dst, pieces, base):
    tile = lax.broadcasted_iota(jnp.int32, (8, HID), 0)
    bias = jnp.where(tile == 0, jnp.broadcast_to(bias_row(flat, rows[2]), (8, HID)), 0.0)
    parts = split(jnp.concatenate([natural(flat, 0, OBS), bias], axis=0) * ROOT_HALF)
    for k in range(pieces):
        dst[base : base + HID, 384 * k : 384 * (k + 1)] = nt(eye, parts[k]).astype(BF16)


def action_layer(flat, eye, square, stack, first, back):
    square[0:ACT, :] = natural(flat, 2 * OBS, ACT)
    square[ACT:, :] = jnp.zeros((32 - ACT, HID), F32)
    value = square[...]
    high, low = split(value * ROOT_HALF)
    none = jnp.zeros_like(high)
    stack[...] = nt(eye, jnp.concatenate([high, high, low, none], axis=0)).astype(BF16)
    if first is not None:
        first[:, 768:896] = nt(eye, jnp.concatenate([high, high, none, low], axis=0)).astype(BF16)
        high, low = split(0.5 * value)
        back[0:32, :] = high
        back[32:64, :] = low


def second_layer(flat, rows, eye, forward, back, back_q=None, head=None):
    value = 0.5 * natural(flat, rows[0], HID)
    high, low = split(value)
    forward[:, 0:HID] = nt(eye, high).astype(BF16)
    if back is not None:
        forward[:, HID : 2 * HID] = nt(eye, low).astype(BF16)
        back[:, 0:HID] = high
        back[:, HID : 2 * HID] = low
    if back_q is not None:
        high, low = split(value * head)
        back_q[:, 0:HID] = high
        back_q[:, HID : 2 * HID] = low


def second_biases(flats, eye, bias):
    rows = [
        jnp.broadcast_to(bias_row(flat, rows[3]) * ROOT_HALF, (LANES, HID)) for flat, rows in flats
    ]
    both = jnp.concatenate([two_pieces(row) for row in rows], axis=0)
    bias[...] = nt(jnp.concatenate([eye, eye], axis=1), both)


def selector(rows, chosen):
    return chosen(rows_of(rows), lanes_of(rows)).astype(F32)


def block_pair(value):
    none = jnp.zeros_like(value)
    return jnp.concatenate(
        [jnp.concatenate([value, none], axis=1), jnp.concatenate([none, value], axis=1)], axis=0
    ).astype(BF16)


def actor_place(row, lane):
    return ((row == lane) & (row < ACT)) | ((row - 24 == lane - ACT) & (row >= 24) & (row < 24 + ACT))


def actor_head(flat, rows, forward, bias, back):
    pieces = unflatten(flat[rows[1] : rows[1] + 72, :] * ROOT_HALF, 2 * ACT)
    place = selector(48, actor_place)
    forward[...] = nt(block_pair(place), pieces).astype(BF16)
    if back is not None:
        none = jnp.zeros((48, LANES), F32)
        high = jnp.concatenate([place, none], axis=1)
        low = jnp.concatenate([none, place], axis=1)
        back[...] = nt(pieces, jnp.concatenate([high, high, low], axis=0).astype(BF16)).astype(BF16)
    heads = column(flat[rows[4] : rows[4] + 1, :])
    bias[0:24, :] = heads[0:24, :]
    bias[24:48, :] = heads[ACT : ACT + 24, :]


def critic_head(flat, rows, eye, forward, bias, back):
    pieces = unflatten(flat[rows[1] : rows[1] + 8, :] * ROOT_HALF, 2)
    place = selector(16, lambda row, lane: (row == lane) & (row < 2))
    both = nt(block_pair(place), pieces)
    forward[...] = both.astype(BF16)
    bias[...] = column(flat[rows[4] : rows[4] + 1, :])[0:8, :]
    if back is None:
        return None
    spread = [
        jnp.concatenate(
            [jnp.broadcast_to(both[16 * part + k : 16 * part + k + 1, :], (LANES, HID)) for part in (0, 1)],
            axis=1,
        )
        for k in (0, 1)
    ]
    columns = nt(jnp.concatenate([eye, eye], axis=1), jnp.concatenate(spread, axis=0).astype(BF16))
    back[...] = ROOT_TWO * columns
    return ROOT_TWO * (both[0:1, :] + both[16:17, :])


def spread_lanes(bias):
    return jnp.concatenate([bias] * (SUB // LANES), axis=1)


def fold(value):
    parts = [value[:, k : k + LANES] for k in range(0, value.shape[1], LANES)]
    total = parts[0]
    for part in parts[1:]:
        total = total + part
    return total


def policy_parts(out, shocks):
    centre = out[0:ACT, :]
    raw = out[24 : 24 + ACT, :]
    soft, slope = softplus_pair(raw)
    spread = soft + 0.05
    pre = centre + spread * shocks
    terms = (
        -0.5 * shocks * shocks
        - jnp.log(spread)
        - HALF_LOG_TWO_PI
        - 2.0 * (LOG_TWO - pre - softplus(-2.0 * pre))
    )
    return jnp.tanh(pre), jnp.sum(terms, axis=0, keepdims=True), spread, slope


def stacked_action(value, pad):
    tall = jnp.concatenate([value, pad], axis=0)
    high, low = split(tall)
    return jnp.concatenate([high, low, high, jnp.zeros_like(high)], axis=0)


def loss_kernel(
    builds, tiles, half, chunk, block,
    meta, log_alpha, obs, nxt, act, misc_wide, noise_own, misc_own,
    own_actor, other_actor, own_critic, other_critic,
    keep, send,
    flat_ta, flat_oa, flat_tc, flat_oc,
    w1_t, w1a, w1c, wa_t, wa_o, wa_back, w2_ta, w2_tc, w2a, w2c, w2a_back, w2c_back, w2q_back,
    bias2, w3_ta, w3_oa, w3_tc, w3_oc, w3a_back, w3c_back, bias3_ta, bias3_oa, bias3_tc, bias3_oc,
    square,
    g1a, g1c, g2a, g2c, g3a, g3c, gb2a, gb2c, gb3a, gb3c, sums, total,
    z1_t, z1_a, z1_c, h1c, h2c, dz1c, dz2c, doc, h1a, h2a, dz1a, dz2a, doa,
    table, got, wide, states_before, states, states_after, nexts_after, aux, aux_after,
    own_table, tall, listed, chosen, count, peaks, done,
):
    grid_step = pl.program_id(0)
    step = grid_step - builds

    def first_products(rows, next_rows, which=(0, 1, 2)):
        x = rows[...]
        x3 = x[:, 0:384]
        if 0 in which:
            z1_c[...] = nt(w1c[...], jnp.concatenate([x3, x], axis=1))
        if 1 in which:
            z1_a[...] = nt(w1a[...], jnp.concatenate([x3, x3], axis=1))
        if 2 in which:
            z1_t[...] = nt(w1_t[...], next_rows[...])

    def gradients(rows, which=range(6)):
        x = rows[...]
        if 0 in which:
            g2c[...] += nt(h1c[...], dz2c[...])
        if 1 in which:
            g3c[...] += nt(doc[...], h2c[...])
        if 2 in which:
            g1c[...] += nn(dz1c[...], x)
        if 3 in which:
            g2a[...] += nt(h1a[...], dz2a[...])
        if 4 in which:
            g3a[...] += nt(doa[...], h2a[...])
        if 5 in which:
            g1a[...] += nn(dz1a[...], x[:, 0:384])

    @pl.when(grid_step == 0)
    def _():
        wide[...] = jnp.zeros_like(wide)
        tall[...] = jnp.zeros_like(tall)
        peaks[...] = jnp.zeros_like(peaks)
        listed[...] = jnp.zeros_like(listed)
        count[0] = 0

    @pl.when(grid_step < builds)
    def _():
        build_table(grid_step, block, obs, nxt, act, misc_wide, table, wide)
        build_own(grid_step, half // builds, noise_own, misc_own, own_table, tall)
        choose(grid_step, half // builds, misc_own, listed, count)
        for k in range(0, half // builds, LANES):
            peaks[0:1, :] = jnp.maximum(peaks[0:1, :], misc_own[1:2, k : k + LANES])

    @pl.when(grid_step == builds - 1)
    def _():
        @pl.when(meta[0] == 0)
        def _():
            copy_flat(flat_ta, own_actor)
            copy_flat(flat_oa, other_actor)
            copy_flat(flat_tc, own_critic)
            copy_flat(flat_oc, other_critic)

        @pl.when(meta[0] != 0)
        def _():
            copy_flat(flat_ta, other_actor)
            copy_flat(flat_oa, own_actor)
            copy_flat(flat_tc, other_critic)
            copy_flat(flat_oc, own_critic)

        copy = pltpu.make_async_copy(listed, chosen, done)
        copy.start()
        eye = square_eye()
        first_layer(flat_ta, A_ROWS, eye, w1_t, 1, 0)
        first_layer(flat_tc, C_ROWS, eye, w1_t, 1, HID)
        first_layer(flat_oa, A_ROWS, eye, w1a, 2, 0)
        first_layer(flat_oc, C_ROWS, eye, w1c, 2, 0)
        action_layer(flat_tc, eye, square, wa_t, None, None)
        action_layer(flat_oc, eye, square, wa_o, w1c, wa_back)
        actor_head(flat_ta, A_ROWS, w3_ta, bias3_ta, None)
        actor_head(flat_oa, A_ROWS, w3_oa, bias3_oa, w3a_back)
        critic_head(flat_tc, C_ROWS, eye, w3_tc, bias3_tc, None)
        mean_row = critic_head(flat_oc, C_ROWS, eye, w3_oc, bias3_oc, w3c_back)
        second_layer(flat_ta, A_ROWS, eye, w2_ta, None)
        second_layer(flat_tc, C_ROWS, eye, w2_tc, None)
        second_layer(flat_oa, A_ROWS, eye, w2a, w2a_back)
        second_layer(flat_oc, C_ROWS, eye, w2c, w2c_back, w2q_back, mean_row)
        second_biases(
            ((flat_ta, A_ROWS), (flat_tc, C_ROWS), (flat_oa, A_ROWS), (flat_oc, C_ROWS)), eye, bias2
        )
        copy.wait()
        for ref in (g1a, g1c, g2a, g2c, g3a, g3c, gb2a, gb2c, gb3a, gb3c, sums):
            ref[...] = jnp.zeros_like(ref)
        for ref in (h1c, h2c, dz1c, dz2c, doc, h1a, h2a, dz1a, dz2a, doa):
            ref[...] = jnp.zeros_like(ref)
        fetch_rows(chosen, 0, table, own_table, got, 0, TILE)
        turn_rows(got, states, nexts_after, aux)
        first_products(states, nexts_after)
        states_before[...] = states[...]

    @pl.when((grid_step >= builds) & (step * TILE < count[0]))
    def _():
        alpha = jnp.exp(jnp.full((1, SUB), log_alpha[0], F32))
        col0 = spread_lanes(w3c_back[:, 0:LANES])
        col1 = spread_lanes(w3c_back[:, LANES : 2 * LANES])
        pad = jnp.zeros((32 - ACT, SUB), F32)
        gap = jnp.zeros((24 - ACT, SUB), F32)
        row16 = lax.broadcasted_iota(jnp.int32, (16, SUB), 0)

        def head(weights, hidden, bias, size):
            tick()
            both = nn(weights[...], hidden)
            return both[0:size, :] + both[size : 2 * size, :] + spread_lanes(bias)

        def tick():
            task = beside.pop(0) if beside else None
            if task is not None:
                task()

        def gelu_t(t):
            tick()
            return gelu(t)

        def pair_t(t):
            tick()
            return gelu_pair(t)

        def nn_t(left, right):
            tick()
            return nn(left, right)

        def part(sub):
            lanes = slice(sub * SUB, (sub + 1) * SUB)
            noise = aux[AUX_ROWS : AUX_ROWS + 2 * ACT + 1, lanes]
            place = step * TILE + sub * SUB + lax.broadcasted_iota(jnp.int32, (1, SUB), 1)
            counted = (place < count[0]).astype(F32)
            importance = aux[AUX_ROWS + OWN_WEIGHT + 1 : AUX_ROWS + OWN_WEIGHT + 2, lanes]
            weight = counted * importance
            h1 = gelu_t(z1_t[0:HID, lanes])
            z2_t = nn_t(w2_ta[...], h1) + spread_lanes(bias2[:, 0 * LANES : 1 * LANES])
            hidden_a, s1a = pair_t(z1_a[:, lanes])
            z2_a = nn_t(w2a[...], twice(hidden_a)) + spread_lanes(bias2[:, 2 * LANES : 3 * LANES])
            hidden_c, s1c = pair_t(z1_c[:, lanes])
            z2_c = nn_t(w2c[...], twice(hidden_c)) + spread_lanes(bias2[:, 3 * LANES : 4 * LANES])
            yield
            h2 = gelu_t(z2_t)
            out = head(w3_ta, h2, bias3_ta[...], 48)
            last_a, s2a = pair_t(z2_a)
            out_a = head(w3_oa, last_a, bias3_oa[...], 48)
            last_c, s2c = pair_t(z2_c)
            both = nn_t(w3_oc[...], last_c)
            out_c = both[0:8, :] + both[16:24, :] + spread_lanes(bias3_oc[...])
            yield
            next_action, next_logp, _, _ = policy_parts(out, noise[0:ACT, :])
            z1_n = z1_t[HID:, lanes] + nn_t(wa_t[...], stacked_action(next_action, pad))
            shocks = noise[ACT : 2 * ACT, :]
            action, logp, spread_a, slope_a = policy_parts(out_a, shocks)
            old_action = aux[0:ACT, lanes] + aux[AUX_LOW : AUX_LOW + ACT, lanes]
            z1_q = z1_c[:, lanes] + nn_t(wa_o[...], stacked_action(action - old_action, pad))
            yield
            h1 = gelu_t(z1_n)
            z2_n = nn_t(w2_tc[...], h1) + spread_lanes(bias2[:, 1 * LANES : 2 * LANES])
            h1q, s1q = pair_t(z1_q)
            z2_q = nn_t(w2c[...], twice(h1q)) + spread_lanes(bias2[:, 3 * LANES : 4 * LANES])
            yield
            h2 = gelu_t(z2_n)
            both = nn_t(w3_tc[...], h2)
            out_t = both[0:8, :] + both[16:24, :] + spread_lanes(bias3_tc[...])
            h2q, s2q = pair_t(z2_q)
            both = nn_t(w3_oc[...], h2q)
            value_now = both[0:1, :] + both[16:17, :] + spread_lanes(bias3_oc[0:1, :])
            dz1q = nn_t(w2q_back[...], twice(s2q.astype(BF16))) * s1q
            yield
            both = nn_t(wa_back[...], dz1q.astype(BF16))
            value_back = both[0:ACT, :] + both[32 : 32 + ACT, :]
            next_spread = softplus(out_t[1:2, :]) + 0.1
            reward = aux[AUX_REWARD : AUX_REWARD + 1, lanes]
            goal = reward + DISCOUNT * (
                out_t[0:1, :] + next_spread * noise[2 * ACT : 2 * ACT + 1, :] - alpha * next_logp
            )
            q_value = out_c[0:1, :]
            soft, slope = softplus_pair(out_c[1:2, :])
            spread = soft + 0.1
            inverse = 1.0 / spread
            square_inverse = inverse * inverse
            miss = goal - q_value
            bound = jnp.minimum(jnp.maximum(miss, -3.0 * spread), 3.0 * spread)
            critic_loss = weight * (
                0.5 * miss * miss * square_inverse
                + 0.5 * bound * bound * square_inverse
                + jnp.log(spread)
            )
            mean_back = -weight * miss * square_inverse
            spread_back = weight * (1.0 - bound * bound * square_inverse) * inverse * slope
            dz2 = (col0 * mean_back + col1 * spread_back) * s2c
            back = dz2.astype(BF16)
            gb2c[...] += fold(dz2)
            dz1 = nn_t(w2c_back[...], twice(back)) * s1c
            do_c = jnp.where(
                row16 == 0,
                jnp.broadcast_to(mean_back, (16, SUB)),
                jnp.where(row16 == 1, jnp.broadcast_to(spread_back, (16, SUB)), 0.0),
            )
            gb3c[...] += fold(do_c)
            dz2c[:, lanes] = back
            dz1c[:, lanes] = dz1.astype(BF16)
            doc[:, lanes] = do_c.astype(BF16)
            h1c[:, lanes] = hidden_c
            h2c[:, lanes] = last_c
            yield
            counted_alpha = counted * alpha
            d_pre = counted_alpha * 2.0 * action - counted * value_back * (1.0 - action * action)
            d_raw = (d_pre * shocks - counted_alpha / spread_a) * slope_a
            do_a = jnp.concatenate([d_pre, gap, d_raw, gap], axis=0)
            high, low = split(ROOT_TWO * do_a)
            dz2 = nn_t(w3a_back[...], jnp.concatenate([high, low, high], axis=0)) * s2a
            back = dz2.astype(BF16)
            gb2a[...] += fold(dz2)
            gb3a[...] += fold(do_a)
            sums[0:1, :] += fold(counted)
            sums[1:2, :] += fold(counted * logp)
            sums[2:3, :] += fold(critic_loss)
            sums[3:4, :] += fold(counted * (alpha * logp - value_now))
            yield
            dz1 = nn_t(w2a_back[...], twice(back)) * s1a
            dz2a[:, lanes] = back
            dz1a[:, lanes] = dz1.astype(BF16)
            doa[:, lanes] = high
            h1a[:, lanes] = hidden_a
            h2a[:, lanes] = last_a

        first_pick = jnp.minimum(step + 1, tiles - 1) * (TILE // LANES)

        fetches = [
            lambda k=k: fetch_rows(chosen, first_pick, table, own_table, got, k, k + 16)
            for k in range(0, TILE, 16)
        ]
        sums_before = [
            lambda which=which: gradients(states_before, (which,)) for which in range(6)
        ]
        products_after = [
            lambda: turn_rows(got, states_after, nexts_after, aux_after),
            lambda: first_products(states_after, nexts_after, (0,)),
            lambda: first_products(states_after, nexts_after, (1,)),
            lambda: first_products(states_after, nexts_after, (2,)),
        ]
        beside = []
        for k, fetch in enumerate(fetches):
            beside.append(fetch)
            if k % 5 == 2 and sums_before:
                beside.append(sums_before.pop(0))
        for product in products_after:
            beside += [product, None, None, None, None]

        running = [part(sub) for sub in range(TILE // SUB)]
        while running:
            running = [piece for piece in running if next(piece, True) is None]
        while beside:
            tick()
        states_before[...] = states[...]
        states[...] = states_after[...]
        aux[...] = aux_after[...]

    @pl.when(step == tiles - 1)
    def _():
        gradients(states_before)
        total[...] = jnp.zeros_like(total)

        def sum_row(block):
            return jnp.sum(block.T, axis=0, keepdims=True)

        for side in (0, 1):
            at = side * LANES
            turned = 0.5 * g1a[at : at + LANES, :].T
            total[A_W1[side] : A_W1[side] + OBS, :] = turned[0:OBS, :]
            total[A_B + side : A_B + side + 1, :] = turned[ONE_LANE : ONE_LANE + 1, :]
            total[A_W2[side] : A_W2[side] + HID, :] = (0.5 * ROOT_HALF) * g2a[:, at : at + LANES]
            total[A_W3[side] : A_W3[side] + ACT, :] = 0.5 * g3a[0:ACT, at : at + LANES]
            total[A_W3[side] + ACT : A_W3[side] + 2 * ACT, :] = (
                0.5 * g3a[24 : 24 + ACT, at : at + LANES]
            )
            total[A_B + 2 + side : A_B + 3 + side, :] = 0.5 * sum_row(gb2a[at : at + LANES, :])
            turned = 0.5 * g1c[at : at + LANES, :].T
            total[C_W1[side] : C_W1[side] + OBS, :] = turned[0:OBS, :]
            total[C_W1[side] + OBS : C_W1[side] + OBS + ACT, :] = (
                turned[384 : 384 + ACT, :] + turned[384 + AUX_LOW : 384 + AUX_LOW + ACT, :]
            )
            total[C_B + side : C_B + side + 1, :] = turned[ONE_LANE : ONE_LANE + 1, :]
            total[C_W2[side] : C_W2[side] + HID, :] = (0.5 * ROOT_HALF) * g2c[:, at : at + LANES]
            total[C_W3[side] : C_W3[side] + 2, :] = ROOT_HALF * g3c[0:2, at : at + LANES]
            total[C_B + 2 + side : C_B + 3 + side, :] = 0.5 * sum_row(gb2c[at : at + LANES, :])
        none = jnp.zeros((LANES - 2 * ACT, LANES), F32)
        total[A_B + 4 : A_B + 5, :] = sum_row(
            jnp.concatenate([gb3a[0:ACT, :], gb3a[24 : 24 + ACT, :], none], axis=0)
        )
        none = jnp.zeros((LANES - 16, LANES), F32)
        total[C_B + 4 : C_B + 5, :] = sum_row(jnp.concatenate([gb3c[...], none], axis=0))
        total[EXTRA : EXTRA + 4, :] = sums[0:4, :]
        peak = jnp.max(peaks[0:1, :], axis=1, keepdims=True)
        for k in range(EXTRA + 8 - EXTRA_SLOTS):
            total[EXTRA_SLOTS + k : EXTRA_SLOTS + k + 1, :] = jnp.where(
                lanes_of(1) + k * LANES == meta[1], jnp.broadcast_to(peak, (1, LANES)), 0.0
            )
        count = keep.shape[0] // chunk
        for p in range(count):
            at = pl.multiple_of((meta[1] ^ p) * chunk, 8)
            keep[p * chunk : (p + 1) * chunk, :] = total[pl.ds(at, chunk), :]
            at = pl.multiple_of((meta[1] ^ (p + count)) * chunk, 8)
            send[p * chunk : (p + 1) * chunk, :] = total[pl.ds(at, chunk), :]


def losses(
    meta, log_alpha, obs, nxt, act, noise, misc, own_a, other_a, own_c, other_c, devices
):
    rows = obs.shape[1]
    half = noise.shape[1] // 2
    tiles = -(-half // TILE)
    block = next(size for size in (1280, 640, 512, 256, 128) if rows % size == 0)
    builds = rows // block
    own = half // builds
    list_rows = -(-(tiles * (TILE // LANES) + 1) // 8) * 8
    chunk = chunk_rows(devices)
    buffer_rows = chunk * devices

    def fixed(i, meta):
        return (0, 0)

    def source(i, meta):
        return (0, jnp.minimum(i, builds - 1))

    def own_source(i, meta):
        return (0, meta[0] * builds + jnp.minimum(i, builds - 1))

    def body(*refs):
        loss_kernel(builds, tiles, half, chunk, block, *refs)

    def bf(*shape):
        return pltpu.VMEM(shape, BF16)

    def f32(*shape):
        return pltpu.VMEM(shape, F32)

    features = noise.shape[0]
    once = pl.Buffered(1)
    return pl.pallas_call(
        body,
        out_shape=(
            jax.ShapeDtypeStruct((buffer_rows // 2, LANES), F32),
            jax.ShapeDtypeStruct((buffer_rows // 2, LANES), F32),
        ),
        grid_spec=pltpu.PrefetchScalarGridSpec(
            num_scalar_prefetch=1,
            grid=(builds + tiles,),
            in_specs=[
                pl.BlockSpec(memory_space=pltpu.SMEM),
                pl.BlockSpec((OBS, block), source),
                pl.BlockSpec((OBS, block), source),
                pl.BlockSpec((ACT, block), source),
                pl.BlockSpec((8, block), source),
                pl.BlockSpec((features, own), own_source),
                pl.BlockSpec((8, own), own_source),
                pl.BlockSpec((1, A_SIZE), fixed, pipeline_mode=once),
                pl.BlockSpec((1, A_SIZE), fixed, pipeline_mode=once),
                pl.BlockSpec((1, C_SIZE), fixed, pipeline_mode=once),
                pl.BlockSpec((1, C_SIZE), fixed, pipeline_mode=once),
            ],
            out_specs=(
                pl.BlockSpec((buffer_rows // 2, LANES), fixed),
                pl.BlockSpec((buffer_rows // 2, LANES), fixed),
            ),
            scratch_shapes=[
                f32(A_FLAT, LANES), f32(A_FLAT, LANES), f32(C_FLAT, LANES), f32(C_FLAT, LANES),
                bf(512, 384), bf(HID, 768), bf(HID, 896),
                bf(HID, LANES), bf(HID, LANES), bf(64, HID),
                bf(HID, HID), bf(HID, HID),
                bf(HID, 512), bf(HID, 512), bf(HID, 512), bf(HID, 512), bf(HID, 512),
                f32(HID, 4 * LANES), bf(96, HID), bf(96, HID), bf(32, HID), bf(32, HID),
                bf(HID, 144), f32(HID, 2 * LANES),
                f32(48, LANES), f32(48, LANES), f32(8, LANES), f32(8, LANES),
                f32(32, HID),
                f32(HID, 384), f32(HID, 512), f32(HID, HID), f32(HID, HID),
                f32(48, HID), f32(16, HID), f32(HID, LANES), f32(HID, LANES),
                f32(48, LANES), f32(16, LANES), f32(8, LANES), f32(buffer_rows, LANES),
                f32(2 * HID, TILE), f32(HID, TILE), f32(HID, TILE),
                bf(HID, TILE), bf(HID, TILE), bf(HID, TILE), bf(HID, TILE), bf(16, TILE),
                bf(HID, TILE), bf(HID, TILE), bf(HID, TILE), bf(HID, TILE), bf(48, TILE),
                f32(rows * 8, LANES), f32(TILE * 8, LANES), f32(LANES, block),
                bf(TILE, 512), bf(TILE, 512), bf(TILE, 512), bf(TILE, 384),
                f32(AUX_ROWS + OWN_ROWS, TILE), f32(AUX_ROWS + OWN_ROWS, TILE),
                f32(half, LANES), f32(LANES, own),
                pltpu.VMEM((2, list_rows, LANES), jnp.int32),
                pltpu.SMEM((2, list_rows, LANES), jnp.int32),
                pltpu.SMEM((1,), jnp.int32), f32(8, LANES), pltpu.SemaphoreType.DMA,
            ],
        ),
        compiler_params=pltpu.CompilerParams(
            dimension_semantics=("arbitrary",), vmem_limit_bytes=VMEM_BYTES
        ),
        name="losses",
    )(meta, log_alpha, obs, nxt, act, misc, noise, misc, own_a, other_a, own_c, other_c)


def stat_pieces(width_in, width_out):
    sizes = [width_in, HID, HID, HID, HID, width_out, HID, HID, width_out]
    starts = [sum(sizes[:k]) for k in range(len(sizes))]
    rows = [-(-size // LANES) for size in sizes]
    return sizes, starts, [sum(rows[:k]) for k in range(len(rows))], sum(rows)


def aligned_stats(statistics, width_in, width_out):
    sizes, starts, _, rows = stat_pieces(width_in, width_out)
    pieces = [
        jnp.pad(statistics[start : start + size], (0, -size % LANES))
        for size, start in zip(sizes, starts)
    ]
    pieces.append(jnp.zeros((-rows % 8 * LANES,), F32))
    return jnp.concatenate(pieces).reshape(-1, LANES)


def store_line(out, lead, value):
    size = out.shape[-1]
    count = value.shape[0]
    whole = size // 1024
    for k in range(whole):
        part = value[8 * k : 8 * k + 8, :]
        out[pl.ds(1024 * k, 1024)] = part.reshape(1024)
    for k in range(8 * whole, count):
        width = min(LANES, size - k * LANES)
        if width > 0:
            out[pl.ds(k * LANES, width)] = value[k : k + 1, 0:width].reshape(width)


def net_update(
    total, scale, old_stats, width_in, width_out, w1, w2, w3, bias_at, rows, fg, fu, stats_out
):
    sizes, starts, first, _ = stat_pieces(width_in, width_out)
    lines = [[] for _ in sizes]

    def old_row(piece, k):
        return old_stats[first[piece] + k : first[piece] + k + 1, :]

    def blend(old, new):
        return DECAY_RATE * old + (1.0 - DECAY_RATE) * new

    def clip_scale(square_sum, number):
        root = jnp.sqrt(square_sum / number)
        return 1.0 / jnp.maximum(1.0, root / CLIP_LEVEL)

    def whole_sum(value):
        return jnp.sum(jnp.sum(value, axis=0, keepdims=True), axis=1, keepdims=True)

    for layer, (places, height, flat_at) in enumerate(
        ((w1, width_in, 0), (w2, HID, rows[0]))
    ):
        parts = [total[at : at + height, :] * scale for at in places]
        squares = [g * g + TINY_TERM for g in parts]
        blocks = -(-height // LANES)
        old = jnp.concatenate([column(old_row(layer, k)) for k in range(blocks)], axis=0)
        old = old[0:height, :]
        mean = jnp.sum(squares[0] + squares[1], axis=1, keepdims=True) * (1.0 / HID)
        row_stat = blend(old, jnp.broadcast_to(mean, (height, LANES)))
        for k in range(blocks):
            block = row_stat[k * LANES : min(height, (k + 1) * LANES), :]
            if block.shape[0] < LANES:
                block = jnp.concatenate(
                    [block, jnp.zeros((LANES - block.shape[0], LANES), F32)], axis=0
                )
            lines[layer].append(block.T[0:1, :])
        mean_row = jnp.sum(row_stat, axis=0, keepdims=True) * (1.0 / height)
        row_root = lax.rsqrt(row_stat)
        steps = []
        for side in (0, 1):
            col_stat = blend(
                old_row(3 + layer, side),
                jnp.sum(squares[side], axis=0, keepdims=True) * (1.0 / height),
            )
            lines[3 + layer].append(col_stat)
            steps.append((parts[side] * row_root) * (lax.rsqrt(col_stat) * jnp.sqrt(mean_row)))
        factor = clip_scale(
            whole_sum(steps[0] * steps[0] + steps[1] * steps[1]), float(height * HID)
        )
        for side in (0, 1):
            fg[pl.ds(flat_at + side, height, stride=2), :] = parts[side]
            fu[pl.ds(flat_at + side, height, stride=2), :] = steps[side] * factor

    tall = -(-width_out // 8) * 8
    parts = [total[at : at + tall, :] * scale for at in w3]
    real = rows_of(tall) < width_out
    squares = [jnp.where(real, g * g + TINY_TERM, 0.0) for g in parts]
    old = column(old_row(5, 0))[0:tall, :]
    mean = jnp.sum(squares[0] + squares[1], axis=1, keepdims=True) * (1.0 / HID)
    col_stat = blend(old, jnp.broadcast_to(mean, (tall, LANES)))
    lines[5].append(
        jnp.concatenate([col_stat, jnp.zeros((LANES - tall, LANES), F32)], axis=0).T[0:1, :]
    )
    row_stats = []
    for side in (0, 1):
        row_stats.append(
            blend(
                old_row(2, side),
                jnp.sum(squares[side], axis=0, keepdims=True) * (1.0 / width_out),
            )
        )
        lines[2].append(row_stats[side])
    mean_row = jnp.sum(row_stats[0] + row_stats[1], axis=1, keepdims=True) * (1.0 / HID)
    col_root = jnp.where(real, lax.rsqrt(col_stat), 0.0)
    steps = [
        (parts[side] * lax.rsqrt(row_stats[side])) * (col_root * jnp.sqrt(mean_row))
        for side in (0, 1)
    ]
    factor = clip_scale(
        whole_sum(steps[0] * steps[0] + steps[1] * steps[1]), float(HID * width_out)
    )
    pad = jnp.zeros((LANES - tall, LANES), F32)
    size = rows[2] - rows[1]
    padded = -(-size // 8) * 8
    for flat, pair in ((fg, parts), (fu, [u * factor for u in steps])):
        turned = jnp.concatenate(
            [
                jnp.concatenate([jnp.where(real, pair[side], 0.0), pad], axis=0).T
                for side in (0, 1)
            ],
            axis=0,
        )
        flat[rows[1] : rows[1] + size, :] = flatten(turned, width_out, padded)[0:size, :]

    grad = total[bias_at : bias_at + 8, :] * scale
    line = rows_of(8)
    lane = lanes_of(8)
    real = (line < 4) | ((line == 4) & (lane < width_out))
    grad = jnp.where(real, grad, 0.0)
    stat = blend(old_stats[first[6] : first[6] + 5, :], grad[0:5, :] * grad[0:5, :] + TINY_TERM)
    step = jnp.where(real[0:5, :], grad[0:5, :] * lax.rsqrt(stat), 0.0)
    factor = clip_scale(whole_sum(step * step), float(2 * HID + width_out))
    fg[rows[2] : rows[2] + 5, :] = grad[0:5, :]
    fu[rows[2] : rows[2] + 5, :] = step * factor
    for k in range(5):
        lines[6 + k // 2].append(stat[k : k + 1, :])

    size = stats_out.shape[0]
    count = -(-size // LANES)
    made = [jnp.zeros((1, LANES), F32) for _ in range(count + 1)]
    lane = lanes_of(1)
    for piece, pieces in enumerate(lines):
        for k, value in enumerate(pieces):
            start = starts[piece] + k * LANES
            width = min(LANES, sizes[piece] - k * LANES)
            value = jnp.where(lane < width, value, 0.0)
            shift = start % LANES
            at = start // LANES
            if shift:
                value = pltpu.roll(value, shift, 1)
            made[at] = made[at] + jnp.where(lane >= shift, value, 0.0)
            if shift:
                made[at + 1] = made[at + 1] + jnp.where(lane < shift, value, 0.0)
    for k in range(count):
        width = min(LANES, size - k * LANES)
        stats_out[pl.ds(k * LANES, width)] = made[k][:, 0:width].reshape(width)


def write_net(side, own, other, fg, fu, slot, copy, grad):
    size = own.shape[1]
    whole = size // 1024

    def piece(at, row, width, count):
        mine = own[0:1, pl.ds(at, width)].reshape(count, width // count)
        theirs = other[0:1, pl.ds(at, width)].reshape(count, width // count)
        wide = width // count
        step = fu[pl.ds(row, count), 0:wide]
        online = jnp.where(side == 0, theirs, mine)
        new = online - LEARN_RATE * step
        held = jnp.where(side == 0, POLYAK_RATE * new + (1.0 - POLYAK_RATE) * mine, new)
        slot[0:1, pl.ds(at, width)] = held.reshape(1, width)
        copy[0:1, pl.ds(at, width)] = held.reshape(1, width).astype(BF16)
        grad[pl.ds(at, width)] = fg[pl.ds(row, count), 0:wide].reshape(width)

    for k in range(whole):
        piece(k * 1024, k * 8, 1024, 8)
    full = size // LANES
    for row in range(whole * 8, full):
        piece(row * LANES, row, LANES, 1)
    piece(full * LANES, full, size - full * LANES, 1)


def update_kernel(
    chunk, devices,
    meta, log_alpha, mine, theirs, own_a, other_a, own_c, other_c, stats_a, stats_c,
    slot_a, slot_c, copy_a, copy_c, grad_a, grad_c, new_a, new_c, summary, alpha_out,
    total, fg_a, fu_a, fg_c, fu_c,
):
    count = devices // 2
    for p in range(count):
        at = pl.multiple_of((meta[1] ^ p) * chunk, 8)
        total[pl.ds(at, chunk), :] = mine[p * chunk : (p + 1) * chunk, :]
        at = pl.multiple_of((meta[1] ^ (p + count)) * chunk, 8)
        total[pl.ds(at, chunk), :] = theirs[p * chunk : (p + 1) * chunk, :]

    sums = jnp.sum(total[EXTRA : EXTRA + 8, :], axis=1, keepdims=True)
    peak = jnp.max(total[EXTRA_SLOTS : EXTRA + 8, :], axis=1, keepdims=True)
    peak = jnp.max(peak, axis=0, keepdims=True)
    counted = sums[0:1, :]
    scale_a = 1.0 / counted
    scale_c = scale_a / peak
    lane = lanes_of(1)
    line = jnp.where(
        lane == 0,
        jnp.broadcast_to(sums[2:3, :] / peak, (1, LANES)),
        jnp.where(
            lane == 1,
            jnp.broadcast_to(sums[3:4, :], (1, LANES)),
            jnp.broadcast_to(counted, (1, LANES)),
        ),
    )
    summary[...] = line
    alpha_out[...] = log_alpha[0] + ALPHA_STEP * (
        jnp.broadcast_to(sums[1:2, :] / counted, (1, LANES)) - ACT
    )
    net_update(
        total, scale_a, stats_a, OBS, 2 * ACT, A_W1, A_W2, A_W3, A_B, A_ROWS, fg_a, fu_a, new_a
    )
    net_update(
        total, scale_c, stats_c, OBS + ACT, 2, C_W1, C_W2, C_W3, C_B, C_ROWS, fg_c, fu_c, new_c
    )
    write_net(meta[0], own_a, other_a, fg_a, fu_a, slot_a, copy_a, grad_a)
    write_net(meta[0], own_c, other_c, fg_c, fu_c, slot_c, copy_c, grad_c)


def update(meta, log_alpha, mine, theirs, own_a, other_a, own_c, other_c, stats_a, stats_c, sizes, devices):
    chunk = chunk_rows(devices)

    def body(*refs):
        update_kernel(chunk, devices, *refs)

    def f32(*shape):
        return jax.ShapeDtypeStruct(shape, F32)

    smem = pl.BlockSpec(memory_space=pltpu.SMEM)
    vmem = pl.BlockSpec(memory_space=pltpu.VMEM)
    return pl.pallas_call(
        body,
        out_shape=(
            f32(1, A_SIZE), f32(1, C_SIZE),
            jax.ShapeDtypeStruct((1, A_SIZE), BF16), jax.ShapeDtypeStruct((1, C_SIZE), BF16),
            f32(A_SIZE), f32(C_SIZE), f32(sizes[0]), f32(sizes[1]), f32(1, LANES), f32(1, LANES),
        ),
        in_specs=[smem, smem] + [vmem] * 8,
        out_specs=tuple([vmem] * 10),
        scratch_shapes=[
            pltpu.VMEM((chunk * devices, LANES), F32),
            pltpu.VMEM((A_FLAT, LANES), F32), pltpu.VMEM((A_FLAT, LANES), F32),
            pltpu.VMEM((C_FLAT, LANES), F32), pltpu.VMEM((C_FLAT, LANES), F32),
        ],
        compiler_params=pltpu.CompilerParams(vmem_limit_bytes=VMEM_BYTES),
        name="optimizer",
    )(meta, log_alpha, mine, theirs, own_a, other_a, own_c, other_c, stats_a, stats_c)


def chunk_rows(devices):
    return -(-DATA_ROWS // (8 * devices)) * 8


def radices(count):
    found = []
    while count > 1:
        found.append(4 if count % 4 == 0 else 2)
        count //= found[-1]
    return found


def swap_groups(value):
    return lax.ppermute(value, "grp", [(0, 1), (1, 0)])


def exchange(value, mask):
    count = lax.axis_size("dp")
    return lax.ppermute(value, "dp", [(i, i ^ mask) for i in range(count)])


def buffer_place(group_side, count):
    rest = lax.axis_index("dp")
    place = group_side
    for radix in radices(count):
        place = place * radix + rest % radix
        rest = rest // radix
    return place


def all_sum(keep, send):
    stages = radices(lax.axis_size("dp"))
    value = keep + swap_groups(send)
    stride = 1
    for radix in stages:
        rows = value.shape[0] // radix
        parts = [value[k * rows : (k + 1) * rows] for k in range(radix)]
        came = [exchange(parts[k], k * stride) for k in range(1, radix)]
        value = parts[0]
        for part in came:
            value = value + part
        stride *= radix
    for radix in reversed(stages):
        stride //= radix
        value = jnp.concatenate(
            [value] + [exchange(value, k * stride) for k in range(1, radix)], axis=0
        )
    return value, swap_groups(value)


def shards(
    obs_rows,
    next_rows,
    action_rows,
    reward_rows,
    batch_index,
    valid_mask,
    noise,
    importance,
    actor_params,
    critic_params,
    actor_stats,
    critic_stats,
    log_alpha,
):
    devices = lax.axis_size("dp") * lax.axis_size("grp")
    group_side = lax.axis_index("grp")
    other_a = swap_groups(actor_params)
    other_c = swap_groups(critic_params)
    meta = jnp.stack([group_side, buffer_place(group_side, lax.axis_size("dp"))]).astype(jnp.int32)
    spot = (batch_index // 8) * 64 + batch_index % 8
    blank = jnp.zeros_like(importance)
    misc = jnp.stack(
        [reward_rows, importance, valid_mask.astype(F32), spot.astype(F32), blank, blank, blank, blank]
    )
    keep, send = losses(
        meta, log_alpha, obs_rows.T, next_rows.T, action_rows.T, noise.T, misc,
        actor_params, other_a, critic_params, other_c, devices,
    )
    mine, theirs = all_sum(keep, send)
    (
        slot_a, slot_c, copy_a, copy_c, grad_a, grad_c, new_a, new_c, summary, alpha
    ) = update(
        meta, log_alpha, mine, theirs, actor_params, other_a, critic_params, other_c,
        aligned_stats(actor_stats, OBS, 2 * ACT), aligned_stats(critic_stats, OBS + ACT, 2),
        (actor_stats.shape[0], critic_stats.shape[0]), devices,
    )
    return (
        slot_a, slot_c, copy_a, copy_c, grad_a, grad_c, new_a, new_c,
        summary[0, 0:3], alpha[0, 0:1],
    )


def solution(mesh):
    return jax.shard_map(
        shards,
        mesh=mesh,
        in_specs=(
            P("dp", None),
            P("dp", None),
            P("dp", None),
            P("dp"),
            P("dp"),
            P("dp"),
            P("dp", None),
            P("dp"),
            P("grp", None),
            P("grp", None),
            P(),
            P(),
            P(),
        ),
        out_specs=(
            P("grp", None),
            P("grp", None),
            P("grp", None),
            P("grp", None),
            P(),
            P(),
            P(),
            P(),
            P(),
            P(),
        ),
        check_vma=False,
    )
```

```python
import jax
import jax.numpy as jnp
from jax import lax
from jax.experimental import pallas as pl
from jax.experimental.pallas import tpu as pltpu
from jax.sharding import PartitionSpec as P

OBS = 376
ACT = 17
HID = 256
LANES = 128
TILE = 512
SUB = 256

DISCOUNT = 0.99
POLYAK_RATE = 0.1
DECAY_RATE = 0.5
LEARN_RATE = 0.1
CLIP_LEVEL = 0.1
ALPHA_STEP = 0.01
TINY_TERM = 1e-30
HALF_LOG_TWO_PI = 0.9189385332046727
LOG_TWO = 0.6931471805599453
ROOT_HALF = 0.7071067811865476
ROOT_TWO = 1.4142135623730951
LOG2_E = 1.4426950408889634
LOG2_TWO_OVER_ROOT_PI = 0.17425193548825

F32 = jnp.float32
BF16 = jnp.bfloat16
VMEM_BYTES = 62 * 2**20
UPDATE_VMEM_BYTES = 24 * 2**20

ONE_LANE = OBS
AUX_LOW = 32
AUX_REWARD = 64
AUX_AGAIN = 96
AUX_ROWS = 72
OWN_WEIGHT = 40
OWN_ROWS = 48
MISC_WEIGHT = 1
MISC_VALID = 2
MISC_INDEX = 3


def flat_rows(width_in, width_out):
    w2 = width_in * HID // LANES
    w3 = w2 + HID * HID // LANES
    b1 = w3 + HID * width_out // LANES
    return w2, w3, b1, b1 + 2, b1 + 4


A_ROWS = flat_rows(OBS, 2 * ACT)
C_ROWS = flat_rows(OBS + ACT, 2)
A_SIZE = A_ROWS[4] * LANES + 2 * ACT
C_SIZE = C_ROWS[4] * LANES + 2
A_FLAT = -(-A_SIZE // 1024) * 8
C_FLAT = -(-C_SIZE // 1024) * 8

A_W1 = (0, OBS)
A_W2 = (2 * OBS, 2 * OBS + HID)
A_W3 = (2 * OBS + 2 * HID, 2 * OBS + 2 * HID + 40)
A_B = A_W3[1] + 40
C_W1 = (A_B + 8, A_B + 8 + 400)
C_W2 = (C_W1[1] + 400, C_W1[1] + 400 + HID)
C_W3 = (C_W2[1] + HID, C_W2[1] + HID + 8)
C_B = C_W3[1] + 8
EXTRA = C_B + 8
EXTRA_SLOTS = EXTRA + 4
DATA_ROWS = EXTRA + 8


def nn(left, right):
    return lax.dot_general(
        left, right, (((1,), (0,)), ((), ())), preferred_element_type=F32
    )


def nt(left, right):
    return lax.dot_general(
        left, right, (((1,), (1,)), ((), ())), preferred_element_type=F32
    )


def split(value):
    high = value.astype(BF16)
    return high, (value - high.astype(F32)).astype(BF16)


def twice(value):
    return jnp.concatenate([value, value], axis=0)


def gelu(t):
    return (t * (1.0 + lax.erf(t))).astype(BF16)


def gelu_pair(t):
    double_cdf = 1.0 + lax.erf(t)
    bell = jnp.exp2(LOG2_TWO_OVER_ROOT_PI - LOG2_E * (t * t))
    return (t * double_cdf).astype(BF16), double_cdf + t * bell


def softplus(x):
    return jnp.maximum(x, 0.0) + jnp.log(1.0 + jnp.exp(-jnp.abs(x)))


def softplus_pair(x):
    decay = jnp.exp(-jnp.abs(x))
    inverse = 1.0 / (1.0 + decay)
    return jnp.maximum(x, 0.0) + jnp.log(1.0 + decay), jnp.where(x >= 0.0, inverse, decay * inverse)


def column(row):
    return jnp.broadcast_to(row, (LANES, LANES)).T


def rows_of(count):
    return lax.broadcasted_iota(jnp.int32, (count, LANES), 0)


def lanes_of(count):
    return lax.broadcasted_iota(jnp.int32, (count, LANES), 1)


def square_eye(reverse=False):
    row = lax.broadcasted_iota(jnp.int32, (HID, HID), 0)
    lane = lax.broadcasted_iota(jnp.int32, (HID, HID), 1)
    return (row == (HID - 1 - lane if reverse else lane)).astype(F32).astype(BF16)


def two_pieces(value):
    return jnp.concatenate(split(value), axis=1)


def turns(value, shift, stride):
    turn = (rows_of(HID) * stride + shift) % LANES
    for step in (2, 4, 8, 16, 32, 64):
        value = jnp.where((turn & step) != 0, pltpu.roll(value, step, 1), value)
        yield value


def strided_roll(value, shift, stride):
    for value in turns(value, shift, stride):
        pass
    return value


def unflatten(flat, width):
    rows = flat.shape[0]
    first = (HID - 1 - rows_of(HID)) * width
    lane = lanes_of(HID)
    owner = first // LANES
    picks = jnp.concatenate([(owner == lane), (owner + 1 == lane)], axis=0).astype(F32).astype(BF16)
    found = nn(picks[:, 0:rows], two_pieces(flat))
    yield
    found = found[:, 0:LANES] + found[:, LANES:]
    mixed = jnp.where(lane >= first % LANES, found[0:HID, :], found[HID:, :])
    for turned in turns(mixed, -(HID - 1) * width % LANES, width):
        yield
    pieces = nn(square_eye(True), two_pieces(turned)).astype(BF16)
    yield
    return pieces


def flatten(values, width, rows):
    first = rows_of(HID) * width % LANES
    lane = lanes_of(HID)
    turned = strided_roll(values[0] + pltpu.roll(values[1], 64, 1), 0, width)
    swapped = pltpu.roll(turned, 64, 1)
    begun = (lane >= first) & (lane < first + width)
    wrapped = lane < first + width - LANES
    parts = []
    for value in (turned, swapped):
        parts.append(
            jnp.concatenate([jnp.where(begun, value, 0.0), jnp.where(wrapped, value, 0.0)], axis=0)
        )
    both = jnp.concatenate(parts, axis=1)
    high, low = split(both)
    least = (both - high.astype(F32) - low.astype(F32)).astype(BF16)
    owner = lax.broadcasted_iota(jnp.int32, (rows, HID), 1) * width // LANES
    row = lax.broadcasted_iota(jnp.int32, (rows, HID), 0)
    places = jnp.concatenate([owner == row, owner + 1 == row], axis=1).astype(F32).astype(BF16)
    found = nn(places, jnp.concatenate([high, low, least], axis=1))
    found = found[:, 0:HID] + found[:, HID : 2 * HID] + found[:, 2 * HID :]
    return found[:, 0:LANES], found[:, LANES:]


def build_table(step, block, obs, nxt, act, misc, table, wide):
    groups = block // 8
    table3 = table.reshape(table.shape[0] // 64, 64, LANES)
    at = pl.multiple_of(step * groups, groups)

    def put(value, first):
        for c in range(value.shape[1] // LANES):
            table3[pl.ds(at, groups), 8 * (first + c) : 8 * (first + c) + 8, :] = value[
                :, LANES * c : LANES * (c + 1)
            ].reshape(groups, 8, LANES)

    ones = (lax.broadcasted_iota(jnp.int32, (8, block), 0) == 0).astype(F32)
    whole = OBS // 16 * 16

    def padded(source):
        value = source[...]
        rest = jnp.concatenate([value[whole:, :].astype(F32), ones], axis=0).astype(BF16)
        return jnp.concatenate([value[0:whole, :], rest], axis=0)

    value = padded(obs)
    eye = square_eye()
    turned = [nt(eye, value[:, k : k + HID]) for k in range(0, block, HID)]
    put(jnp.concatenate(turned, axis=0), 0)
    put(padded(nxt).T.astype(F32), 3)
    action = act[...]
    high = action.astype(BF16).astype(F32)
    wide[0:ACT, :] = high
    wide[AUX_LOW : AUX_LOW + ACT, :] = action - high
    wide[AUX_AGAIN : AUX_AGAIN + ACT, :] = high
    wide[AUX_REWARD : AUX_REWARD + 8, :] = misc[...]
    put(wide[...].T, 6)


def choose(size, noise, misc, listed, gathered, count):
    lane = lanes_of(1)
    wide_lane = lanes_of(OWN_ROWS)
    parts = size // LANES
    counted = misc[MISC_VALID : MISC_VALID + 1, :]
    flags = [counted[:, LANES * k : LANES * (k + 1)] for k in range(parts)]
    stacked = jnp.concatenate(flags + [jnp.zeros((-parts % 16, LANES), F32)], axis=0).astype(BF16)
    before = nn(stacked, (rows_of(LANES) < lanes_of(LANES)).astype(F32).astype(BF16))
    before = before.astype(jnp.int32)
    index = misc[MISC_INDEX : MISC_INDEX + 1, :].astype(jnp.int32)
    spot = ((index >> 3) << 6) + (index & 7)
    digits = jnp.concatenate([spot >> 8, spot & 255] + [jnp.zeros_like(spot)] * 14, axis=0)
    gap = jnp.zeros((OWN_WEIGHT - 2 * ACT - 1, size), F32)
    high, low = split(jnp.concatenate([noise[...], gap, misc[...]], axis=0))
    value = jnp.concatenate([digits.astype(F32).astype(BF16), high, low], axis=0)
    place = count[0]
    for k in range(parts):
        where = (before[k : k + 1, :] + place) & (LANES - 1)
        where = jnp.where(flags[k] > 0.0, where, -1)
        hit = (jnp.broadcast_to(where, (LANES, LANES)) == rows_of(LANES)).astype(F32).astype(BF16)
        moved = nt(value[:, LANES * k : LANES * (k + 1)], hit)
        spots = moved[0:2, :].astype(jnp.int32)
        spots = (spots[0:1, :] << 8) + spots[1:2, :]
        values = moved[16 : 16 + OWN_ROWS, :] + moved[16 + OWN_ROWS :, :]
        row = place >> 7
        start = place & (LANES - 1)
        listed[pl.ds(row, 1), :] += jnp.where(lane >= start, spots, 0)
        listed[pl.ds(row + 1, 1), :] += jnp.where(lane >= start, 0, spots)
        gathered[row] += jnp.where(wide_lane >= start, values, 0.0)
        gathered[row + 1] += jnp.where(wide_lane >= start, 0.0, values)
        place = place + jnp.sum(flags[k]).astype(jnp.int32)
    count[0] = place


def fetch_rows(chosen, first, table, got, start, stop, batch=16):
    for base in range(start, stop, batch):
        found = [
            table[pl.ds(chosen[first + j // LANES, j % LANES], 8, stride=8), :]
            for j in range(base, base + batch)
        ]
        for j in range(base, base + batch):
            got[pl.ds((j // 8) * 64 + j % 8, 8, stride=8), :] = found[j - base]


def turn_rows(got, states, nexts, aux):
    got3 = got.reshape(TILE // 8, 64, LANES)

    def chunk(c):
        return got3[:, 8 * c : 8 * c + 8, :].reshape(TILE, LANES)

    for c in range(3):
        states[:, LANES * c : LANES * (c + 1)] = chunk(c).astype(BF16)
        nexts[:, LANES * c : LANES * (c + 1)] = chunk(3 + c).astype(BF16)
    extra = chunk(6)
    states[:, 3 * LANES :] = extra.astype(BF16)
    aux[...] = extra.T[0:AUX_ROWS, :]


def copy_flat(flat, source):
    size = source.shape[1]
    whole = size // 1024

    for k in range(whole):
        flat[8 * k : 8 * k + 8, :] = source[0:1, 1024 * k : 1024 * (k + 1)].reshape(8, LANES)
    flat[8 * whole : 8 * whole + 8, :] = jnp.zeros((8, LANES), F32)
    full = (size - whole * 1024) // LANES
    for k in range(full):
        flat[8 * whole + k : 8 * whole + k + 1, :] = source[
            0:1, whole * 1024 + k * LANES : whole * 1024 + (k + 1) * LANES
        ]
    rest = size - whole * 1024 - full * LANES
    flat[8 * whole + full : 8 * whole + full + 1, 0:rest] = source[0:1, size - rest : size]


def halves(flat, start, height):
    return [flat[pl.ds(start + side, height, stride=2), :] for side in (0, 1)]


def natural(flat, start, height):
    return jnp.concatenate([flat[pl.ds(start + side, height, stride=2), :] for side in (0, 1)], axis=1)


def bias_row(flat, at):
    return jnp.concatenate([flat[at : at + 1, :], flat[at + 1 : at + 2, :]], axis=1)


def first_layer(flat, rows, eye, dst, pieces, base):
    tile = lax.broadcasted_iota(jnp.int32, (8, HID), 0)
    bias = jnp.where(tile == 0, jnp.broadcast_to(bias_row(flat, rows[2]), (8, HID)), 0.0)
    parts = split(jnp.concatenate([natural(flat, 0, OBS), bias], axis=0) * ROOT_HALF)
    for k in range(pieces):
        dst[base : base + HID, 384 * k : 384 * (k + 1)] = nt(eye, parts[k]).astype(BF16)


def action_layer(flat, eye, square, stack, first, back):
    square[0:ACT, :] = natural(flat, 2 * OBS, ACT)
    square[ACT:, :] = jnp.zeros((32 - ACT, HID), F32)
    value = square[...]
    high, low = split(value * ROOT_HALF)
    none = jnp.zeros_like(high)
    stack[...] = nt(eye, jnp.concatenate([high, high, low, none], axis=0)).astype(BF16)
    if first is not None:
        first[:, 768:896] = nt(eye, jnp.concatenate([high, high, none, low], axis=0)).astype(BF16)
        high, low = split(0.5 * value)
        back[0:32, :] = high
        back[32:64, :] = low


def second_layer(flat, rows, eye, forward, back, back_q=None, head=None):
    value = 0.5 * natural(flat, rows[0], HID)
    high, low = split(value)
    forward[:, 0:HID] = nt(eye, high).astype(BF16)
    if back is not None:
        forward[:, HID : 2 * HID] = nt(eye, low).astype(BF16)
        back[:, 0:HID] = high
        back[:, HID : 2 * HID] = low
    if back_q is not None:
        high, low = split(value * head)
        back_q[:, 0:HID] = high
        back_q[:, HID : 2 * HID] = low


def second_biases(flats, eye, bias):
    rows = [
        jnp.broadcast_to(bias_row(flat, rows[3]) * ROOT_HALF, (LANES, HID)) for flat, rows in flats
    ]
    both = jnp.concatenate([two_pieces(row) for row in rows], axis=0)
    bias[...] = nt(jnp.concatenate([eye, eye], axis=1), both)


def selector(rows, chosen):
    return chosen(rows_of(rows), lanes_of(rows)).astype(F32)


def block_pair(value):
    none = jnp.zeros_like(value)
    return jnp.concatenate(
        [jnp.concatenate([value, none], axis=1), jnp.concatenate([none, value], axis=1)], axis=0
    ).astype(BF16)


def actor_place(row, lane):
    return ((row == lane) & (row < ACT)) | ((row - 24 == lane - ACT) & (row >= 24) & (row < 24 + ACT))


def actor_head(flat, rows, forward, bias, back):
    pieces = yield from unflatten(flat[rows[1] : rows[1] + 72, :] * ROOT_HALF, 2 * ACT)
    place = selector(48, actor_place)
    forward[...] = nt(block_pair(place), pieces).astype(BF16)
    if back is not None:
        none = jnp.zeros((48, LANES), F32)
        high = jnp.concatenate([place, none], axis=1)
        low = jnp.concatenate([none, place], axis=1)
        back[...] = nt(pieces, jnp.concatenate([high, high, low], axis=0).astype(BF16)).astype(BF16)
    heads = column(flat[rows[4] : rows[4] + 1, :])
    bias[0:24, :] = heads[0:24, :]
    bias[24:48, :] = heads[ACT : ACT + 24, :]


def critic_head(flat, rows, eye, forward, bias, back, use_mean_row=None):
    pieces = yield from unflatten(flat[rows[1] : rows[1] + 8, :] * ROOT_HALF, 2)
    place = selector(16, lambda row, lane: (row == lane) & (row < 2))
    both = nt(block_pair(place), pieces)
    forward[...] = both.astype(BF16)
    bias[...] = column(flat[rows[4] : rows[4] + 1, :])[0:8, :]
    if back is None:
        return
    yield
    spread = [
        jnp.concatenate(
            [jnp.broadcast_to(both[16 * part + k : 16 * part + k + 1, :], (LANES, HID)) for part in (0, 1)],
            axis=1,
        )
        for k in (0, 1)
    ]
    columns = nt(jnp.concatenate([eye, eye], axis=1), jnp.concatenate(spread, axis=0).astype(BF16))
    back[...] = ROOT_TWO * columns
    yield
    use_mean_row(ROOT_TWO * (both[0:1, :] + both[16:17, :]))


def spread_lanes(bias):
    return jnp.concatenate([bias] * (SUB // LANES), axis=1)


def fold(value):
    parts = [value[:, k : k + LANES] for k in range(0, value.shape[1], LANES)]
    total = parts[0]
    for part in parts[1:]:
        total = total + part
    return total


def policy_parts(out, shocks):
    centre = out[0:ACT, :]
    raw = out[24 : 24 + ACT, :]
    soft, slope = softplus_pair(raw)
    spread = soft + 0.05
    pre = centre + spread * shocks
    terms = (
        -0.5 * shocks * shocks
        - jnp.log(spread)
        - HALF_LOG_TWO_PI
        - 2.0 * (LOG_TWO - pre - softplus(-2.0 * pre))
    )
    return jnp.tanh(pre), jnp.sum(terms, axis=0, keepdims=True), spread, slope


def stacked_action(value, pad):
    tall = jnp.concatenate([value, pad], axis=0)
    high, low = split(tall)
    return jnp.concatenate([high, low, high, jnp.zeros_like(high)], axis=0)


def loss_kernel(
    builds, tiles, half, chunk, block,
    meta, log_alpha, obs, nxt, act, misc_wide, noise_own, misc_own,
    own_actor, other_actor, own_critic, other_critic,
    keep, send,
    flat_ta, flat_oa, flat_tc, flat_oc,
    w1_t, w1a, w1c, wa_t, wa_o, wa_back, w2_ta, w2_tc, w2a, w2c, w2a_back, w2c_back, w2q_back,
    bias2, w3_ta, w3_oa, w3_tc, w3_oc, w3a_back, w3c_back, bias3_ta, bias3_oa, bias3_tc, bias3_oc,
    square,
    g1a, g1c, g2a, g2c, g3a, g3c, gb2a, gb2c, gb3a, gb3c, sums, total,
    z1_t, z1_a, z1_c, h1c, h2c, dz1c, dz2c, doc, h1a, h2a, dz1a, dz2a, doa,
    table, got, wide, states_before, states, states_after, nexts_after, aux, aux_after,
    gathered, listed, chosen, count, peaks, done,
):
    grid_step = pl.program_id(0)
    step = grid_step - builds

    def first_products(rows, next_rows, which=(0, 1, 2)):
        x = rows[...]
        x3 = x[:, 0:384]
        if 0 in which:
            z1_c[...] = nt(w1c[...], jnp.concatenate([x3, x], axis=1))
        if 1 in which:
            z1_a[...] = nt(w1a[...], jnp.concatenate([x3, x3], axis=1))
        if 2 in which:
            z1_t[...] = nt(w1_t[...], next_rows[...])

    def gradients(rows, which=range(6)):
        x = rows[...]
        if 0 in which:
            g2c[...] += nt(h1c[...], dz2c[...])
        if 1 in which:
            g3c[...] += nt(doc[...], h2c[...])
        if 2 in which:
            g1c[...] += nn(dz1c[...], x)
        if 3 in which:
            g2a[...] += nt(h1a[...], dz2a[...])
        if 4 in which:
            g3a[...] += nt(doa[...], h2a[...])
        if 5 in which:
            g1a[...] += nn(dz1a[...], x[:, 0:384])

    @pl.when(grid_step == 0)
    def _():
        wide[...] = jnp.zeros_like(wide)
        gathered[...] = jnp.zeros_like(gathered)
        peaks[...] = jnp.zeros_like(peaks)
        listed[...] = jnp.zeros_like(listed)
        count[0] = 0

    @pl.when(grid_step < builds)
    def _():
        build_table(grid_step, block, obs, nxt, act, misc_wide, table, wide)
        choose(half // builds, noise_own, misc_own, listed, gathered, count)
        for k in range(0, half // builds, LANES):
            peaks[0:1, :] = jnp.maximum(peaks[0:1, :], misc_own[MISC_WEIGHT : MISC_WEIGHT + 1, k : k + LANES])

    @pl.when(grid_step == builds - 1)
    def _():
        @pl.when(meta[0] == 0)
        def _():
            copy_flat(flat_ta, own_actor)
            copy_flat(flat_oa, other_actor)
            copy_flat(flat_tc, own_critic)
            copy_flat(flat_oc, other_critic)

        @pl.when(meta[0] != 0)
        def _():
            copy_flat(flat_ta, other_actor)
            copy_flat(flat_oa, own_actor)
            copy_flat(flat_tc, other_critic)
            copy_flat(flat_oc, own_critic)

        copy = pltpu.make_async_copy(listed, chosen, done)
        copy.start()
        eye = square_eye()
        running = [
            actor_head(flat_ta, A_ROWS, w3_ta, bias3_ta, None),
            actor_head(flat_oa, A_ROWS, w3_oa, bias3_oa, w3a_back),
            critic_head(flat_tc, C_ROWS, eye, w3_tc, bias3_tc, None),
            critic_head(
                flat_oc, C_ROWS, eye, w3_oc, bias3_oc, w3c_back,
                lambda row: second_layer(flat_oc, C_ROWS, eye, w2c, w2c_back, w2q_back, row),
            ),
        ]
        flats = ((flat_ta, A_ROWS), (flat_tc, C_ROWS), (flat_oa, A_ROWS), (flat_oc, C_ROWS))
        beside = [
            lambda: first_layer(flat_oc, C_ROWS, eye, w1c, 2, 0),
            lambda: first_layer(flat_oa, A_ROWS, eye, w1a, 2, 0),
            copy.wait,
            lambda: first_layer(flat_ta, A_ROWS, eye, w1_t, 1, 0),
            lambda: first_layer(flat_tc, C_ROWS, eye, w1_t, 1, HID),
            lambda: action_layer(flat_oc, eye, square, wa_o, w1c, wa_back),
            lambda: action_layer(flat_tc, eye, square, wa_t, None, None),
            lambda: second_layer(flat_oa, A_ROWS, eye, w2a, w2a_back),
            lambda: second_layer(flat_ta, A_ROWS, eye, w2_ta, None),
            lambda: second_layer(flat_tc, C_ROWS, eye, w2_tc, None),
            lambda: second_biases(flats, eye, bias2),
        ]
        zeros = [g1a, g1c, g2a, g2c, g3a, g3c, gb2a, gb2c, gb3a, gb3c, sums]
        zeros += [h1c, h2c, dz1c, dz2c, doc, h1a, h2a, dz1a, dz2a, doa]
        fetched = 0
        while running or beside:
            running = [piece for piece in running if next(piece, True) is None]
            if beside:
                task = beside.pop(0)
                task()
                waited = task == copy.wait or fetched > 0
            for ref in zeros[:2]:
                ref[...] = jnp.zeros_like(ref)
            zeros = zeros[2:]
            if waited and fetched < TILE:
                fetch_rows(chosen, 0, table, got, fetched, fetched + 64)
                fetched += 64
        for ref in zeros:
            ref[...] = jnp.zeros_like(ref)
        fetch_rows(chosen, 0, table, got, fetched, TILE)
        turn_rows(got, states, nexts_after, aux)
        first_products(states, nexts_after)
        states_before[...] = states[...]

    @pl.when((grid_step >= builds) & (step * TILE < count[0]))
    def _():
        alpha = jnp.exp(jnp.full((1, SUB), log_alpha[0], F32))
        col0 = spread_lanes(w3c_back[:, 0:LANES])
        col1 = spread_lanes(w3c_back[:, LANES : 2 * LANES])
        pad = jnp.zeros((32 - ACT, SUB), F32)
        gap = jnp.zeros((24 - ACT, SUB), F32)
        row16 = lax.broadcasted_iota(jnp.int32, (16, SUB), 0)

        def head(weights, hidden, bias, size):
            tick()
            both = nn(weights[...], hidden)
            return both[0:size, :] + both[size : 2 * size, :] + spread_lanes(bias)

        def tick():
            task = beside.pop(0) if beside else None
            if task is not None:
                task()

        def gelu_t(t):
            tick()
            return gelu(t)

        def pair_t(t):
            tick()
            return gelu_pair(t)

        def nn_t(left, right):
            tick()
            return nn(left, right)

        def part(sub):
            lanes = slice(sub * SUB, (sub + 1) * SUB)
            per = SUB // LANES
            blocks = [gathered[step * (TILE // LANES) + sub * per + k] for k in range(per)]
            own = jnp.concatenate(blocks, axis=1)
            noise = own[0 : 2 * ACT + 1, :]
            place = step * TILE + sub * SUB + lax.broadcasted_iota(jnp.int32, (1, SUB), 1)
            counted = (place < count[0]).astype(F32)
            importance = own[OWN_WEIGHT + MISC_WEIGHT : OWN_WEIGHT + MISC_WEIGHT + 1, :]
            weight = counted * importance
            h1 = gelu_t(z1_t[0:HID, lanes])
            z2_t = nn_t(w2_ta[...], h1) + spread_lanes(bias2[:, 0 * LANES : 1 * LANES])
            hidden_a, s1a = pair_t(z1_a[:, lanes])
            z2_a = nn_t(w2a[...], twice(hidden_a)) + spread_lanes(bias2[:, 2 * LANES : 3 * LANES])
            hidden_c, s1c = pair_t(z1_c[:, lanes])
            z2_c = nn_t(w2c[...], twice(hidden_c)) + spread_lanes(bias2[:, 3 * LANES : 4 * LANES])
            yield
            h2 = gelu_t(z2_t)
            out = head(w3_ta, h2, bias3_ta[...], 48)
            last_a, s2a = pair_t(z2_a)
            out_a = head(w3_oa, last_a, bias3_oa[...], 48)
            last_c, s2c = pair_t(z2_c)
            both = nn_t(w3_oc[...], last_c)
            out_c = both[0:8, :] + both[16:24, :] + spread_lanes(bias3_oc[...])
            yield
            next_action, next_logp, _, _ = policy_parts(out, noise[0:ACT, :])
            z1_n = z1_t[HID:, lanes] + nn_t(wa_t[...], stacked_action(next_action, pad))
            shocks = noise[ACT : 2 * ACT, :]
            action, logp, spread_a, slope_a = policy_parts(out_a, shocks)
            old_action = aux[0:ACT, lanes] + aux[AUX_LOW : AUX_LOW + ACT, lanes]
            z1_q = z1_c[:, lanes] + nn_t(wa_o[...], stacked_action(action - old_action, pad))
            yield
            h1 = gelu_t(z1_n)
            z2_n = nn_t(w2_tc[...], h1) + spread_lanes(bias2[:, 1 * LANES : 2 * LANES])
            h1q, s1q = pair_t(z1_q)
            z2_q = nn_t(w2c[...], twice(h1q)) + spread_lanes(bias2[:, 3 * LANES : 4 * LANES])
            yield
            h2 = gelu_t(z2_n)
            both = nn_t(w3_tc[...], h2)
            out_t = both[0:8, :] + both[16:24, :] + spread_lanes(bias3_tc[...])
            h2q, s2q = pair_t(z2_q)
            both = nn_t(w3_oc[...], h2q)
            value_now = both[0:1, :] + both[16:17, :] + spread_lanes(bias3_oc[0:1, :])
            dz1q = nn_t(w2q_back[...], twice(s2q.astype(BF16))) * s1q
            yield
            both = nn_t(wa_back[...], dz1q.astype(BF16))
            value_back = both[0:ACT, :] + both[32 : 32 + ACT, :]
            next_spread = softplus(out_t[1:2, :]) + 0.1
            reward = aux[AUX_REWARD : AUX_REWARD + 1, lanes]
            goal = reward + DISCOUNT * (
                out_t[0:1, :] + next_spread * noise[2 * ACT : 2 * ACT + 1, :] - alpha * next_logp
            )
            q_value = out_c[0:1, :]
            soft, slope = softplus_pair(out_c[1:2, :])
            spread = soft + 0.1
            inverse = 1.0 / spread
            square_inverse = inverse * inverse
            miss = goal - q_value
            bound = jnp.minimum(jnp.maximum(miss, -3.0 * spread), 3.0 * spread)
            critic_loss = weight * (
                0.5 * miss * miss * square_inverse
                + 0.5 * bound * bound * square_inverse
                + jnp.log(spread)
            )
            mean_back = -weight * miss * square_inverse
            spread_back = weight * (1.0 - bound * bound * square_inverse) * inverse * slope
            dz2 = (col0 * mean_back + col1 * spread_back) * s2c
            back = dz2.astype(BF16)
            gb2c[...] += fold(dz2)
            dz1 = nn_t(w2c_back[...], twice(back)) * s1c
            do_c = jnp.where(
                row16 == 0,
                jnp.broadcast_to(mean_back, (16, SUB)),
                jnp.where(row16 == 1, jnp.broadcast_to(spread_back, (16, SUB)), 0.0),
            )
            gb3c[...] += fold(do_c)
            dz2c[:, lanes] = back
            dz1c[:, lanes] = dz1.astype(BF16)
            doc[:, lanes] = do_c.astype(BF16)
            h1c[:, lanes] = hidden_c
            h2c[:, lanes] = last_c
            yield
            counted_alpha = counted * alpha
            d_pre = counted_alpha * 2.0 * action - counted * value_back * (1.0 - action * action)
            d_raw = (d_pre * shocks - counted_alpha / spread_a) * slope_a
            do_a = jnp.concatenate([d_pre, gap, d_raw, gap], axis=0)
            high, low = split(ROOT_TWO * do_a)
            dz2 = nn_t(w3a_back[...], jnp.concatenate([high, low, high], axis=0)) * s2a
            back = dz2.astype(BF16)
            gb2a[...] += fold(dz2)
            gb3a[...] += fold(do_a)
            sums[0:1, :] += fold(counted)
            sums[1:2, :] += fold(counted * logp)
            sums[2:3, :] += fold(critic_loss)
            sums[3:4, :] += fold(counted * (alpha * logp - value_now))
            yield
            dz1 = nn_t(w2a_back[...], twice(back)) * s1a
            dz2a[:, lanes] = back
            dz1a[:, lanes] = dz1.astype(BF16)
            doa[:, lanes] = high
            h1a[:, lanes] = hidden_a
            h2a[:, lanes] = last_a

        first_pick = jnp.minimum(step + 1, tiles - 1) * (TILE // LANES)

        fetches = [
            lambda k=k: fetch_rows(chosen, first_pick, table, got, k, k + 16)
            for k in range(0, TILE, 16)
        ]
        sums_before = [
            lambda which=which: gradients(states_before, (which,)) for which in range(6)
        ]
        products_after = [
            lambda: turn_rows(got, states_after, nexts_after, aux_after),
            lambda: first_products(states_after, nexts_after, (0,)),
            lambda: first_products(states_after, nexts_after, (1,)),
            lambda: first_products(states_after, nexts_after, (2,)),
        ]
        beside = []
        for k, fetch in enumerate(fetches):
            beside.append(fetch)
            if k % 5 == 2 and sums_before:
                beside.append(sums_before.pop(0))
        for product in products_after:
            beside += [product, None, None, None, None]

        running = [part(sub) for sub in range(TILE // SUB)]
        while running:
            running = [piece for piece in running if next(piece, True) is None]
        while beside:
            tick()
        states_before[...] = states[...]
        states[...] = states_after[...]
        aux[...] = aux_after[...]

    @pl.when(step == tiles - 1)
    def _():
        gradients(states_before)
        total[...] = jnp.zeros_like(total)

        def sum_row(block):
            return jnp.sum(block.T, axis=0, keepdims=True)

        for side in (0, 1):
            at = side * LANES
            turned = 0.5 * g1a[at : at + LANES, :].T
            total[A_W1[side] : A_W1[side] + OBS, :] = turned[0:OBS, :]
            total[A_B + side : A_B + side + 1, :] = turned[ONE_LANE : ONE_LANE + 1, :]
            total[A_W2[side] : A_W2[side] + HID, :] = (0.5 * ROOT_HALF) * g2a[:, at : at + LANES]
            total[A_W3[side] : A_W3[side] + ACT, :] = 0.5 * g3a[0:ACT, at : at + LANES]
            total[A_W3[side] + ACT : A_W3[side] + 2 * ACT, :] = (
                0.5 * g3a[24 : 24 + ACT, at : at + LANES]
            )
            total[A_B + 2 + side : A_B + 3 + side, :] = 0.5 * sum_row(gb2a[at : at + LANES, :])
            turned = 0.5 * g1c[at : at + LANES, :].T
            total[C_W1[side] : C_W1[side] + OBS, :] = turned[0:OBS, :]
            total[C_W1[side] + OBS : C_W1[side] + OBS + ACT, :] = (
                turned[384 : 384 + ACT, :] + turned[384 + AUX_LOW : 384 + AUX_LOW + ACT, :]
            )
            total[C_B + side : C_B + side + 1, :] = turned[ONE_LANE : ONE_LANE + 1, :]
            total[C_W2[side] : C_W2[side] + HID, :] = (0.5 * ROOT_HALF) * g2c[:, at : at + LANES]
            total[C_W3[side] : C_W3[side] + 2, :] = ROOT_HALF * g3c[0:2, at : at + LANES]
            total[C_B + 2 + side : C_B + 3 + side, :] = 0.5 * sum_row(gb2c[at : at + LANES, :])
        none = jnp.zeros((LANES - 2 * ACT, LANES), F32)
        total[A_B + 4 : A_B + 5, :] = sum_row(
            jnp.concatenate([gb3a[0:ACT, :], gb3a[24 : 24 + ACT, :], none], axis=0)
        )
        none = jnp.zeros((LANES - 16, LANES), F32)
        total[C_B + 4 : C_B + 5, :] = sum_row(jnp.concatenate([gb3c[...], none], axis=0))
        total[EXTRA : EXTRA + 4, :] = sums[0:4, :]
        peak = jnp.max(peaks[0:1, :], axis=1, keepdims=True)
        for k in range(EXTRA + 8 - EXTRA_SLOTS):
            total[EXTRA_SLOTS + k : EXTRA_SLOTS + k + 1, :] = jnp.where(
                lanes_of(1) + k * LANES == meta[1], jnp.broadcast_to(peak, (1, LANES)), 0.0
            )
        count = keep.shape[0] // chunk
        for p in range(count):
            at = pl.multiple_of((meta[1] ^ p) * chunk, 8)
            keep[p * chunk : (p + 1) * chunk, :] = total[pl.ds(at, chunk), :]
            at = pl.multiple_of((meta[1] ^ (p + count)) * chunk, 8)
            send[p * chunk : (p + 1) * chunk, :] = total[pl.ds(at, chunk), :]


def losses(
    meta, log_alpha, obs, nxt, act, noise, misc, own_a, other_a, own_c, other_c, devices
):
    rows = obs.shape[1]
    half = noise.shape[1] // 2
    tiles = -(-half // TILE)
    block = next(size for size in (1280, 640, 512, 256, 128) if rows % size == 0)
    builds = rows // block
    own = half // builds
    list_rows = -(-(tiles * (TILE // LANES) + 1) // 8) * 8
    chunk = chunk_rows(devices)
    buffer_rows = chunk * devices

    def fixed(i, meta):
        return (0, 0)

    def source(i, meta):
        return (0, jnp.minimum(i, builds - 1))

    def own_source(i, meta):
        return (0, meta[0] * builds + jnp.minimum(i, builds - 1))

    def body(*refs):
        loss_kernel(builds, tiles, half, chunk, block, *refs)

    def bf(*shape):
        return pltpu.VMEM(shape, BF16)

    def f32(*shape):
        return pltpu.VMEM(shape, F32)

    features = noise.shape[0]
    once = pl.Buffered(1)
    return pl.pallas_call(
        body,
        out_shape=(
            jax.ShapeDtypeStruct((buffer_rows // 2, LANES), F32),
            jax.ShapeDtypeStruct((buffer_rows // 2, LANES), F32),
        ),
        grid_spec=pltpu.PrefetchScalarGridSpec(
            num_scalar_prefetch=1,
            grid=(builds + tiles,),
            in_specs=[
                pl.BlockSpec(memory_space=pltpu.SMEM),
                pl.BlockSpec((OBS, block), source),
                pl.BlockSpec((OBS, block), source),
                pl.BlockSpec((ACT, block), source),
                pl.BlockSpec((8, block), source),
                pl.BlockSpec((features, own), own_source),
                pl.BlockSpec((8, own), own_source),
                pl.BlockSpec((1, A_SIZE), fixed, pipeline_mode=once),
                pl.BlockSpec((1, A_SIZE), fixed, pipeline_mode=once),
                pl.BlockSpec((1, C_SIZE), fixed, pipeline_mode=once),
                pl.BlockSpec((1, C_SIZE), fixed, pipeline_mode=once),
            ],
            out_specs=(
                pl.BlockSpec((buffer_rows // 2, LANES), fixed),
                pl.BlockSpec((buffer_rows // 2, LANES), fixed),
            ),
            scratch_shapes=[
                f32(A_FLAT, LANES), f32(A_FLAT, LANES), f32(C_FLAT, LANES), f32(C_FLAT, LANES),
                bf(512, 384), bf(HID, 768), bf(HID, 896),
                bf(HID, LANES), bf(HID, LANES), bf(64, HID),
                bf(HID, HID), bf(HID, HID),
                bf(HID, 512), bf(HID, 512), bf(HID, 512), bf(HID, 512), bf(HID, 512),
                f32(HID, 4 * LANES), bf(96, HID), bf(96, HID), bf(32, HID), bf(32, HID),
                bf(HID, 144), f32(HID, 2 * LANES),
                f32(48, LANES), f32(48, LANES), f32(8, LANES), f32(8, LANES),
                f32(32, HID),
                f32(HID, 384), f32(HID, 512), f32(HID, HID), f32(HID, HID),
                f32(48, HID), f32(16, HID), f32(HID, LANES), f32(HID, LANES),
                f32(48, LANES), f32(16, LANES), f32(8, LANES), f32(buffer_rows, LANES),
                f32(2 * HID, TILE), f32(HID, TILE), f32(HID, TILE),
                bf(HID, TILE), bf(HID, TILE), bf(HID, TILE), bf(HID, TILE), bf(16, TILE),
                bf(HID, TILE), bf(HID, TILE), bf(HID, TILE), bf(HID, TILE), bf(48, TILE),
                f32(rows * 8, LANES), f32(TILE * 8, LANES), f32(LANES, block),
                bf(TILE, 512), bf(TILE, 512), bf(TILE, 512), bf(TILE, 384),
                f32(AUX_ROWS, TILE), f32(AUX_ROWS, TILE),
                f32(list_rows, OWN_ROWS, LANES),
                pltpu.VMEM((list_rows, LANES), jnp.int32),
                pltpu.SMEM((list_rows, LANES), jnp.int32),
                pltpu.SMEM((1,), jnp.int32), f32(8, LANES), pltpu.SemaphoreType.DMA,
            ],
        ),
        compiler_params=pltpu.CompilerParams(
            dimension_semantics=("arbitrary",), vmem_limit_bytes=VMEM_BYTES
        ),
        name="losses",
    )(meta, log_alpha, obs, nxt, act, misc, noise, misc, own_a, other_a, own_c, other_c)


def stat_pieces(width_in, width_out):
    sizes = [width_in, HID, HID, HID, HID, width_out, HID, HID, width_out]
    starts = [sum(sizes[:k]) for k in range(len(sizes))]
    rows = [-(-size // LANES) for size in sizes]
    return sizes, starts, [sum(rows[:k]) for k in range(len(rows))], sum(rows)


def aligned_stats(statistics, width_in, width_out):
    sizes, starts, _, rows = stat_pieces(width_in, width_out)
    pieces = [
        jnp.pad(statistics[start : start + size], (0, -size % LANES))
        for size, start in zip(sizes, starts)
    ]
    pieces.append(jnp.zeros((-rows % 8 * LANES,), F32))
    return jnp.concatenate(pieces).reshape(-1, LANES)


def store_line(out, lead, value):
    size = out.shape[-1]
    count = value.shape[0]
    whole = size // 1024
    for k in range(whole):
        part = value[8 * k : 8 * k + 8, :]
        out[pl.ds(1024 * k, 1024)] = part.reshape(1024)
    for k in range(8 * whole, count):
        width = min(LANES, size - k * LANES)
        if width > 0:
            out[pl.ds(k * LANES, width)] = value[k : k + 1, 0:width].reshape(width)


def net_update(
    total, scale, old_stats, width_in, width_out, w1, w2, w3, bias_at, rows, fg, fu, stats_out
):
    sizes, starts, first, _ = stat_pieces(width_in, width_out)
    lines = [[] for _ in sizes]

    def old_row(piece, k):
        return old_stats[first[piece] + k : first[piece] + k + 1, :]

    def blend(old, new):
        return DECAY_RATE * old + (1.0 - DECAY_RATE) * new

    def clip_scale(square_sum, number):
        root = jnp.sqrt(square_sum / number)
        return 1.0 / jnp.maximum(1.0, root / CLIP_LEVEL)

    def whole_sum(value):
        return jnp.sum(jnp.sum(value, axis=0, keepdims=True), axis=1, keepdims=True)

    for layer, (places, height, flat_at) in enumerate(
        ((w1, width_in, 0), (w2, HID, rows[0]))
    ):
        parts = [total[at : at + height, :] * scale for at in places]
        squares = [g * g + TINY_TERM for g in parts]
        blocks = -(-height // LANES)
        old = jnp.concatenate([column(old_row(layer, k)) for k in range(blocks)], axis=0)
        old = old[0:height, :]
        mean = jnp.sum(squares[0] + squares[1], axis=1, keepdims=True) * (1.0 / HID)
        row_stat = blend(old, jnp.broadcast_to(mean, (height, LANES)))
        for k in range(blocks):
            block = row_stat[k * LANES : min(height, (k + 1) * LANES), :]
            if block.shape[0] < LANES:
                block = jnp.concatenate(
                    [block, jnp.zeros((LANES - block.shape[0], LANES), F32)], axis=0
                )
            lines[layer].append(block.T[0:1, :])
        mean_row = jnp.sum(row_stat, axis=0, keepdims=True) * (1.0 / height)
        row_root = lax.rsqrt(row_stat)
        steps = []
        for side in (0, 1):
            col_stat = blend(
                old_row(3 + layer, side),
                jnp.sum(squares[side], axis=0, keepdims=True) * (1.0 / height),
            )
            lines[3 + layer].append(col_stat)
            steps.append((parts[side] * row_root) * (lax.rsqrt(col_stat) * jnp.sqrt(mean_row)))
        factor = clip_scale(
            whole_sum(steps[0] * steps[0] + steps[1] * steps[1]), float(height * HID)
        )
        for side in (0, 1):
            fg[pl.ds(flat_at + side, height, stride=2), :] = parts[side]
            fu[pl.ds(flat_at + side, height, stride=2), :] = steps[side] * factor

    tall = -(-width_out // 8) * 8
    parts = [total[at : at + tall, :] * scale for at in w3]
    real = rows_of(tall) < width_out
    squares = [jnp.where(real, g * g + TINY_TERM, 0.0) for g in parts]
    old = column(old_row(5, 0))[0:tall, :]
    mean = jnp.sum(squares[0] + squares[1], axis=1, keepdims=True) * (1.0 / HID)
    col_stat = blend(old, jnp.broadcast_to(mean, (tall, LANES)))
    lines[5].append(
        jnp.concatenate([col_stat, jnp.zeros((LANES - tall, LANES), F32)], axis=0).T[0:1, :]
    )
    row_stats = []
    for side in (0, 1):
        row_stats.append(
            blend(
                old_row(2, side),
                jnp.sum(squares[side], axis=0, keepdims=True) * (1.0 / width_out),
            )
        )
        lines[2].append(row_stats[side])
    mean_row = jnp.sum(row_stats[0] + row_stats[1], axis=1, keepdims=True) * (1.0 / HID)
    col_root = jnp.where(real, lax.rsqrt(col_stat), 0.0)
    steps = [
        (parts[side] * lax.rsqrt(row_stats[side])) * (col_root * jnp.sqrt(mean_row))
        for side in (0, 1)
    ]
    factor = clip_scale(
        whole_sum(steps[0] * steps[0] + steps[1] * steps[1]), float(HID * width_out)
    )
    pad = jnp.zeros((LANES - tall, LANES), F32)
    size = rows[2] - rows[1]
    padded = -(-size // 8) * 8
    turned = [
        jnp.concatenate(
            [jnp.concatenate([jnp.where(real, part, 0.0), pad], axis=0).T for part in pair], axis=0
        )
        for pair in (parts, [u * factor for u in steps])
    ]
    flat_parts = flatten(turned, width_out, padded)
    for flat, part in zip((fg, fu), flat_parts):
        flat[rows[1] : rows[1] + size, :] = part[0:size, :]

    grad = total[bias_at : bias_at + 8, :] * scale
    line = rows_of(8)
    lane = lanes_of(8)
    real = (line < 4) | ((line == 4) & (lane < width_out))
    grad = jnp.where(real, grad, 0.0)
    stat = blend(old_stats[first[6] : first[6] + 5, :], grad[0:5, :] * grad[0:5, :] + TINY_TERM)
    step = jnp.where(real[0:5, :], grad[0:5, :] * lax.rsqrt(stat), 0.0)
    factor = clip_scale(whole_sum(step * step), float(2 * HID + width_out))
    fg[rows[2] : rows[2] + 5, :] = grad[0:5, :]
    fu[rows[2] : rows[2] + 5, :] = step * factor
    for k in range(5):
        lines[6 + k // 2].append(stat[k : k + 1, :])

    size = stats_out.shape[0]
    count = -(-size // LANES)
    made = [jnp.zeros((1, LANES), F32) for _ in range(count + 1)]
    lane = lanes_of(1)
    for piece, pieces in enumerate(lines):
        for k, value in enumerate(pieces):
            start = starts[piece] + k * LANES
            width = min(LANES, sizes[piece] - k * LANES)
            value = jnp.where(lane < width, value, 0.0)
            shift = start % LANES
            at = start // LANES
            if shift:
                value = pltpu.roll(value, shift, 1)
            made[at] = made[at] + jnp.where(lane >= shift, value, 0.0)
            if shift:
                made[at + 1] = made[at + 1] + jnp.where(lane < shift, value, 0.0)
    for k in range(count):
        width = min(LANES, size - k * LANES)
        stats_out[pl.ds(k * LANES, width)] = made[k][:, 0:width].reshape(width)


def write_net(side, own, other, fg, fu, slot, copy, grad):
    size = own.shape[1]
    whole = size // 1024

    def piece(at, row, width, count):
        mine = own[0:1, pl.ds(at, width)].reshape(count, width // count)
        theirs = other[0:1, pl.ds(at, width)].reshape(count, width // count)
        wide = width // count
        step = fu[pl.ds(row, count), 0:wide]
        online = jnp.where(side == 0, theirs, mine)
        new = online - LEARN_RATE * step
        held = jnp.where(side == 0, POLYAK_RATE * new + (1.0 - POLYAK_RATE) * mine, new)
        slot[0:1, pl.ds(at, width)] = held.reshape(1, width)
        copy[0:1, pl.ds(at, width)] = held.reshape(1, width).astype(BF16)
        grad[pl.ds(at, width)] = fg[pl.ds(row, count), 0:wide].reshape(width)

    for k in range(whole):
        piece(k * 1024, k * 8, 1024, 8)
    full = size // LANES
    for row in range(whole * 8, full):
        piece(row * LANES, row, LANES, 1)
    piece(full * LANES, full, size - full * LANES, 1)


def update_kernel(
    chunk, devices,
    meta, log_alpha, mine, theirs, own_a, other_a, own_c, other_c, stats_a, stats_c,
    slot_a, slot_c, copy_a, copy_c, grad_a, grad_c, new_a, new_c, summary, alpha_out,
    total, fg_a, fu_a, fg_c, fu_c,
):
    count = devices // 2
    for p in range(count):
        at = pl.multiple_of((meta[1] ^ p) * chunk, 8)
        total[pl.ds(at, chunk), :] = mine[p * chunk : (p + 1) * chunk, :]
        at = pl.multiple_of((meta[1] ^ (p + count)) * chunk, 8)
        total[pl.ds(at, chunk), :] = theirs[p * chunk : (p + 1) * chunk, :]

    sums = jnp.sum(total[EXTRA : EXTRA + 8, :], axis=1, keepdims=True)
    peak = jnp.max(total[EXTRA_SLOTS : EXTRA + 8, :], axis=1, keepdims=True)
    peak = jnp.max(peak, axis=0, keepdims=True)
    counted = sums[0:1, :]
    scale_a = 1.0 / counted
    scale_c = scale_a / peak
    lane = lanes_of(1)
    line = jnp.where(
        lane == 0,
        jnp.broadcast_to(sums[2:3, :] / peak, (1, LANES)),
        jnp.where(
            lane == 1,
            jnp.broadcast_to(sums[3:4, :], (1, LANES)),
            jnp.broadcast_to(counted, (1, LANES)),
        ),
    )
    summary[...] = line[:, 0:3].reshape(3)
    new_alpha = log_alpha[0] + ALPHA_STEP * (
        jnp.broadcast_to(sums[1:2, :] / counted, (1, LANES)) - ACT
    )
    alpha_out[...] = new_alpha[:, 0:1].reshape(1)
    net_update(
        total, scale_a, stats_a, OBS, 2 * ACT, A_W1, A_W2, A_W3, A_B, A_ROWS, fg_a, fu_a, new_a
    )
    net_update(
        total, scale_c, stats_c, OBS + ACT, 2, C_W1, C_W2, C_W3, C_B, C_ROWS, fg_c, fu_c, new_c
    )
    write_net(meta[0], own_a, other_a, fg_a, fu_a, slot_a, copy_a, grad_a)
    write_net(meta[0], own_c, other_c, fg_c, fu_c, slot_c, copy_c, grad_c)


def update(meta, log_alpha, mine, theirs, own_a, other_a, own_c, other_c, stats_a, stats_c, sizes, devices):
    chunk = chunk_rows(devices)

    def body(*refs):
        update_kernel(chunk, devices, *refs)

    def f32(*shape):
        return jax.ShapeDtypeStruct(shape, F32)

    smem = pl.BlockSpec(memory_space=pltpu.SMEM)
    vmem = pl.BlockSpec(memory_space=pltpu.VMEM)
    return pl.pallas_call(
        body,
        out_shape=(
            f32(1, A_SIZE), f32(1, C_SIZE),
            jax.ShapeDtypeStruct((1, A_SIZE), BF16), jax.ShapeDtypeStruct((1, C_SIZE), BF16),
            f32(A_SIZE), f32(C_SIZE), f32(sizes[0]), f32(sizes[1]), f32(3), f32(1),
        ),
        in_specs=[smem, smem] + [vmem] * 8,
        out_specs=tuple([vmem] * 10),
        scratch_shapes=[
            pltpu.VMEM((chunk * devices, LANES), F32),
            pltpu.VMEM((A_FLAT, LANES), F32), pltpu.VMEM((A_FLAT, LANES), F32),
            pltpu.VMEM((C_FLAT, LANES), F32), pltpu.VMEM((C_FLAT, LANES), F32),
        ],
        compiler_params=pltpu.CompilerParams(vmem_limit_bytes=UPDATE_VMEM_BYTES),
        name="optimizer",
    )(meta, log_alpha, mine, theirs, own_a, other_a, own_c, other_c, stats_a, stats_c)


def chunk_rows(devices):
    return -(-DATA_ROWS // (8 * devices)) * 8


def radices(count):
    found = []
    while count > 1:
        found.append(4 if count % 4 == 0 else 2)
        count //= found[-1]
    return found


def swap_groups(value):
    return lax.ppermute(value, "grp", [(0, 1), (1, 0)])


def exchange(value, mask):
    count = lax.axis_size("dp")
    return lax.ppermute(value, "dp", [(i, i ^ mask) for i in range(count)])


def buffer_place(group_side, count):
    rest = lax.axis_index("dp")
    place = group_side
    for radix in radices(count):
        place = place * radix + rest % radix
        rest = rest // radix
    return place


def all_sum(keep, send):
    stages = radices(lax.axis_size("dp"))
    value = keep + swap_groups(send)
    stride = 1
    for radix in stages:
        rows = value.shape[0] // radix
        parts = [value[k * rows : (k + 1) * rows] for k in range(radix)]
        came = [exchange(parts[k], k * stride) for k in range(1, radix)]
        value = parts[0]
        for part in came:
            value = value + part
        stride *= radix
    for radix in reversed(stages):
        stride //= radix
        value = jnp.concatenate(
            [value] + [exchange(value, k * stride) for k in range(1, radix)], axis=0
        )
    return value, swap_groups(value)


def shards(
    obs_rows,
    next_rows,
    action_rows,
    reward_rows,
    batch_index,
    valid_mask,
    noise,
    importance,
    actor_params,
    critic_params,
    actor_stats,
    critic_stats,
    log_alpha,
):
    devices = lax.axis_size("dp") * lax.axis_size("grp")
    group_side = lax.axis_index("grp")
    other_a = swap_groups(actor_params)
    other_c = swap_groups(critic_params)
    place = buffer_place(group_side, lax.axis_size("dp"))
    meta = jnp.where(jnp.arange(2) == 0, group_side, place).astype(jnp.int32)
    row = lax.broadcasted_iota(jnp.int32, (8, batch_index.shape[0]), 0)
    misc = jnp.where(row == MISC_VALID, valid_mask[None], batch_index[None]).astype(F32)
    misc = jnp.where(row == MISC_WEIGHT, importance[None], misc)
    misc = jnp.where(row == 0, reward_rows[None], misc)
    keep, send = losses(
        meta, log_alpha, obs_rows.T, next_rows.T, action_rows.T, noise.T, misc,
        actor_params, other_a, critic_params, other_c, devices,
    )
    keep, send, actor_stats, critic_stats = lax.optimization_barrier(
        (keep, send, actor_stats, critic_stats)
    )
    mine, theirs = all_sum(keep, send)
    (
        slot_a, slot_c, copy_a, copy_c, grad_a, grad_c, new_a, new_c, summary, alpha
    ) = update(
        meta, log_alpha, mine, theirs, actor_params, other_a, critic_params, other_c,
        aligned_stats(actor_stats, OBS, 2 * ACT), aligned_stats(critic_stats, OBS + ACT, 2),
        (actor_stats.shape[0], critic_stats.shape[0]), devices,
    )
    return (
        slot_a, slot_c, copy_a, copy_c, grad_a, grad_c, new_a, new_c,
        summary, alpha,
    )


def solution(mesh):
    return jax.shard_map(
        shards,
        mesh=mesh,
        in_specs=(
            P("dp", None),
            P("dp", None),
            P("dp", None),
            P("dp"),
            P("dp"),
            P("dp"),
            P("dp", None),
            P("dp"),
            P("grp", None),
            P("grp", None),
            P(),
            P(),
            P(),
        ),
        out_specs=(
            P("grp", None),
            P("grp", None),
            P("grp", None),
            P("grp", None),
            P(),
            P(),
            P(),
            P(),
            P(),
            P(),
        ),
        check_vma=False,
    )
```

```python
import jax
import jax.numpy as jnp
from jax import lax
from jax.experimental import pallas as pl
from jax.experimental.pallas import tpu as pltpu
from jax.sharding import PartitionSpec as P

OBS = 376
ACT = 17
HID = 256
LANES = 128
TILE = 512
SUB = 256

DISCOUNT = 0.99
POLYAK_RATE = 0.1
DECAY_RATE = 0.5
LEARN_RATE = 0.1
CLIP_LEVEL = 0.1
ALPHA_STEP = 0.01
TINY_TERM = 1e-30
HALF_LOG_TWO_PI = 0.9189385332046727
LOG_TWO = 0.6931471805599453
ROOT_HALF = 0.7071067811865476
ROOT_TWO = 1.4142135623730951
LOG2_E = 1.4426950408889634
LOG2_TWO_OVER_ROOT_PI = 0.17425193548825

F32 = jnp.float32
BF16 = jnp.bfloat16
VMEM_BYTES = 57 * 2**20
UPDATE_VMEM_BYTES = 24 * 2**20

ONE_LANE = OBS
AUX_LOW = 32
AUX_REWARD = 64
AUX_AGAIN = 96
AUX_ROWS = 72
CHUNKS = 7
OWN_WEIGHT = 40
OWN_ROWS = 48
MISC_WEIGHT = 1
MISC_VALID = 2
MISC_INDEX = 3


def flat_rows(width_in, width_out):
    w2 = width_in * HID // LANES
    w3 = w2 + HID * HID // LANES
    b1 = w3 + HID * width_out // LANES
    return w2, w3, b1, b1 + 2, b1 + 4


A_ROWS = flat_rows(OBS, 2 * ACT)
C_ROWS = flat_rows(OBS + ACT, 2)
A_SIZE = A_ROWS[4] * LANES + 2 * ACT
C_SIZE = C_ROWS[4] * LANES + 2
A_FLAT = -(-A_SIZE // 1024) * 8
C_FLAT = -(-C_SIZE // 1024) * 8

A_W1 = (0, OBS)
A_W2 = (2 * OBS, 2 * OBS + HID)
A_W3 = (2 * OBS + 2 * HID, 2 * OBS + 2 * HID + 40)
A_B = A_W3[1] + 40
C_W1 = (A_B + 8, A_B + 8 + 400)
C_W2 = (C_W1[1] + 400, C_W1[1] + 400 + HID)
C_W3 = (C_W2[1] + HID, C_W2[1] + HID + 8)
C_B = C_W3[1] + 8
EXTRA = C_B + 8
EXTRA_SLOTS = EXTRA + 4
DATA_ROWS = EXTRA + 8


def nn(left, right):
    return lax.dot_general(
        left, right, (((1,), (0,)), ((), ())), preferred_element_type=F32
    )


def nt(left, right):
    return lax.dot_general(
        left, right, (((1,), (1,)), ((), ())), preferred_element_type=F32
    )


def split(value):
    high = value.astype(BF16)
    return high, (value - high.astype(F32)).astype(BF16)


def twice(value):
    return jnp.concatenate([value, value], axis=0)


def gelu(t):
    return (t * (1.0 + lax.erf(t))).astype(BF16)


def gelu_pair(t):
    double_cdf = 1.0 + lax.erf(t)
    bell = jnp.exp2(LOG2_TWO_OVER_ROOT_PI - LOG2_E * (t * t))
    return (t * double_cdf).astype(BF16), double_cdf + t * bell


def softplus(x):
    return jnp.maximum(x, 0.0) + jnp.log(1.0 + jnp.exp(-jnp.abs(x)))


def softplus_pair(x):
    decay = jnp.exp(-jnp.abs(x))
    inverse = 1.0 / (1.0 + decay)
    return jnp.maximum(x, 0.0) + jnp.log(1.0 + decay), jnp.where(x >= 0.0, inverse, decay * inverse)


def column(row):
    return jnp.broadcast_to(row, (LANES, LANES)).T


def rows_of(count):
    return lax.broadcasted_iota(jnp.int32, (count, LANES), 0)


def lanes_of(count):
    return lax.broadcasted_iota(jnp.int32, (count, LANES), 1)


def square_eye(reverse=False):
    row = lax.broadcasted_iota(jnp.int32, (HID, HID), 0)
    lane = lax.broadcasted_iota(jnp.int32, (HID, HID), 1)
    return (row == (HID - 1 - lane if reverse else lane)).astype(F32).astype(BF16)


def two_pieces(value):
    return jnp.concatenate(split(value), axis=1)


def turns(value, shift, stride):
    turn = (rows_of(HID) * stride + shift) % LANES
    for step in (2, 4, 8, 16, 32, 64):
        value = jnp.where((turn & step) != 0, pltpu.roll(value, step, 1), value)
        yield value


def unflatten(flat, width):
    rows = flat.shape[0]
    first = (HID - 1 - rows_of(HID)) * width
    lane = lanes_of(HID)
    owner = first // LANES
    picks = jnp.concatenate([(owner == lane), (owner + 1 == lane)], axis=0).astype(F32).astype(BF16)
    found = nn(picks[:, 0:rows], two_pieces(flat))
    yield
    found = found[:, 0:LANES] + found[:, LANES:]
    mixed = jnp.where(lane >= first % LANES, found[0:HID, :], found[HID:, :])
    for turned in turns(mixed, -(HID - 1) * width % LANES, width):
        yield
    pieces = nn(square_eye(True), two_pieces(turned)).astype(BF16)
    yield
    return pieces


def flatten(values, width, rows):
    first = rows_of(HID) * width % LANES
    lane = lanes_of(HID)
    for turned in turns(values[0] + pltpu.roll(values[1], 64, 1), 0, width):
        yield
    swapped = pltpu.roll(turned, 64, 1)
    begun = (lane >= first) & (lane < first + width)
    wrapped = lane < first + width - LANES
    parts = []
    for value in (turned, swapped):
        parts.append(
            jnp.concatenate([jnp.where(begun, value, 0.0), jnp.where(wrapped, value, 0.0)], axis=0)
        )
    both = jnp.concatenate(parts, axis=1)
    high, low = split(both)
    least = (both - high.astype(F32) - low.astype(F32)).astype(BF16)
    owner = lax.broadcasted_iota(jnp.int32, (rows, HID), 1) * width // LANES
    row = lax.broadcasted_iota(jnp.int32, (rows, HID), 0)
    places = jnp.concatenate([owner == row, owner + 1 == row], axis=1).astype(F32).astype(BF16)
    yield
    found = nn(places, jnp.concatenate([high, low, least], axis=1))
    yield
    found = found[:, 0:HID] + found[:, HID : 2 * HID] + found[:, 2 * HID :]
    return found[:, 0:LANES], found[:, LANES:]


def build_table(step, block, obs, nxt, act, misc, table, wide):
    groups = block // 8
    table3 = table.reshape(table.shape[0] // (8 * CHUNKS), 8 * CHUNKS, LANES)
    at = pl.multiple_of(step * groups, groups)

    def put(value, first):
        for c in range(value.shape[1] // LANES):
            table3[pl.ds(at, groups), 8 * (first + c) : 8 * (first + c) + 8, :] = value[
                :, LANES * c : LANES * (c + 1)
            ].reshape(groups, 8, LANES)

    ones = (lax.broadcasted_iota(jnp.int32, (8, block), 0) == 0).astype(F32)
    whole = OBS // 16 * 16

    def padded(source):
        value = source[...]
        rest = jnp.concatenate([value[whole:, :].astype(F32), ones], axis=0).astype(BF16)
        return jnp.concatenate([value[0:whole, :], rest], axis=0)

    value = padded(obs)
    eye = square_eye()
    turned = [nt(eye, value[:, k : k + HID]) for k in range(0, block, HID)]
    put(jnp.concatenate(turned, axis=0), 0)
    put(padded(nxt).T.astype(F32), 3)
    action = act[...]
    high = action.astype(BF16).astype(F32)
    wide[0:ACT, :] = high
    wide[AUX_LOW : AUX_LOW + ACT, :] = action - high
    wide[AUX_AGAIN : AUX_AGAIN + ACT, :] = high
    wide[AUX_REWARD : AUX_REWARD + 8, :] = misc[...]
    put(wide[...].T, 6)


def choose(size, noise, misc, listed, gathered, count):
    lane = lanes_of(1)
    wide_lane = lanes_of(OWN_ROWS)
    parts = size // LANES
    counted = misc[MISC_VALID : MISC_VALID + 1, :]
    flags = [counted[:, LANES * k : LANES * (k + 1)] for k in range(parts)]
    stacked = jnp.concatenate(flags + [jnp.zeros((-parts % 16, LANES), F32)], axis=0).astype(BF16)
    before = nn(stacked, (rows_of(LANES) < lanes_of(LANES)).astype(F32).astype(BF16))
    before = before.astype(jnp.int32)
    index = misc[MISC_INDEX : MISC_INDEX + 1, :].astype(jnp.int32)
    spot = (index >> 3) * (8 * CHUNKS) + (index & 7)
    digits = jnp.concatenate([spot >> 8, spot & 255] + [jnp.zeros_like(spot)] * 14, axis=0)
    gap = jnp.zeros((OWN_WEIGHT - 2 * ACT - 1, size), F32)
    high, low = split(jnp.concatenate([noise[...], gap, misc[...]], axis=0))
    value = jnp.concatenate([digits.astype(F32).astype(BF16), high, low], axis=0)
    place = count[0]
    for k in range(parts):
        where = (before[k : k + 1, :] + place) & (LANES - 1)
        where = jnp.where(flags[k] > 0.0, where, -1)
        hit = (jnp.broadcast_to(where, (LANES, LANES)) == rows_of(LANES)).astype(F32).astype(BF16)
        moved = nt(value[:, LANES * k : LANES * (k + 1)], hit)
        spots = moved[0:2, :].astype(jnp.int32)
        spots = (spots[0:1, :] << 8) + spots[1:2, :]
        values = moved[16 : 16 + OWN_ROWS, :] + moved[16 + OWN_ROWS :, :]
        row = place >> 7
        start = place & (LANES - 1)
        listed[pl.ds(row, 1), :] += jnp.where(lane >= start, spots, 0)
        listed[pl.ds(row + 1, 1), :] += jnp.where(lane >= start, 0, spots)
        gathered[row] += jnp.where(wide_lane >= start, values, 0.0)
        gathered[row + 1] += jnp.where(wide_lane >= start, 0.0, values)
        place = place + jnp.sum(flags[k]).astype(jnp.int32)
    count[0] = place


def fetch_rows(chosen, first, table, got, start, stop, batch=16):
    for base in range(start, stop, batch):
        found = [
            table[pl.ds(chosen[first + j // LANES, j % LANES], 8, stride=8), :]
            for j in range(base, base + batch)
        ]
        for j in range(base, base + batch):
            got[pl.ds((j // 8) * 64 + j % 8, 8, stride=8), :] = found[j - base]


def turn_rows(got, states, nexts, aux):
    got3 = got.reshape(TILE // 8, 64, LANES)

    def chunk(c):
        return got3[:, 8 * c : 8 * c + 8, :].reshape(TILE, LANES)

    for c in range(3):
        states[:, LANES * c : LANES * (c + 1)] = chunk(c).astype(BF16)
        nexts[:, LANES * c : LANES * (c + 1)] = chunk(3 + c).astype(BF16)
    extra = chunk(6)
    states[:, 3 * LANES :] = extra.astype(BF16)
    aux[...] = extra.T[0:AUX_ROWS, :]


def copy_flat(flat, source):
    size = source.shape[1]
    whole = size // 1024

    for k in range(whole):
        flat[8 * k : 8 * k + 8, :] = source[0:1, 1024 * k : 1024 * (k + 1)].reshape(8, LANES)
    flat[8 * whole : 8 * whole + 8, :] = jnp.zeros((8, LANES), F32)
    full = (size - whole * 1024) // LANES
    for k in range(full):
        flat[8 * whole + k : 8 * whole + k + 1, :] = source[
            0:1, whole * 1024 + k * LANES : whole * 1024 + (k + 1) * LANES
        ]
    rest = size - whole * 1024 - full * LANES
    flat[8 * whole + full : 8 * whole + full + 1, 0:rest] = source[0:1, size - rest : size]


def halves(flat, start, height):
    return [flat[pl.ds(start + side, height, stride=2), :] for side in (0, 1)]


def natural(flat, start, height):
    return jnp.concatenate([flat[pl.ds(start + side, height, stride=2), :] for side in (0, 1)], axis=1)


def bias_row(flat, at):
    return jnp.concatenate([flat[at : at + 1, :], flat[at + 1 : at + 2, :]], axis=1)


def first_layer(flat, rows, eye, dst, pieces, base):
    tile = lax.broadcasted_iota(jnp.int32, (8, HID), 0)
    bias = jnp.where(tile == 0, jnp.broadcast_to(bias_row(flat, rows[2]), (8, HID)), 0.0)
    parts = split(jnp.concatenate([natural(flat, 0, OBS), bias], axis=0) * ROOT_HALF)
    for k in range(pieces):
        dst[base : base + HID, 384 * k : 384 * (k + 1)] = nt(eye, parts[k]).astype(BF16)


def action_layer(flat, eye, square, stack, first, back):
    square[0:ACT, :] = natural(flat, 2 * OBS, ACT)
    square[ACT:, :] = jnp.zeros((32 - ACT, HID), F32)
    value = square[...]
    high, low = split(value * ROOT_HALF)
    none = jnp.zeros_like(high)
    stack[...] = nt(eye, jnp.concatenate([high, high, low, none], axis=0)).astype(BF16)
    if first is not None:
        first[:, 768:896] = nt(eye, jnp.concatenate([high, high, none, low], axis=0)).astype(BF16)
        high, low = split(0.5 * value)
        back[0:32, :] = high
        back[32:64, :] = low


def second_layer(flat, rows, eye, forward, back, back_q=None, head=None):
    value = 0.5 * natural(flat, rows[0], HID)
    high, low = split(value)
    forward[:, 0:HID] = nt(eye, high).astype(BF16)
    if back is not None:
        forward[:, HID : 2 * HID] = nt(eye, low).astype(BF16)
        back[:, 0:HID] = high
        back[:, HID : 2 * HID] = low
    if back_q is not None:
        high, low = split(value * head)
        back_q[:, 0:HID] = high
        back_q[:, HID : 2 * HID] = low


def second_biases(flats, eye, bias):
    rows = [
        jnp.broadcast_to(bias_row(flat, rows[3]) * ROOT_HALF, (LANES, HID)) for flat, rows in flats
    ]
    both = jnp.concatenate([two_pieces(row) for row in rows], axis=0)
    bias[...] = nt(jnp.concatenate([eye, eye], axis=1), both)


def selector(rows, chosen):
    return chosen(rows_of(rows), lanes_of(rows)).astype(F32)


def block_pair(value):
    none = jnp.zeros_like(value)
    return jnp.concatenate(
        [jnp.concatenate([value, none], axis=1), jnp.concatenate([none, value], axis=1)], axis=0
    ).astype(BF16)


def actor_place(row, lane):
    return ((row == lane) & (row < ACT)) | ((row - 24 == lane - ACT) & (row >= 24) & (row < 24 + ACT))


def actor_head(flat, rows, forward, bias, back):
    pieces = yield from unflatten(flat[rows[1] : rows[1] + 72, :] * ROOT_HALF, 2 * ACT)
    place = selector(48, actor_place)
    forward[...] = nt(block_pair(place), pieces).astype(BF16)
    if back is not None:
        none = jnp.zeros((48, LANES), F32)
        high = jnp.concatenate([place, none], axis=1)
        low = jnp.concatenate([none, place], axis=1)
        back[...] = nt(pieces, jnp.concatenate([high, high, low], axis=0).astype(BF16)).astype(BF16)
    heads = column(flat[rows[4] : rows[4] + 1, :])
    bias[0:24, :] = heads[0:24, :]
    bias[24:48, :] = heads[ACT : ACT + 24, :]


def critic_head(flat, rows, eye, forward, bias, back, use_mean_row=None):
    pieces = yield from unflatten(flat[rows[1] : rows[1] + 8, :] * ROOT_HALF, 2)
    place = selector(16, lambda row, lane: (row == lane) & (row < 2))
    both = nt(block_pair(place), pieces)
    forward[...] = both.astype(BF16)
    bias[...] = column(flat[rows[4] : rows[4] + 1, :])[0:8, :]
    if back is None:
        return
    yield
    spread = [
        jnp.concatenate(
            [jnp.broadcast_to(both[16 * part + k : 16 * part + k + 1, :], (LANES, HID)) for part in (0, 1)],
            axis=1,
        )
        for k in (0, 1)
    ]
    columns = nt(jnp.concatenate([eye, eye], axis=1), jnp.concatenate(spread, axis=0).astype(BF16))
    back[...] = ROOT_TWO * columns
    yield
    use_mean_row(ROOT_TWO * (both[0:1, :] + both[16:17, :]))


def spread_lanes(bias):
    return jnp.concatenate([bias] * (SUB // LANES), axis=1)


def fold(value):
    parts = [value[:, k : k + LANES] for k in range(0, value.shape[1], LANES)]
    total = parts[0]
    for part in parts[1:]:
        total = total + part
    return total


def policy_parts(out, shocks):
    centre = out[0:ACT, :]
    raw = out[24 : 24 + ACT, :]
    soft, slope = softplus_pair(raw)
    spread = soft + 0.05
    pre = centre + spread * shocks
    terms = (
        -0.5 * shocks * shocks
        - jnp.log(spread)
        - HALF_LOG_TWO_PI
        - 2.0 * (LOG_TWO - pre - softplus(-2.0 * pre))
    )
    return jnp.tanh(pre), jnp.sum(terms, axis=0, keepdims=True), spread, slope


def stacked_action(value, pad):
    tall = jnp.concatenate([value, pad], axis=0)
    high, low = split(tall)
    return jnp.concatenate([high, low, high, jnp.zeros_like(high)], axis=0)


def loss_kernel(
    builds, tiles, half, chunk, block,
    meta, log_alpha, obs, nxt, act, misc_wide, noise_own, misc_own,
    own_actor, other_actor, own_critic, other_critic,
    keep, send,
    flat_ta, flat_oa, flat_tc, flat_oc,
    w1_t, w1a, w1c, wa_t, wa_o, wa_back, w2_ta, w2_tc, w2a, w2c, w2a_back, w2c_back, w2q_back,
    bias2, w3_ta, w3_oa, w3_tc, w3_oc, w3a_back, w3c_back, bias3_ta, bias3_oa, bias3_tc, bias3_oc,
    square,
    g1a, g1c, g2a, g2c, g3a, g3c, gb2a, gb2c, gb3a, gb3c, sums, total,
    z1_t, z1_a, z1_c, h1c, h2c, dz1c, dz2c, doc, h1a, h2a, dz1a, dz2a, doa,
    table, got, wide, states_before, states, states_after, nexts_after, aux, aux_after,
    gathered, listed, chosen, count, peaks, done, raw_ta, raw_oa, raw_tc, raw_oc, arrived,
):
    grid_step = pl.program_id(0)
    step = grid_step - builds

    def first_products(rows, next_rows, which=(0, 1, 2)):
        x = rows[...]
        x3 = x[:, 0:384]
        if 0 in which:
            z1_c[...] = nt(w1c[...], jnp.concatenate([x3, x], axis=1))
        if 1 in which:
            z1_a[...] = nt(w1a[...], jnp.concatenate([x3, x3], axis=1))
        if 2 in which:
            z1_t[...] = nt(w1_t[...], next_rows[...])

    def gradients(rows, which=range(6)):
        x = rows[...]
        if 0 in which:
            g2c[...] += nt(h1c[...], dz2c[...])
        if 1 in which:
            g3c[...] += nt(doc[...], h2c[...])
        if 2 in which:
            g1c[...] += nn(dz1c[...], x)
        if 3 in which:
            g2a[...] += nt(h1a[...], dz2a[...])
        if 4 in which:
            g3a[...] += nt(doa[...], h2a[...])
        if 5 in which:
            g1a[...] += nn(dz1a[...], x[:, 0:384])

    raws = (raw_ta, raw_oa, raw_tc, raw_oc)

    def parameter_copies(first):
        sources = (own_actor, other_actor, own_critic, other_critic)
        if not first:
            sources = (other_actor, own_actor, other_critic, own_critic)
        return [
            pltpu.make_async_copy(source, raw, arrived.at[k])
            for k, (source, raw) in enumerate(zip(sources, raws))
        ]

    @pl.when((grid_step == 0) & (meta[0] == 0))
    def _():
        for copy in parameter_copies(True):
            copy.start()

    @pl.when((grid_step == 0) & (meta[0] != 0))
    def _():
        for copy in parameter_copies(False):
            copy.start()

    @pl.when(grid_step == 0)
    def _():
        wide[...] = jnp.zeros_like(wide)
        gathered[...] = jnp.zeros_like(gathered)
        peaks[...] = jnp.zeros_like(peaks)
        listed[...] = jnp.zeros_like(listed)
        count[0] = 0

    @pl.when(grid_step < builds)
    def _():
        build_table(grid_step, block, obs, nxt, act, misc_wide, table, wide)
        choose(half // builds, noise_own, misc_own, listed, gathered, count)
        for k in range(0, half // builds, LANES):
            peaks[0:1, :] = jnp.maximum(peaks[0:1, :], misc_own[MISC_WEIGHT : MISC_WEIGHT + 1, k : k + LANES])

    @pl.when(grid_step == builds - 1)
    def _():
        for copy in parameter_copies(True):
            copy.wait()
        for flat, raw in zip((flat_ta, flat_oa, flat_tc, flat_oc), raws):
            copy_flat(flat, raw)
        copy = pltpu.make_async_copy(listed, chosen, done)
        copy.start()
        eye = square_eye()
        running = [
            actor_head(flat_ta, A_ROWS, w3_ta, bias3_ta, None),
            actor_head(flat_oa, A_ROWS, w3_oa, bias3_oa, w3a_back),
            critic_head(flat_tc, C_ROWS, eye, w3_tc, bias3_tc, None),
            critic_head(
                flat_oc, C_ROWS, eye, w3_oc, bias3_oc, w3c_back,
                lambda row: second_layer(flat_oc, C_ROWS, eye, w2c, w2c_back, w2q_back, row),
            ),
        ]
        flats = ((flat_ta, A_ROWS), (flat_tc, C_ROWS), (flat_oa, A_ROWS), (flat_oc, C_ROWS))
        beside = [
            lambda: first_layer(flat_oc, C_ROWS, eye, w1c, 2, 0),
            lambda: first_layer(flat_oa, A_ROWS, eye, w1a, 2, 0),
            copy.wait,
            lambda: first_layer(flat_ta, A_ROWS, eye, w1_t, 1, 0),
            lambda: first_layer(flat_tc, C_ROWS, eye, w1_t, 1, HID),
            lambda: action_layer(flat_oc, eye, square, wa_o, w1c, wa_back),
            lambda: action_layer(flat_tc, eye, square, wa_t, None, None),
            lambda: second_layer(flat_oa, A_ROWS, eye, w2a, w2a_back),
            lambda: second_layer(flat_ta, A_ROWS, eye, w2_ta, None),
            lambda: second_layer(flat_tc, C_ROWS, eye, w2_tc, None),
            lambda: second_biases(flats, eye, bias2),
        ]
        zeros = [g1a, g1c, g2a, g2c, g3a, g3c, gb2a, gb2c, gb3a, gb3c, sums]
        zeros += [h1c, h2c, dz1c, dz2c, doc, h1a, h2a, dz1a, dz2a, doa]
        fetched = 0
        while running or beside:
            running = [piece for piece in running if next(piece, True) is None]
            if beside:
                task = beside.pop(0)
                task()
                waited = task == copy.wait or fetched > 0
            for ref in zeros[:2]:
                ref[...] = jnp.zeros_like(ref)
            zeros = zeros[2:]
            if waited and fetched < TILE:
                fetch_rows(chosen, 0, table, got, fetched, fetched + 64)
                fetched += 64
        for ref in zeros:
            ref[...] = jnp.zeros_like(ref)
        fetch_rows(chosen, 0, table, got, fetched, TILE)
        turn_rows(got, states, nexts_after, aux)
        first_products(states, nexts_after)
        states_before[...] = states[...]

    @pl.when((grid_step >= builds) & (step * TILE < count[0]))
    def _():
        alpha = jnp.exp(jnp.full((1, SUB), log_alpha[0], F32))
        col0 = spread_lanes(w3c_back[:, 0:LANES])
        col1 = spread_lanes(w3c_back[:, LANES : 2 * LANES])
        pad = jnp.zeros((32 - ACT, SUB), F32)
        gap = jnp.zeros((24 - ACT, SUB), F32)
        row16 = lax.broadcasted_iota(jnp.int32, (16, SUB), 0)

        def head(weights, hidden, bias, size):
            tick()
            both = nn(weights[...], hidden)
            return both[0:size, :] + both[size : 2 * size, :] + spread_lanes(bias)

        def tick():
            task = beside.pop(0) if beside else None
            if task is not None:
                task()

        def gelu_t(t):
            tick()
            return gelu(t)

        def pair_t(t):
            tick()
            return gelu_pair(t)

        def nn_t(left, right):
            tick()
            return nn(left, right)

        def part(sub):
            lanes = slice(sub * SUB, (sub + 1) * SUB)
            per = SUB // LANES
            blocks = [gathered[step * (TILE // LANES) + sub * per + k] for k in range(per)]
            own = jnp.concatenate(blocks, axis=1)
            noise = own[0 : 2 * ACT + 1, :]
            place = step * TILE + sub * SUB + lax.broadcasted_iota(jnp.int32, (1, SUB), 1)
            counted = (place < count[0]).astype(F32)
            importance = own[OWN_WEIGHT + MISC_WEIGHT : OWN_WEIGHT + MISC_WEIGHT + 1, :]
            weight = counted * importance
            h1 = gelu_t(z1_t[0:HID, lanes])
            z2_t = nn_t(w2_ta[...], h1) + spread_lanes(bias2[:, 0 * LANES : 1 * LANES])
            hidden_a, s1a = pair_t(z1_a[:, lanes])
            z2_a = nn_t(w2a[...], twice(hidden_a)) + spread_lanes(bias2[:, 2 * LANES : 3 * LANES])
            hidden_c, s1c = pair_t(z1_c[:, lanes])
            z2_c = nn_t(w2c[...], twice(hidden_c)) + spread_lanes(bias2[:, 3 * LANES : 4 * LANES])
            yield
            h2 = gelu_t(z2_t)
            out = head(w3_ta, h2, bias3_ta[...], 48)
            last_a, s2a = pair_t(z2_a)
            out_a = head(w3_oa, last_a, bias3_oa[...], 48)
            last_c, s2c = pair_t(z2_c)
            both = nn_t(w3_oc[...], last_c)
            out_c = both[0:8, :] + both[16:24, :] + spread_lanes(bias3_oc[...])
            yield
            next_action, next_logp, _, _ = policy_parts(out, noise[0:ACT, :])
            z1_n = z1_t[HID:, lanes] + nn_t(wa_t[...], stacked_action(next_action, pad))
            shocks = noise[ACT : 2 * ACT, :]
            action, logp, spread_a, slope_a = policy_parts(out_a, shocks)
            old_action = aux[0:ACT, lanes] + aux[AUX_LOW : AUX_LOW + ACT, lanes]
            z1_q = z1_c[:, lanes] + nn_t(wa_o[...], stacked_action(action - old_action, pad))
            yield
            h1 = gelu_t(z1_n)
            z2_n = nn_t(w2_tc[...], h1) + spread_lanes(bias2[:, 1 * LANES : 2 * LANES])
            h1q, s1q = pair_t(z1_q)
            z2_q = nn_t(w2c[...], twice(h1q)) + spread_lanes(bias2[:, 3 * LANES : 4 * LANES])
            yield
            h2 = gelu_t(z2_n)
            both = nn_t(w3_tc[...], h2)
            out_t = both[0:8, :] + both[16:24, :] + spread_lanes(bias3_tc[...])
            h2q, s2q = pair_t(z2_q)
            both = nn_t(w3_oc[...], h2q)
            value_now = both[0:1, :] + both[16:17, :] + spread_lanes(bias3_oc[0:1, :])
            dz1q = nn_t(w2q_back[...], twice(s2q.astype(BF16))) * s1q
            yield
            both = nn_t(wa_back[...], dz1q.astype(BF16))
            value_back = both[0:ACT, :] + both[32 : 32 + ACT, :]
            next_spread = softplus(out_t[1:2, :]) + 0.1
            reward = aux[AUX_REWARD : AUX_REWARD + 1, lanes]
            goal = reward + DISCOUNT * (
                out_t[0:1, :] + next_spread * noise[2 * ACT : 2 * ACT + 1, :] - alpha * next_logp
            )
            q_value = out_c[0:1, :]
            soft, slope = softplus_pair(out_c[1:2, :])
            spread = soft + 0.1
            inverse = 1.0 / spread
            square_inverse = inverse * inverse
            miss = goal - q_value
            bound = jnp.minimum(jnp.maximum(miss, -3.0 * spread), 3.0 * spread)
            critic_loss = weight * (
                0.5 * miss * miss * square_inverse
                + 0.5 * bound * bound * square_inverse
                + jnp.log(spread)
            )
            mean_back = -weight * miss * square_inverse
            spread_back = weight * (1.0 - bound * bound * square_inverse) * inverse * slope
            dz2 = (col0 * mean_back + col1 * spread_back) * s2c
            back = dz2.astype(BF16)
            gb2c[...] += fold(dz2)
            dz1 = nn_t(w2c_back[...], twice(back)) * s1c
            do_c = jnp.where(
                row16 == 0,
                jnp.broadcast_to(mean_back, (16, SUB)),
                jnp.where(row16 == 1, jnp.broadcast_to(spread_back, (16, SUB)), 0.0),
            )
            gb3c[...] += fold(do_c)
            dz2c[:, lanes] = back
            dz1c[:, lanes] = dz1.astype(BF16)
            doc[:, lanes] = do_c.astype(BF16)
            h1c[:, lanes] = hidden_c
            h2c[:, lanes] = last_c
            yield
            counted_alpha = counted * alpha
            d_pre = counted_alpha * 2.0 * action - counted * value_back * (1.0 - action * action)
            d_raw = (d_pre * shocks - counted_alpha / spread_a) * slope_a
            do_a = jnp.concatenate([d_pre, gap, d_raw, gap], axis=0)
            high, low = split(ROOT_TWO * do_a)
            dz2 = nn_t(w3a_back[...], jnp.concatenate([high, low, high], axis=0)) * s2a
            back = dz2.astype(BF16)
            gb2a[...] += fold(dz2)
            gb3a[...] += fold(do_a)
            sums[0:1, :] += fold(counted)
            sums[1:2, :] += fold(counted * logp)
            sums[2:3, :] += fold(critic_loss)
            sums[3:4, :] += fold(counted * (alpha * logp - value_now))
            yield
            dz1 = nn_t(w2a_back[...], twice(back)) * s1a
            dz2a[:, lanes] = back
            dz1a[:, lanes] = dz1.astype(BF16)
            doa[:, lanes] = high
            h1a[:, lanes] = hidden_a
            h2a[:, lanes] = last_a

        first_pick = jnp.minimum(step + 1, tiles - 1) * (TILE // LANES)

        fetches = [
            lambda k=k: fetch_rows(chosen, first_pick, table, got, k, k + 16)
            for k in range(0, TILE, 16)
        ]
        sums_before = [
            lambda which=which: gradients(states_before, (which,)) for which in range(6)
        ]
        products_after = [
            lambda: turn_rows(got, states_after, nexts_after, aux_after),
            lambda: first_products(states_after, nexts_after, (0,)),
            lambda: first_products(states_after, nexts_after, (1,)),
            lambda: first_products(states_after, nexts_after, (2,)),
        ]
        beside = []
        for k, fetch in enumerate(fetches):
            beside.append(fetch)
            if k % 5 == 2 and sums_before:
                beside.append(sums_before.pop(0))
        for product in products_after:
            beside += [product, None, None, None, None]

        running = [part(sub) for sub in range(TILE // SUB)]
        while running:
            running = [piece for piece in running if next(piece, True) is None]
        while beside:
            tick()
        states_before[...] = states[...]
        states[...] = states_after[...]
        aux[...] = aux_after[...]

    @pl.when(step == tiles - 1)
    def _():
        gradients(states_before)
        total[...] = jnp.zeros_like(total)

        def sum_row(block):
            return jnp.sum(block.T, axis=0, keepdims=True)

        for side in (0, 1):
            at = side * LANES
            turned = 0.5 * g1a[at : at + LANES, :].T
            total[A_W1[side] : A_W1[side] + OBS, :] = turned[0:OBS, :]
            total[A_B + side : A_B + side + 1, :] = turned[ONE_LANE : ONE_LANE + 1, :]
            total[A_W2[side] : A_W2[side] + HID, :] = (0.5 * ROOT_HALF) * g2a[:, at : at + LANES]
            total[A_W3[side] : A_W3[side] + ACT, :] = 0.5 * g3a[0:ACT, at : at + LANES]
            total[A_W3[side] + ACT : A_W3[side] + 2 * ACT, :] = (
                0.5 * g3a[24 : 24 + ACT, at : at + LANES]
            )
            total[A_B + 2 + side : A_B + 3 + side, :] = 0.5 * sum_row(gb2a[at : at + LANES, :])
            turned = 0.5 * g1c[at : at + LANES, :].T
            total[C_W1[side] : C_W1[side] + OBS, :] = turned[0:OBS, :]
            total[C_W1[side] + OBS : C_W1[side] + OBS + ACT, :] = (
                turned[384 : 384 + ACT, :] + turned[384 + AUX_LOW : 384 + AUX_LOW + ACT, :]
            )
            total[C_B + side : C_B + side + 1, :] = turned[ONE_LANE : ONE_LANE + 1, :]
            total[C_W2[side] : C_W2[side] + HID, :] = (0.5 * ROOT_HALF) * g2c[:, at : at + LANES]
            total[C_W3[side] : C_W3[side] + 2, :] = ROOT_HALF * g3c[0:2, at : at + LANES]
            total[C_B + 2 + side : C_B + 3 + side, :] = 0.5 * sum_row(gb2c[at : at + LANES, :])
        none = jnp.zeros((LANES - 2 * ACT, LANES), F32)
        total[A_B + 4 : A_B + 5, :] = sum_row(
            jnp.concatenate([gb3a[0:ACT, :], gb3a[24 : 24 + ACT, :], none], axis=0)
        )
        none = jnp.zeros((LANES - 16, LANES), F32)
        total[C_B + 4 : C_B + 5, :] = sum_row(jnp.concatenate([gb3c[...], none], axis=0))
        total[EXTRA : EXTRA + 4, :] = sums[0:4, :]
        peak = jnp.max(peaks[0:1, :], axis=1, keepdims=True)
        for k in range(EXTRA + 8 - EXTRA_SLOTS):
            total[EXTRA_SLOTS + k : EXTRA_SLOTS + k + 1, :] = jnp.where(
                lanes_of(1) + k * LANES == meta[1], jnp.broadcast_to(peak, (1, LANES)), 0.0
            )
        count = keep.shape[0] // chunk
        for p in range(count):
            at = pl.multiple_of((meta[1] ^ p) * chunk, 8)
            keep[p * chunk : (p + 1) * chunk, :] = total[pl.ds(at, chunk), :]
            at = pl.multiple_of((meta[2] ^ p) * chunk, 8)
            send[p * chunk : (p + 1) * chunk, :] = total[pl.ds(at, chunk), :]


def losses(
    meta, log_alpha, obs, nxt, act, noise, misc, own_a, other_a, own_c, other_c, devices
):
    rows = obs.shape[1]
    half = noise.shape[1] // 2
    tiles = -(-half // TILE)
    block = next(size for size in (1280, 640, 512, 256, 128) if rows % size == 0)
    builds = rows // block
    own = half // builds
    list_rows = -(-(tiles * (TILE // LANES) + 1) // 8) * 8
    chunk = chunk_rows(devices)
    buffer_rows = chunk * devices

    def fixed(i, meta):
        return (0, 0)

    def source(i, meta):
        return (0, jnp.minimum(i, builds - 1))

    def own_source(i, meta):
        return (0, meta[0] * builds + jnp.minimum(i, builds - 1))

    def body(*refs):
        loss_kernel(builds, tiles, half, chunk, block, *refs)

    def bf(*shape):
        return pltpu.VMEM(shape, BF16)

    def f32(*shape):
        return pltpu.VMEM(shape, F32)

    features = noise.shape[0]
    return pl.pallas_call(
        body,
        out_shape=(
            jax.ShapeDtypeStruct((buffer_rows // 2, LANES), F32),
            jax.ShapeDtypeStruct((buffer_rows // 2, LANES), F32),
        ),
        grid_spec=pltpu.PrefetchScalarGridSpec(
            num_scalar_prefetch=1,
            grid=(builds + tiles,),
            in_specs=[
                pl.BlockSpec(memory_space=pltpu.SMEM),
                pl.BlockSpec((OBS, block), source),
                pl.BlockSpec((OBS, block), source),
                pl.BlockSpec((ACT, block), source),
                pl.BlockSpec((8, block), source),
                pl.BlockSpec((features, own), own_source),
                pl.BlockSpec((8, own), own_source),
                pl.BlockSpec(memory_space=pl.ANY),
                pl.BlockSpec(memory_space=pl.ANY),
                pl.BlockSpec(memory_space=pl.ANY),
                pl.BlockSpec(memory_space=pl.ANY),
            ],
            out_specs=(
                pl.BlockSpec((buffer_rows // 2, LANES), fixed),
                pl.BlockSpec((buffer_rows // 2, LANES), fixed),
            ),
            scratch_shapes=[
                f32(A_FLAT, LANES), f32(A_FLAT, LANES), f32(C_FLAT, LANES), f32(C_FLAT, LANES),
                bf(512, 384), bf(HID, 768), bf(HID, 896),
                bf(HID, LANES), bf(HID, LANES), bf(64, HID),
                bf(HID, HID), bf(HID, HID),
                bf(HID, 512), bf(HID, 512), bf(HID, 512), bf(HID, 512), bf(HID, 512),
                f32(HID, 4 * LANES), bf(96, HID), bf(96, HID), bf(32, HID), bf(32, HID),
                bf(HID, 144), f32(HID, 2 * LANES),
                f32(48, LANES), f32(48, LANES), f32(8, LANES), f32(8, LANES),
                f32(32, HID),
                f32(HID, 384), f32(HID, 512), f32(HID, HID), f32(HID, HID),
                f32(48, HID), f32(16, HID), f32(HID, LANES), f32(HID, LANES),
                f32(48, LANES), f32(16, LANES), f32(8, LANES), f32(buffer_rows, LANES),
                f32(2 * HID, TILE), f32(HID, TILE), f32(HID, TILE),
                bf(HID, TILE), bf(HID, TILE), bf(HID, TILE), bf(HID, TILE), bf(16, TILE),
                bf(HID, TILE), bf(HID, TILE), bf(HID, TILE), bf(HID, TILE), bf(48, TILE),
                f32((rows + 8) * CHUNKS, LANES), f32(TILE * 8, LANES), f32(LANES, block),
                bf(TILE, 512), bf(TILE, 512), bf(TILE, 512), bf(TILE, 384),
                f32(AUX_ROWS, TILE), f32(AUX_ROWS, TILE),
                f32(list_rows, OWN_ROWS, LANES),
                pltpu.VMEM((list_rows, LANES), jnp.int32),
                pltpu.SMEM((list_rows, LANES), jnp.int32),
                pltpu.SMEM((1,), jnp.int32), f32(8, LANES), pltpu.SemaphoreType.DMA,
                f32(1, A_SIZE), f32(1, A_SIZE), f32(1, C_SIZE), f32(1, C_SIZE),
                pltpu.SemaphoreType.DMA((4,)),
            ],
        ),
        compiler_params=pltpu.CompilerParams(
            dimension_semantics=("arbitrary",), vmem_limit_bytes=VMEM_BYTES
        ),
        name="losses",
    )(meta, log_alpha, obs, nxt, act, misc, noise, misc, own_a, other_a, own_c, other_c)


def stat_pieces(width_in, width_out):
    sizes = [width_in, HID, HID, HID, HID, width_out, HID, HID, width_out]
    starts = [sum(sizes[:k]) for k in range(len(sizes))]
    rows = [-(-size // LANES) for size in sizes]
    return sizes, starts, [sum(rows[:k]) for k in range(len(rows))], sum(rows)


def aligned_stats(statistics, width_in, width_out):
    sizes, starts, _, rows = stat_pieces(width_in, width_out)
    pieces = [
        jnp.pad(statistics[start : start + size], (0, -size % LANES))
        for size, start in zip(sizes, starts)
    ]
    pieces.append(jnp.zeros((-rows % 8 * LANES,), F32))
    return jnp.concatenate(pieces).reshape(-1, LANES)


def blend(old, new):
    return DECAY_RATE * old + (1.0 - DECAY_RATE) * new


def clip_scale(square_sum, number):
    return 1.0 / jnp.maximum(1.0, jnp.sqrt(square_sum / number) / CLIP_LEVEL)


def whole_sum(value):
    return jnp.sum(jnp.sum(value, axis=0, keepdims=True), axis=1, keepdims=True)


def large_layers(total, scale, old_row, width_in, places, rows, fg, fu, lines):
    for layer, (height, flat_at) in enumerate(((width_in, 0), (HID, rows[0]))):
        parts = [total[at : at + height, :] * scale for at in places[layer]]
        squares = [g * g + TINY_TERM for g in parts]
        yield
        blocks = -(-height // LANES)
        old = jnp.concatenate([column(old_row(layer, k)) for k in range(blocks)], axis=0)
        old = old[0:height, :]
        mean = jnp.sum(squares[0] + squares[1], axis=1, keepdims=True) * (1.0 / HID)
        row_stat = blend(old, jnp.broadcast_to(mean, (height, LANES)))
        yield
        for k in range(blocks):
            block = row_stat[k * LANES : min(height, (k + 1) * LANES), :]
            if block.shape[0] < LANES:
                block = jnp.concatenate(
                    [block, jnp.zeros((LANES - block.shape[0], LANES), F32)], axis=0
                )
            lines[layer].append(block.T[0:1, :])
        mean_row = jnp.sum(row_stat, axis=0, keepdims=True) * (1.0 / height)
        row_root = lax.rsqrt(row_stat)
        yield
        steps = []
        square_sum = 0.0
        for side in (0, 1):
            col_stat = blend(
                old_row(3 + layer, side),
                jnp.sum(squares[side], axis=0, keepdims=True) * (1.0 / height),
            )
            lines[3 + layer].append(col_stat)
            step = (parts[side] * row_root) * (lax.rsqrt(col_stat) * jnp.sqrt(mean_row))
            square_sum = square_sum + jnp.sum(step * step, axis=0, keepdims=True)
            steps.append(step)
            fg[pl.ds(flat_at + side, height, stride=2), :] = parts[side]
            yield
        square_sum = jnp.sum(square_sum, axis=1, keepdims=True)
        factor = clip_scale(square_sum, float(height * HID))
        for side in (0, 1):
            fu[pl.ds(flat_at + side, height, stride=2), :] = steps[side] * factor
            yield


def last_layer(total, scale, old_row, width_out, place, rows, fg, fu, lines):
    tall = -(-width_out // 8) * 8
    parts = [total[at : at + tall, :] * scale for at in place]
    real = rows_of(tall) < width_out
    squares = [jnp.where(real, g * g + TINY_TERM, 0.0) for g in parts]
    old = column(old_row(5, 0))[0:tall, :]
    mean = jnp.sum(squares[0] + squares[1], axis=1, keepdims=True) * (1.0 / HID)
    col_stat = blend(old, jnp.broadcast_to(mean, (tall, LANES)))
    pad = jnp.zeros((LANES - tall, LANES), F32)
    lines[5].append(jnp.concatenate([col_stat, pad], axis=0).T[0:1, :])
    yield
    row_stats = []
    for side in (0, 1):
        row_stats.append(
            blend(
                old_row(2, side),
                jnp.sum(squares[side], axis=0, keepdims=True) * (1.0 / width_out),
            )
        )
        lines[2].append(row_stats[side])
    mean_row = jnp.sum(row_stats[0] + row_stats[1], axis=1, keepdims=True) * (1.0 / HID)
    col_root = jnp.where(real, lax.rsqrt(col_stat), 0.0)
    steps = [
        (parts[side] * lax.rsqrt(row_stats[side])) * (col_root * jnp.sqrt(mean_row))
        for side in (0, 1)
    ]
    factor = clip_scale(
        whole_sum(steps[0] * steps[0] + steps[1] * steps[1]), float(HID * width_out)
    )
    yield
    size = rows[2] - rows[1]
    turned = [
        jnp.concatenate(
            [jnp.concatenate([jnp.where(real, part, 0.0), pad], axis=0).T for part in pair], axis=0
        )
        for pair in (parts, [u * factor for u in steps])
    ]
    yield
    flat_parts = yield from flatten(turned, width_out, -(-size // 8) * 8)
    for flat, part in zip((fg, fu), flat_parts):
        flat[rows[1] : rows[1] + size, :] = part[0:size, :]


def biases(total, scale, old, width_out, bias_at, rows, fg, fu, lines):
    grad = total[bias_at : bias_at + 8, :] * scale
    line = rows_of(8)
    lane = lanes_of(8)
    real = (line < 4) | ((line == 4) & (lane < width_out))
    grad = jnp.where(real, grad, 0.0)
    stat = blend(old, grad[0:5, :] * grad[0:5, :] + TINY_TERM)
    step = jnp.where(real[0:5, :], grad[0:5, :] * lax.rsqrt(stat), 0.0)
    yield
    factor = clip_scale(whole_sum(step * step), float(2 * HID + width_out))
    fg[rows[2] : rows[2] + 5, :] = grad[0:5, :]
    fu[rows[2] : rows[2] + 5, :] = step * factor
    for k in range(5):
        lines[6 + k // 2].append(stat[k : k + 1, :])


def store_statistics(lines, width_in, width_out, stats_out):
    sizes, starts, _, _ = stat_pieces(width_in, width_out)
    size = stats_out.shape[0]
    count = -(-size // LANES)
    made = [jnp.zeros((1, LANES), F32) for _ in range(count + 1)]
    lane = lanes_of(1)
    for piece, pieces in enumerate(lines):
        for k, value in enumerate(pieces):
            start = starts[piece] + k * LANES
            width = min(LANES, sizes[piece] - k * LANES)
            value = jnp.where(lane < width, value, 0.0)
            shift = start % LANES
            at = start // LANES
            if shift:
                value = pltpu.roll(value, shift, 1)
            made[at] = made[at] + jnp.where(lane >= shift, value, 0.0)
            if shift:
                made[at + 1] = made[at + 1] + jnp.where(lane < shift, value, 0.0)
    for k in range(count):
        width = min(LANES, size - k * LANES)
        stats_out[pl.ds(k * LANES, width)] = made[k][:, 0:width].reshape(width)


def in_turn(stages):
    while stages:
        stages = [stage for stage in stages if next(stage, True) is None]


def net_update(total, scale, old_stats, width_in, width_out, places, rows, fg, fu):
    sizes, _, first, _ = stat_pieces(width_in, width_out)
    lines = [[] for _ in sizes]

    def old_row(piece, k):
        return old_stats[first[piece] + k : first[piece] + k + 1, :]

    old_bias = old_stats[first[6] : first[6] + 5, :]
    large = large_layers(total, scale, old_row, width_in, places, rows, fg, fu, lines)
    small = [
        last_layer(total, scale, old_row, width_out, places[2], rows, fg, fu, lines),
        biases(total, scale, old_bias, width_out, places[3], rows, fg, fu, lines),
    ]
    return large, small, lines


def write_net(side, own, other, fg, fu, slot, copy, grad):
    size = own.shape[1]
    whole = size // 1024

    def piece(at, row, width, count):
        mine = own[0:1, pl.ds(at, width)].reshape(count, width // count)
        theirs = other[0:1, pl.ds(at, width)].reshape(count, width // count)
        wide = width // count
        step = fu[pl.ds(row, count), 0:wide]
        online = jnp.where(side == 0, theirs, mine)
        new = online - LEARN_RATE * step
        held = jnp.where(side == 0, POLYAK_RATE * new + (1.0 - POLYAK_RATE) * mine, new)
        slot[0:1, pl.ds(at, width)] = held.reshape(1, width)
        copy[0:1, pl.ds(at, width)] = held.reshape(1, width).astype(BF16)
        grad[pl.ds(at, width)] = fg[pl.ds(row, count), 0:wide].reshape(width)

    for k in range(whole):
        piece(k * 1024, k * 8, 1024, 8)
    full = size // LANES
    for row in range(whole * 8, full):
        piece(row * LANES, row, LANES, 1)
    piece(full * LANES, full, size - full * LANES, 1)


def update_kernel(
    chunk, devices,
    meta, log_alpha, mine, theirs, own_a, other_a, own_c, other_c, stats_a, stats_c,
    slot_a, slot_c, copy_a, copy_c, grad_a, grad_c, new_a, new_c, summary, alpha_out,
    total, fg_a, fu_a, fg_c, fu_c,
):
    count = devices // 2
    for p in range(count):
        at = pl.multiple_of((meta[1] ^ p) * chunk, 8)
        total[pl.ds(at, chunk), :] = mine[p * chunk : (p + 1) * chunk, :]
        at = pl.multiple_of((meta[2] ^ p) * chunk, 8)
        total[pl.ds(at, chunk), :] = theirs[p * chunk : (p + 1) * chunk, :]

    sums = jnp.sum(total[EXTRA : EXTRA + 8, :], axis=1, keepdims=True)
    peak = jnp.max(total[EXTRA_SLOTS : EXTRA + 8, :], axis=1, keepdims=True)
    peak = jnp.max(peak, axis=0, keepdims=True)
    counted = sums[0:1, :]
    scale_a = 1.0 / counted
    scale_c = scale_a / peak
    lane = lanes_of(1)
    line = jnp.where(
        lane == 0,
        jnp.broadcast_to(sums[2:3, :] / peak, (1, LANES)),
        jnp.where(
            lane == 1,
            jnp.broadcast_to(sums[3:4, :], (1, LANES)),
            jnp.broadcast_to(counted, (1, LANES)),
        ),
    )
    summary[...] = line[:, 0:3].reshape(3)
    new_alpha = log_alpha[0] + ALPHA_STEP * (
        jnp.broadcast_to(sums[1:2, :] / counted, (1, LANES)) - ACT
    )
    alpha_out[...] = new_alpha[:, 0:1].reshape(1)
    large_a, small_a, lines_a = net_update(
        total, scale_a, stats_a, OBS, 2 * ACT, (A_W1, A_W2, A_W3, A_B), A_ROWS, fg_a, fu_a
    )
    large_c, small_c, lines_c = net_update(
        total, scale_c, stats_c, OBS + ACT, 2, (C_W1, C_W2, C_W3, C_B), C_ROWS, fg_c, fu_c
    )
    in_turn([large_a] + small_a)
    in_turn([large_c] + small_c)
    store_statistics(lines_a, OBS, 2 * ACT, new_a)
    store_statistics(lines_c, OBS + ACT, 2, new_c)
    write_net(meta[0], own_a, other_a, fg_a, fu_a, slot_a, copy_a, grad_a)
    write_net(meta[0], own_c, other_c, fg_c, fu_c, slot_c, copy_c, grad_c)


def update(meta, log_alpha, mine, theirs, own_a, other_a, own_c, other_c, stats_a, stats_c, sizes, devices):
    chunk = chunk_rows(devices)

    def body(*refs):
        update_kernel(chunk, devices, *refs)

    def f32(*shape):
        return jax.ShapeDtypeStruct(shape, F32)

    smem = pl.BlockSpec(memory_space=pltpu.SMEM)
    vmem = pl.BlockSpec(memory_space=pltpu.VMEM)
    return pl.pallas_call(
        body,
        out_shape=(
            f32(1, A_SIZE), f32(1, C_SIZE),
            jax.ShapeDtypeStruct((1, A_SIZE), BF16), jax.ShapeDtypeStruct((1, C_SIZE), BF16),
            f32(A_SIZE), f32(C_SIZE), f32(sizes[0]), f32(sizes[1]), f32(3), f32(1),
        ),
        in_specs=[smem, smem] + [vmem] * 8,
        out_specs=tuple([vmem] * 10),
        scratch_shapes=[
            pltpu.VMEM((chunk * devices, LANES), F32),
            pltpu.VMEM((A_FLAT, LANES), F32), pltpu.VMEM((A_FLAT, LANES), F32),
            pltpu.VMEM((C_FLAT, LANES), F32), pltpu.VMEM((C_FLAT, LANES), F32),
        ],
        compiler_params=pltpu.CompilerParams(vmem_limit_bytes=UPDATE_VMEM_BYTES),
        name="optimizer",
    )(meta, log_alpha, mine, theirs, own_a, other_a, own_c, other_c, stats_a, stats_c)


def chunk_rows(devices):
    return -(-DATA_ROWS // (8 * devices)) * 8


def stage_bits(count, group):
    number = count.bit_length() - 1
    bits = [(bit + 2 * group) % number for bit in range(number)]
    return [bits[k : k + 2] for k in range(0, number, 2)]


def swap_groups(value):
    return lax.ppermute(value, "grp", [(0, 1), (1, 0)])


def exchange(value, stage, digit):
    count = lax.axis_size("dp")
    pairs = []
    for group in (0, 1):
        bits = stage_bits(count, group)[stage]
        mask = sum(1 << bit for k, bit in enumerate(bits) if digit >> k & 1)
        pairs += [(group * count + i, group * count + (i ^ mask)) for i in range(count)]
    return lax.ppermute(value, ("grp", "dp"), pairs)


def buffer_place(group, count):
    index = lax.axis_index("dp")
    place = group
    for bits in stage_bits(count, group):
        for bit in reversed(bits):
            place = place * 2 + (index >> bit & 1)
    return place


def all_sum(keep, send):
    count = lax.axis_size("dp")
    sizes = [1 << len(bits) for bits in stage_bits(count, 0)]
    value = keep + swap_groups(send)
    for stage, size in enumerate(sizes):
        rows = value.shape[0] // size
        parts = [value[k * rows : (k + 1) * rows] for k in range(size)]
        came = [exchange(parts[k], stage, k) for k in range(1, size)]
        value = parts[0]
        for part in came:
            value = value + part
    for stage, size in reversed(list(enumerate(sizes))):
        value = jnp.concatenate(
            [value] + [exchange(value, stage, k) for k in range(1, size)], axis=0
        )
    return value, swap_groups(value)


def shards(
    obs_rows,
    next_rows,
    action_rows,
    reward_rows,
    batch_index,
    valid_mask,
    noise,
    importance,
    actor_params,
    critic_params,
    actor_stats,
    critic_stats,
    log_alpha,
):
    devices = lax.axis_size("dp") * lax.axis_size("grp")
    group_side = lax.axis_index("grp")
    other_a = swap_groups(actor_params)
    other_c = swap_groups(critic_params)
    places = [buffer_place(group, lax.axis_size("dp")) for group in (0, 1)]
    number = jnp.arange(3)
    meta = jnp.where((number == 1) == (group_side == 0), places[0], places[1])
    meta = jnp.where(number == 0, group_side, meta).astype(jnp.int32)
    row = lax.broadcasted_iota(jnp.int32, (8, batch_index.shape[0]), 0)
    misc = jnp.where(row == MISC_VALID, valid_mask[None], batch_index[None]).astype(F32)
    misc = jnp.where(row == MISC_WEIGHT, importance[None], misc)
    misc = jnp.where(row == 0, reward_rows[None], misc)
    keep, send = losses(
        meta, log_alpha, obs_rows.T, next_rows.T, action_rows.T, noise.T, misc,
        actor_params, other_a, critic_params, other_c, devices,
    )
    keep, send, actor_stats, critic_stats = lax.optimization_barrier(
        (keep, send, actor_stats, critic_stats)
    )
    mine, theirs = all_sum(keep, send)
    (
        slot_a, slot_c, copy_a, copy_c, grad_a, grad_c, new_a, new_c, summary, alpha
    ) = update(
        meta, log_alpha, mine, theirs, actor_params, other_a, critic_params, other_c,
        aligned_stats(actor_stats, OBS, 2 * ACT), aligned_stats(critic_stats, OBS + ACT, 2),
        (actor_stats.shape[0], critic_stats.shape[0]), devices,
    )
    return (
        slot_a, slot_c, copy_a, copy_c, grad_a, grad_c, new_a, new_c,
        summary, alpha,
    )


def solution(mesh):
    return jax.shard_map(
        shards,
        mesh=mesh,
        in_specs=(
            P("dp", None),
            P("dp", None),
            P("dp", None),
            P("dp"),
            P("dp"),
            P("dp"),
            P("dp", None),
            P("dp"),
            P("grp", None),
            P("grp", None),
            P(),
            P(),
            P(),
        ),
        out_specs=(
            P("grp", None),
            P("grp", None),
            P("grp", None),
            P("grp", None),
            P(),
            P(),
            P(),
            P(),
            P(),
            P(),
        ),
        check_vma=False,
    )
```

```python
import jax
import jax.numpy as jnp
from jax import lax
from jax.experimental import pallas as pl
from jax.experimental.pallas import tpu as pltpu
from jax.sharding import PartitionSpec as P

OBS = 376
ACT = 17
HID = 256
LANES = 128
TILE = 512
SUB = 256

DISCOUNT = 0.99
POLYAK_RATE = 0.1
DECAY_RATE = 0.5
LEARN_RATE = 0.1
CLIP_LEVEL = 0.1
ALPHA_STEP = 0.01
TINY_TERM = 1e-30
HALF_LOG_TWO_PI = 0.9189385332046727
LOG_TWO = 0.6931471805599453
ROOT_HALF = 0.7071067811865476
ROOT_TWO = 1.4142135623730951
LOG2_E = 1.4426950408889634
LOG2_TWO_OVER_ROOT_PI = 0.17425193548825

F32 = jnp.float32
BF16 = jnp.bfloat16
VMEM_BYTES = 57 * 2**20
UPDATE_VMEM_BYTES = 24 * 2**20

ONE_LANE = OBS
AUX_LOW = 32
AUX_REWARD = 64
AUX_AGAIN = 96
AUX_ROWS = 72
CHUNKS = 7
OWN_WEIGHT = 40
OWN_ROWS = 48
MISC_WEIGHT = 1
MISC_VALID = 2
MISC_INDEX = 3


def flat_rows(width_in, width_out):
    w2 = width_in * HID // LANES
    w3 = w2 + HID * HID // LANES
    b1 = w3 + HID * width_out // LANES
    return w2, w3, b1, b1 + 2, b1 + 4


A_ROWS = flat_rows(OBS, 2 * ACT)
C_ROWS = flat_rows(OBS + ACT, 2)
A_SIZE = A_ROWS[4] * LANES + 2 * ACT
C_SIZE = C_ROWS[4] * LANES + 2
A_FLAT = -(-A_SIZE // 1024) * 8
C_FLAT = -(-C_SIZE // 1024) * 8

A_W1 = (0, OBS)
A_W2 = (2 * OBS, 2 * OBS + HID)
A_W3 = (2 * OBS + 2 * HID, 2 * OBS + 2 * HID + 40)
A_B = A_W3[1] + 40
C_W1 = (A_B + 8, A_B + 8 + 400)
C_W2 = (C_W1[1] + 400, C_W1[1] + 400 + HID)
C_W3 = (C_W2[1] + HID, C_W2[1] + HID + 8)
C_B = C_W3[1] + 8
EXTRA = C_B + 8
EXTRA_SLOTS = EXTRA + 4
DATA_ROWS = EXTRA + 8


def nn(left, right):
    return lax.dot_general(
        left, right, (((1,), (0,)), ((), ())), preferred_element_type=F32
    )


def nt(left, right):
    return lax.dot_general(
        left, right, (((1,), (1,)), ((), ())), preferred_element_type=F32
    )


def split(value):
    high = value.astype(BF16)
    return high, (value - high.astype(F32)).astype(BF16)


def twice(value):
    return jnp.concatenate([value, value], axis=0)


def gelu(t):
    return (t * (1.0 + lax.erf(t))).astype(BF16)


def gelu_pair(t):
    double_cdf = 1.0 + lax.erf(t)
    bell = jnp.exp2(LOG2_TWO_OVER_ROOT_PI - LOG2_E * (t * t))
    return (t * double_cdf).astype(BF16), double_cdf + t * bell


def softplus(x):
    return jnp.maximum(x, 0.0) + jnp.log(1.0 + jnp.exp(-jnp.abs(x)))


def softplus_pair(x):
    decay = jnp.exp(-jnp.abs(x))
    inverse = 1.0 / (1.0 + decay)
    return jnp.maximum(x, 0.0) + jnp.log(1.0 + decay), jnp.where(x >= 0.0, inverse, decay * inverse)


def column(row):
    return jnp.broadcast_to(row, (LANES, LANES)).T


def rows_of(count):
    return lax.broadcasted_iota(jnp.int32, (count, LANES), 0)


def lanes_of(count):
    return lax.broadcasted_iota(jnp.int32, (count, LANES), 1)


def square_eye(reverse=False):
    row = lax.broadcasted_iota(jnp.int32, (HID, HID), 0)
    lane = lax.broadcasted_iota(jnp.int32, (HID, HID), 1)
    return (row == (HID - 1 - lane if reverse else lane)).astype(F32).astype(BF16)


def two_pieces(value):
    return jnp.concatenate(split(value), axis=1)


def turns(value, shift, stride):
    turn = (rows_of(HID) * stride + shift) % LANES
    for step in (2, 4, 8, 16, 32, 64):
        value = jnp.where((turn & step) != 0, pltpu.roll(value, step, 1), value)
        yield value


def unflatten(flat, width):
    rows = flat.shape[0]
    first = (HID - 1 - rows_of(HID)) * width
    lane = lanes_of(HID)
    owner = first // LANES
    picks = jnp.concatenate([(owner == lane), (owner + 1 == lane)], axis=0).astype(F32).astype(BF16)
    found = nn(picks[:, 0:rows], two_pieces(flat))
    yield
    found = found[:, 0:LANES] + found[:, LANES:]
    mixed = jnp.where(lane >= first % LANES, found[0:HID, :], found[HID:, :])
    for turned in turns(mixed, -(HID - 1) * width % LANES, width):
        yield
    pieces = nn(square_eye(True), two_pieces(turned)).astype(BF16)
    yield
    return pieces


def flatten(values, width, rows):
    first = rows_of(HID) * width % LANES
    lane = lanes_of(HID)
    for turned in turns(values[0] + pltpu.roll(values[1], 64, 1), 0, width):
        yield
    swapped = pltpu.roll(turned, 64, 1)
    begun = (lane >= first) & (lane < first + width)
    wrapped = lane < first + width - LANES
    parts = []
    for value in (turned, swapped):
        parts.append(
            jnp.concatenate([jnp.where(begun, value, 0.0), jnp.where(wrapped, value, 0.0)], axis=0)
        )
    both = jnp.concatenate(parts, axis=1)
    high, low = split(both)
    least = (both - high.astype(F32) - low.astype(F32)).astype(BF16)
    owner = lax.broadcasted_iota(jnp.int32, (rows, HID), 1) * width // LANES
    row = lax.broadcasted_iota(jnp.int32, (rows, HID), 0)
    places = jnp.concatenate([owner == row, owner + 1 == row], axis=1).astype(F32).astype(BF16)
    yield
    found = nn(places, jnp.concatenate([high, low, least], axis=1))
    yield
    found = found[:, 0:HID] + found[:, HID : 2 * HID] + found[:, 2 * HID :]
    return found[:, 0:LANES], found[:, LANES:]


def build_table(step, block, obs, nxt, act, misc, table, wide):
    groups = block // 8
    table3 = table.reshape(table.shape[0] // (8 * CHUNKS), 8 * CHUNKS, LANES)
    at = pl.multiple_of(step * groups, groups)

    def put(value, first):
        for c in range(value.shape[1] // LANES):
            table3[pl.ds(at, groups), 8 * (first + c) : 8 * (first + c) + 8, :] = value[
                :, LANES * c : LANES * (c + 1)
            ].reshape(groups, 8, LANES)

    ones = (lax.broadcasted_iota(jnp.int32, (8, block), 0) == 0).astype(F32)
    whole = OBS // 16 * 16

    def padded(source):
        value = source[...]
        rest = jnp.concatenate([value[whole:, :].astype(F32), ones], axis=0).astype(BF16)
        return jnp.concatenate([value[0:whole, :], rest], axis=0)

    value = padded(obs)
    eye = square_eye()
    turned = [nt(eye, value[:, k : k + HID]) for k in range(0, block, HID)]
    put(jnp.concatenate(turned, axis=0), 0)
    put(padded(nxt).T.astype(F32), 3)
    action = act[...]
    high = action.astype(BF16).astype(F32)
    wide[0:ACT, :] = high
    wide[AUX_LOW : AUX_LOW + ACT, :] = action - high
    wide[AUX_AGAIN : AUX_AGAIN + ACT, :] = high
    wide[AUX_REWARD : AUX_REWARD + 8, :] = misc[...]
    put(wide[...].T, 6)


def choose(size, noise, misc, listed, gathered, count):
    lane = lanes_of(1)
    wide_lane = lanes_of(OWN_ROWS)
    parts = size // LANES
    counted = misc[MISC_VALID : MISC_VALID + 1, :]
    flags = [counted[:, LANES * k : LANES * (k + 1)] for k in range(parts)]
    stacked = jnp.concatenate(flags + [jnp.zeros((-parts % 16, LANES), F32)], axis=0).astype(BF16)
    before = nn(stacked, (rows_of(LANES) < lanes_of(LANES)).astype(F32).astype(BF16))
    before = before.astype(jnp.int32)
    index = misc[MISC_INDEX : MISC_INDEX + 1, :].astype(jnp.int32)
    spot = (index >> 3) * (8 * CHUNKS) + (index & 7)
    digits = jnp.concatenate([spot >> 8, spot & 255] + [jnp.zeros_like(spot)] * 14, axis=0)
    gap = jnp.zeros((OWN_WEIGHT - 2 * ACT - 1, size), F32)
    high, low = split(jnp.concatenate([noise[...], gap, misc[...]], axis=0))
    value = jnp.concatenate([digits.astype(F32).astype(BF16), high, low], axis=0)
    place = count[0]
    for k in range(parts):
        where = (before[k : k + 1, :] + place) & (LANES - 1)
        where = jnp.where(flags[k] > 0.0, where, -1)
        hit = (jnp.broadcast_to(where, (LANES, LANES)) == rows_of(LANES)).astype(F32).astype(BF16)
        moved = nt(value[:, LANES * k : LANES * (k + 1)], hit)
        spots = moved[0:2, :].astype(jnp.int32)
        spots = (spots[0:1, :] << 8) + spots[1:2, :]
        values = moved[16 : 16 + OWN_ROWS, :] + moved[16 + OWN_ROWS :, :]
        row = place >> 7
        start = place & (LANES - 1)
        listed[pl.ds(row, 1), :] += jnp.where(lane >= start, spots, 0)
        listed[pl.ds(row + 1, 1), :] += jnp.where(lane >= start, 0, spots)
        gathered[row] += jnp.where(wide_lane >= start, values, 0.0)
        gathered[row + 1] += jnp.where(wide_lane >= start, 0.0, values)
        place = place + jnp.sum(flags[k]).astype(jnp.int32)
    count[0] = place


def fetch_rows(chosen, first, table, got, start, stop, batch=16):
    for base in range(start, stop, batch):
        found = [
            table[pl.ds(chosen[first + j // LANES, j % LANES], 8, stride=8), :]
            for j in range(base, base + batch)
        ]
        for j in range(base, base + batch):
            got[pl.ds((j // 8) * 64 + j % 8, 8, stride=8), :] = found[j - base]


def turn_rows(got, states, nexts, aux):
    got3 = got.reshape(TILE // 8, 64, LANES)

    def chunk(c):
        return got3[:, 8 * c : 8 * c + 8, :].reshape(TILE, LANES)

    for c in range(3):
        states[:, LANES * c : LANES * (c + 1)] = chunk(c).astype(BF16)
        nexts[:, LANES * c : LANES * (c + 1)] = chunk(3 + c).astype(BF16)
    extra = chunk(6)
    states[:, 3 * LANES :] = extra.astype(BF16)
    aux[...] = extra.T[0:AUX_ROWS, :]


def copy_flat(flat, source):
    size = source.shape[1]
    whole = size // 1024

    for k in range(whole):
        flat[8 * k : 8 * k + 8, :] = source[0:1, 1024 * k : 1024 * (k + 1)].reshape(8, LANES)
    flat[8 * whole : 8 * whole + 8, :] = jnp.zeros((8, LANES), F32)
    full = (size - whole * 1024) // LANES
    for k in range(full):
        flat[8 * whole + k : 8 * whole + k + 1, :] = source[
            0:1, whole * 1024 + k * LANES : whole * 1024 + (k + 1) * LANES
        ]
    rest = size - whole * 1024 - full * LANES
    flat[8 * whole + full : 8 * whole + full + 1, 0:rest] = source[0:1, size - rest : size]


def halves(flat, start, height):
    return [flat[pl.ds(start + side, height, stride=2), :] for side in (0, 1)]


def natural(flat, start, height):
    return jnp.concatenate([flat[pl.ds(start + side, height, stride=2), :] for side in (0, 1)], axis=1)


def bias_row(flat, at):
    return jnp.concatenate([flat[at : at + 1, :], flat[at + 1 : at + 2, :]], axis=1)


def first_layer(flat, rows, eye, dst, pieces, base):
    tile = lax.broadcasted_iota(jnp.int32, (8, HID), 0)
    bias = jnp.where(tile == 0, jnp.broadcast_to(bias_row(flat, rows[2]), (8, HID)), 0.0)
    parts = split(jnp.concatenate([natural(flat, 0, OBS), bias], axis=0) * ROOT_HALF)
    for k in range(pieces):
        dst[base : base + HID, 384 * k : 384 * (k + 1)] = nt(eye, parts[k]).astype(BF16)


def action_layer(flat, eye, square, stack, first, back):
    square[0:ACT, :] = natural(flat, 2 * OBS, ACT)
    square[ACT:, :] = jnp.zeros((32 - ACT, HID), F32)
    value = square[...]
    high, low = split(value * ROOT_HALF)
    none = jnp.zeros_like(high)
    stack[...] = nt(eye, jnp.concatenate([high, high, low, none], axis=0)).astype(BF16)
    if first is not None:
        first[:, 768:896] = nt(eye, jnp.concatenate([high, high, none, low], axis=0)).astype(BF16)
        high, low = split(0.5 * value)
        back[0:32, :] = high
        back[32:64, :] = low


def second_layer(flat, rows, eye, forward, back, back_q=None, head=None):
    value = 0.5 * natural(flat, rows[0], HID)
    high, low = split(value)
    forward[:, 0:HID] = nt(eye, high).astype(BF16)
    if back is not None:
        forward[:, HID : 2 * HID] = nt(eye, low).astype(BF16)
        back[:, 0:HID] = high
        back[:, HID : 2 * HID] = low
    if back_q is not None:
        high, low = split(value * head)
        back_q[:, 0:HID] = high
        back_q[:, HID : 2 * HID] = low


def second_biases(flats, eye, bias):
    rows = [
        jnp.broadcast_to(bias_row(flat, rows[3]) * ROOT_HALF, (LANES, HID)) for flat, rows in flats
    ]
    both = jnp.concatenate([two_pieces(row) for row in rows], axis=0)
    bias[...] = nt(jnp.concatenate([eye, eye], axis=1), both)


def selector(rows, chosen):
    return chosen(rows_of(rows), lanes_of(rows)).astype(F32)


def block_pair(value):
    none = jnp.zeros_like(value)
    return jnp.concatenate(
        [jnp.concatenate([value, none], axis=1), jnp.concatenate([none, value], axis=1)], axis=0
    ).astype(BF16)


def actor_place(row, lane):
    return ((row == lane) & (row < ACT)) | ((row - 24 == lane - ACT) & (row >= 24) & (row < 24 + ACT))


def actor_head(flat, rows, forward, bias, back):
    pieces = yield from unflatten(flat[rows[1] : rows[1] + 72, :] * ROOT_HALF, 2 * ACT)
    place = selector(48, actor_place)
    forward[...] = nt(block_pair(place), pieces).astype(BF16)
    if back is not None:
        none = jnp.zeros((48, LANES), F32)
        high = jnp.concatenate([place, none], axis=1)
        low = jnp.concatenate([none, place], axis=1)
        back[...] = nt(pieces, jnp.concatenate([high, high, low], axis=0).astype(BF16)).astype(BF16)
    heads = column(flat[rows[4] : rows[4] + 1, :])
    bias[0:24, :] = heads[0:24, :]
    bias[24:48, :] = heads[ACT : ACT + 24, :]


def critic_head(flat, rows, eye, forward, bias, back, use_mean_row=None):
    pieces = yield from unflatten(flat[rows[1] : rows[1] + 8, :] * ROOT_HALF, 2)
    place = selector(16, lambda row, lane: (row == lane) & (row < 2))
    both = nt(block_pair(place), pieces)
    forward[...] = both.astype(BF16)
    bias[...] = column(flat[rows[4] : rows[4] + 1, :])[0:8, :]
    if back is None:
        return
    yield
    spread = [
        jnp.concatenate(
            [jnp.broadcast_to(both[16 * part + k : 16 * part + k + 1, :], (LANES, HID)) for part in (0, 1)],
            axis=1,
        )
        for k in (0, 1)
    ]
    columns = nt(jnp.concatenate([eye, eye], axis=1), jnp.concatenate(spread, axis=0).astype(BF16))
    back[...] = ROOT_TWO * columns
    yield
    use_mean_row(ROOT_TWO * (both[0:1, :] + both[16:17, :]))


def spread_lanes(bias):
    return jnp.concatenate([bias] * (SUB // LANES), axis=1)


def fold(value):
    parts = [value[:, k : k + LANES] for k in range(0, value.shape[1], LANES)]
    total = parts[0]
    for part in parts[1:]:
        total = total + part
    return total


def policy_parts(out, shocks):
    centre = out[0:ACT, :]
    raw = out[24 : 24 + ACT, :]
    soft, slope = softplus_pair(raw)
    spread = soft + 0.05
    pre = centre + spread * shocks
    terms = (
        -0.5 * shocks * shocks
        - jnp.log(spread)
        - HALF_LOG_TWO_PI
        - 2.0 * (LOG_TWO - pre - softplus(-2.0 * pre))
    )
    return jnp.tanh(pre), jnp.sum(terms, axis=0, keepdims=True), spread, slope


def stacked_action(value, pad):
    tall = jnp.concatenate([value, pad], axis=0)
    high, low = split(tall)
    return jnp.concatenate([high, low, high, jnp.zeros_like(high)], axis=0)


def loss_kernel(
    builds, tiles, half, chunk, block,
    meta, log_alpha, obs, nxt, act, misc_wide, noise_own, misc_own,
    own_actor, other_actor, own_critic, other_critic,
    keep, send,
    flat_ta, flat_oa, flat_tc, flat_oc,
    w1_t, w1a, w1c, wa_t, wa_o, wa_back, w2_ta, w2_tc, w2a, w2c, w2a_back, w2c_back, w2q_back,
    bias2, w3_ta, w3_oa, w3_tc, w3_oc, w3a_back, w3c_back, bias3_ta, bias3_oa, bias3_tc, bias3_oc,
    square,
    g1a, g1c, g2a, g2c, g3a, g3c, gb2a, gb2c, gb3a, gb3c, sums, total,
    z1_t, z1_a, z1_c, h1c, h2c, dz1c, dz2c, doc, h1a, h2a, dz1a, dz2a, doa,
    table, got, wide, states_before, states, states_after, nexts_after, aux, aux_after,
    gathered, listed, chosen, count, peaks, done, raw_ta, raw_oa, raw_tc, raw_oc, arrived,
):
    grid_step = pl.program_id(0)
    step = grid_step - builds

    def first_products(rows, next_rows, which=(0, 1, 2)):
        x = rows[...]
        x3 = x[:, 0:384]
        if 0 in which:
            z1_c[...] = nt(w1c[...], jnp.concatenate([x3, x], axis=1))
        if 1 in which:
            z1_a[...] = nt(w1a[...], jnp.concatenate([x3, x3], axis=1))
        if 2 in which:
            z1_t[...] = nt(w1_t[...], next_rows[...])

    def gradients(rows, which=range(6)):
        x = rows[...]
        if 0 in which:
            g2c[...] += nt(h1c[...], dz2c[...])
        if 1 in which:
            g3c[...] += nt(doc[...], h2c[...])
        if 2 in which:
            g1c[...] += nn(dz1c[...], x)
        if 3 in which:
            g2a[...] += nt(h1a[...], dz2a[...])
        if 4 in which:
            g3a[...] += nt(doa[...], h2a[...])
        if 5 in which:
            g1a[...] += nn(dz1a[...], x[:, 0:384])

    raws = (raw_ta, raw_oa, raw_tc, raw_oc)

    def parameter_copies(first):
        sources = (own_actor, other_actor, own_critic, other_critic)
        if not first:
            sources = (other_actor, own_actor, other_critic, own_critic)
        return [
            pltpu.make_async_copy(source, raw, arrived.at[k])
            for k, (source, raw) in enumerate(zip(sources, raws))
        ]

    @pl.when((grid_step == 0) & (meta[0] == 0))
    def _():
        for copy in parameter_copies(True):
            copy.start()

    @pl.when((grid_step == 0) & (meta[0] != 0))
    def _():
        for copy in parameter_copies(False):
            copy.start()

    @pl.when(grid_step == 0)
    def _():
        wide[...] = jnp.zeros_like(wide)
        gathered[...] = jnp.zeros_like(gathered)
        peaks[...] = jnp.zeros_like(peaks)
        listed[...] = jnp.zeros_like(listed)
        count[0] = 0

    @pl.when(grid_step < builds)
    def _():
        build_table(grid_step, block, obs, nxt, act, misc_wide, table, wide)
        choose(half // builds, noise_own, misc_own, listed, gathered, count)
        for k in range(0, half // builds, LANES):
            peaks[0:1, :] = jnp.maximum(peaks[0:1, :], misc_own[MISC_WEIGHT : MISC_WEIGHT + 1, k : k + LANES])

    @pl.when(grid_step == builds - 1)
    def _():
        for copy in parameter_copies(True):
            copy.wait()
        for flat, raw in zip((flat_ta, flat_oa, flat_tc, flat_oc), raws):
            copy_flat(flat, raw)
        copy = pltpu.make_async_copy(listed, chosen, done)
        copy.start()
        eye = square_eye()
        running = [
            actor_head(flat_ta, A_ROWS, w3_ta, bias3_ta, None),
            actor_head(flat_oa, A_ROWS, w3_oa, bias3_oa, w3a_back),
            critic_head(flat_tc, C_ROWS, eye, w3_tc, bias3_tc, None),
            critic_head(
                flat_oc, C_ROWS, eye, w3_oc, bias3_oc, w3c_back,
                lambda row: second_layer(flat_oc, C_ROWS, eye, w2c, w2c_back, w2q_back, row),
            ),
        ]
        flats = ((flat_ta, A_ROWS), (flat_tc, C_ROWS), (flat_oa, A_ROWS), (flat_oc, C_ROWS))
        beside = [
            lambda: first_layer(flat_oc, C_ROWS, eye, w1c, 2, 0),
            lambda: first_layer(flat_oa, A_ROWS, eye, w1a, 2, 0),
            copy.wait,
            lambda: first_layer(flat_ta, A_ROWS, eye, w1_t, 1, 0),
            lambda: first_layer(flat_tc, C_ROWS, eye, w1_t, 1, HID),
            lambda: action_layer(flat_oc, eye, square, wa_o, w1c, wa_back),
            lambda: action_layer(flat_tc, eye, square, wa_t, None, None),
            lambda: second_layer(flat_oa, A_ROWS, eye, w2a, w2a_back),
            lambda: second_layer(flat_ta, A_ROWS, eye, w2_ta, None),
            lambda: second_layer(flat_tc, C_ROWS, eye, w2_tc, None),
            lambda: second_biases(flats, eye, bias2),
        ]
        zeros = [g1a, g1c, g2a, g2c, g3a, g3c, gb2a, gb2c, gb3a, gb3c, sums]
        zeros += [h1c, h2c, dz1c, dz2c, doc, h1a, h2a, dz1a, dz2a, doa]
        fetched = 0
        while running or beside:
            running = [piece for piece in running if next(piece, True) is None]
            if beside:
                task = beside.pop(0)
                task()
                waited = task == copy.wait or fetched > 0
            for ref in zeros[:2]:
                ref[...] = jnp.zeros_like(ref)
            zeros = zeros[2:]
            if waited and fetched < TILE:
                fetch_rows(chosen, 0, table, got, fetched, fetched + 64)
                fetched += 64
        for ref in zeros:
            ref[...] = jnp.zeros_like(ref)
        fetch_rows(chosen, 0, table, got, fetched, TILE)
        turn_rows(got, states, nexts_after, aux)
        first_products(states, nexts_after)
        states_before[...] = states[...]

    @pl.when((grid_step >= builds) & (step * TILE < count[0]))
    def _():
        alpha = jnp.exp(jnp.full((1, SUB), log_alpha[0], F32))
        col0 = spread_lanes(w3c_back[:, 0:LANES])
        col1 = spread_lanes(w3c_back[:, LANES : 2 * LANES])
        pad = jnp.zeros((32 - ACT, SUB), F32)
        gap = jnp.zeros((24 - ACT, SUB), F32)
        row16 = lax.broadcasted_iota(jnp.int32, (16, SUB), 0)

        def head(weights, hidden, bias, size):
            tick()
            both = nn(weights[...], hidden)
            return both[0:size, :] + both[size : 2 * size, :] + spread_lanes(bias)

        def tick():
            task = beside.pop(0) if beside else None
            if task is not None:
                task()

        def gelu_t(t):
            tick()
            return gelu(t)

        def pair_t(t):
            tick()
            return gelu_pair(t)

        def nn_t(left, right):
            tick()
            return nn(left, right)

        def part(sub):
            lanes = slice(sub * SUB, (sub + 1) * SUB)
            per = SUB // LANES
            blocks = [gathered[step * (TILE // LANES) + sub * per + k] for k in range(per)]
            own = jnp.concatenate(blocks, axis=1)
            noise = own[0 : 2 * ACT + 1, :]
            place = step * TILE + sub * SUB + lax.broadcasted_iota(jnp.int32, (1, SUB), 1)
            counted = (place < count[0]).astype(F32)
            importance = own[OWN_WEIGHT + MISC_WEIGHT : OWN_WEIGHT + MISC_WEIGHT + 1, :]
            weight = counted * importance
            h1 = gelu_t(z1_t[0:HID, lanes])
            z2_t = nn_t(w2_ta[...], h1) + spread_lanes(bias2[:, 0 * LANES : 1 * LANES])
            hidden_a, s1a = pair_t(z1_a[:, lanes])
            z2_a = nn_t(w2a[...], twice(hidden_a)) + spread_lanes(bias2[:, 2 * LANES : 3 * LANES])
            hidden_c, s1c = pair_t(z1_c[:, lanes])
            z2_c = nn_t(w2c[...], twice(hidden_c)) + spread_lanes(bias2[:, 3 * LANES : 4 * LANES])
            yield
            h2 = gelu_t(z2_t)
            out = head(w3_ta, h2, bias3_ta[...], 48)
            last_a, s2a = pair_t(z2_a)
            out_a = head(w3_oa, last_a, bias3_oa[...], 48)
            last_c, s2c = pair_t(z2_c)
            both = nn_t(w3_oc[...], last_c)
            out_c = both[0:8, :] + both[16:24, :] + spread_lanes(bias3_oc[...])
            yield
            next_action, next_logp, _, _ = policy_parts(out, noise[0:ACT, :])
            z1_n = z1_t[HID:, lanes] + nn_t(wa_t[...], stacked_action(next_action, pad))
            shocks = noise[ACT : 2 * ACT, :]
            action, logp, spread_a, slope_a = policy_parts(out_a, shocks)
            old_action = aux[0:ACT, lanes] + aux[AUX_LOW : AUX_LOW + ACT, lanes]
            z1_q = z1_c[:, lanes] + nn_t(wa_o[...], stacked_action(action - old_action, pad))
            yield
            h1 = gelu_t(z1_n)
            z2_n = nn_t(w2_tc[...], h1) + spread_lanes(bias2[:, 1 * LANES : 2 * LANES])
            h1q, s1q = pair_t(z1_q)
            z2_q = nn_t(w2c[...], twice(h1q)) + spread_lanes(bias2[:, 3 * LANES : 4 * LANES])
            yield
            h2 = gelu_t(z2_n)
            both = nn_t(w3_tc[...], h2)
            out_t = both[0:8, :] + both[16:24, :] + spread_lanes(bias3_tc[...])
            h2q, s2q = pair_t(z2_q)
            both = nn_t(w3_oc[...], h2q)
            value_now = both[0:1, :] + both[16:17, :] + spread_lanes(bias3_oc[0:1, :])
            dz1q = nn_t(w2q_back[...], twice(s2q.astype(BF16))) * s1q
            yield
            both = nn_t(wa_back[...], dz1q.astype(BF16))
            value_back = both[0:ACT, :] + both[32 : 32 + ACT, :]
            next_spread = softplus(out_t[1:2, :]) + 0.1
            reward = aux[AUX_REWARD : AUX_REWARD + 1, lanes]
            goal = reward + DISCOUNT * (
                out_t[0:1, :] + next_spread * noise[2 * ACT : 2 * ACT + 1, :] - alpha * next_logp
            )
            q_value = out_c[0:1, :]
            soft, slope = softplus_pair(out_c[1:2, :])
            spread = soft + 0.1
            inverse = 1.0 / spread
            square_inverse = inverse * inverse
            miss = goal - q_value
            bound = jnp.minimum(jnp.maximum(miss, -3.0 * spread), 3.0 * spread)
            critic_loss = weight * (
                0.5 * miss * miss * square_inverse
                + 0.5 * bound * bound * square_inverse
                + jnp.log(spread)
            )
            mean_back = -weight * miss * square_inverse
            spread_back = weight * (1.0 - bound * bound * square_inverse) * inverse * slope
            dz2 = (col0 * mean_back + col1 * spread_back) * s2c
            back = dz2.astype(BF16)
            gb2c[...] += fold(dz2)
            dz1 = nn_t(w2c_back[...], twice(back)) * s1c
            do_c = jnp.where(
                row16 == 0,
                jnp.broadcast_to(mean_back, (16, SUB)),
                jnp.where(row16 == 1, jnp.broadcast_to(spread_back, (16, SUB)), 0.0),
            )
            gb3c[...] += fold(do_c)
            dz2c[:, lanes] = back
            dz1c[:, lanes] = dz1.astype(BF16)
            doc[:, lanes] = do_c.astype(BF16)
            h1c[:, lanes] = hidden_c
            h2c[:, lanes] = last_c
            yield
            counted_alpha = counted * alpha
            d_pre = counted_alpha * 2.0 * action - counted * value_back * (1.0 - action * action)
            d_raw = (d_pre * shocks - counted_alpha / spread_a) * slope_a
            do_a = jnp.concatenate([d_pre, gap, d_raw, gap], axis=0)
            high, low = split(ROOT_TWO * do_a)
            dz2 = nn_t(w3a_back[...], jnp.concatenate([high, low, high], axis=0)) * s2a
            back = dz2.astype(BF16)
            gb2a[...] += fold(dz2)
            gb3a[...] += fold(do_a)
            sums[0:1, :] += fold(counted)
            sums[1:2, :] += fold(counted * logp)
            sums[2:3, :] += fold(critic_loss)
            sums[3:4, :] += fold(counted * (alpha * logp - value_now))
            yield
            dz1 = nn_t(w2a_back[...], twice(back)) * s1a
            dz2a[:, lanes] = back
            dz1a[:, lanes] = dz1.astype(BF16)
            doa[:, lanes] = high
            h1a[:, lanes] = hidden_a
            h2a[:, lanes] = last_a

        first_pick = jnp.minimum(step + 1, tiles - 1) * (TILE // LANES)

        fetches = [
            lambda k=k: fetch_rows(chosen, first_pick, table, got, k, k + 16)
            for k in range(0, TILE, 16)
        ]
        sums_before = [
            lambda which=which: gradients(states_before, (which,)) for which in range(6)
        ]
        products_after = [
            lambda: turn_rows(got, states_after, nexts_after, aux_after),
            lambda: first_products(states_after, nexts_after, (0,)),
            lambda: first_products(states_after, nexts_after, (1,)),
            lambda: first_products(states_after, nexts_after, (2,)),
        ]
        beside = []
        for k, fetch in enumerate(fetches):
            beside.append(fetch)
            if k % 5 == 2 and sums_before:
                beside.append(sums_before.pop(0))
        for product in products_after:
            beside += [product, None, None, None, None]

        running = [part(sub) for sub in range(TILE // SUB)]
        while running:
            running = [piece for piece in running if next(piece, True) is None]
        while beside:
            tick()
        states_before[...] = states[...]
        states[...] = states_after[...]
        aux[...] = aux_after[...]

    @pl.when(step == tiles - 1)
    def _():
        gradients(states_before)
        total[...] = jnp.zeros_like(total)

        def sum_row(block):
            return jnp.sum(block.T, axis=0, keepdims=True)

        for side in (0, 1):
            at = side * LANES
            turned = 0.5 * g1a[at : at + LANES, :].T
            total[A_W1[side] : A_W1[side] + OBS, :] = turned[0:OBS, :]
            total[A_B + side : A_B + side + 1, :] = turned[ONE_LANE : ONE_LANE + 1, :]
            total[A_W2[side] : A_W2[side] + HID, :] = (0.5 * ROOT_HALF) * g2a[:, at : at + LANES]
            total[A_W3[side] : A_W3[side] + ACT, :] = 0.5 * g3a[0:ACT, at : at + LANES]
            total[A_W3[side] + ACT : A_W3[side] + 2 * ACT, :] = (
                0.5 * g3a[24 : 24 + ACT, at : at + LANES]
            )
            total[A_B + 2 + side : A_B + 3 + side, :] = 0.5 * sum_row(gb2a[at : at + LANES, :])
            turned = 0.5 * g1c[at : at + LANES, :].T
            total[C_W1[side] : C_W1[side] + OBS, :] = turned[0:OBS, :]
            total[C_W1[side] + OBS : C_W1[side] + OBS + ACT, :] = (
                turned[384 : 384 + ACT, :] + turned[384 + AUX_LOW : 384 + AUX_LOW + ACT, :]
            )
            total[C_B + side : C_B + side + 1, :] = turned[ONE_LANE : ONE_LANE + 1, :]
            total[C_W2[side] : C_W2[side] + HID, :] = (0.5 * ROOT_HALF) * g2c[:, at : at + LANES]
            total[C_W3[side] : C_W3[side] + 2, :] = ROOT_HALF * g3c[0:2, at : at + LANES]
            total[C_B + 2 + side : C_B + 3 + side, :] = 0.5 * sum_row(gb2c[at : at + LANES, :])
        none = jnp.zeros((LANES - 2 * ACT, LANES), F32)
        total[A_B + 4 : A_B + 5, :] = sum_row(
            jnp.concatenate([gb3a[0:ACT, :], gb3a[24 : 24 + ACT, :], none], axis=0)
        )
        none = jnp.zeros((LANES - 16, LANES), F32)
        total[C_B + 4 : C_B + 5, :] = sum_row(jnp.concatenate([gb3c[...], none], axis=0))
        total[EXTRA : EXTRA + 4, :] = sums[0:4, :]
        peak = jnp.max(peaks[0:1, :], axis=1, keepdims=True)
        for k in range(EXTRA + 8 - EXTRA_SLOTS):
            total[EXTRA_SLOTS + k : EXTRA_SLOTS + k + 1, :] = jnp.where(
                lanes_of(1) + k * LANES == meta[1], jnp.broadcast_to(peak, (1, LANES)), 0.0
            )
        count = keep.shape[0] // chunk
        for p in range(count):
            at = pl.multiple_of((meta[1] ^ p) * chunk, 8)
            keep[p * chunk : (p + 1) * chunk, :] = total[pl.ds(at, chunk), :]
            at = pl.multiple_of((meta[2] ^ p) * chunk, 8)
            send[p * chunk : (p + 1) * chunk, :] = total[pl.ds(at, chunk), :]


def losses(
    meta, log_alpha, obs, nxt, act, noise, misc, own_a, other_a, own_c, other_c, devices
):
    rows = obs.shape[1]
    half = noise.shape[1] // 2
    tiles = -(-half // TILE)
    block = next(size for size in (1280, 640, 512, 256, 128) if rows % size == 0)
    builds = rows // block
    own = half // builds
    list_rows = -(-(tiles * (TILE // LANES) + 1) // 8) * 8
    chunk = chunk_rows(devices)
    buffer_rows = chunk * devices

    def fixed(i, meta):
        return (0, 0)

    def source(i, meta):
        return (0, jnp.minimum(i, builds - 1))

    def own_source(i, meta):
        return (0, meta[0] * builds + jnp.minimum(i, builds - 1))

    def body(*refs):
        loss_kernel(builds, tiles, half, chunk, block, *refs)

    def bf(*shape):
        return pltpu.VMEM(shape, BF16)

    def f32(*shape):
        return pltpu.VMEM(shape, F32)

    features = noise.shape[0]
    return pl.pallas_call(
        body,
        out_shape=(
            jax.ShapeDtypeStruct((buffer_rows // 2, LANES), F32),
            jax.ShapeDtypeStruct((buffer_rows // 2, LANES), F32),
        ),
        grid_spec=pltpu.PrefetchScalarGridSpec(
            num_scalar_prefetch=1,
            grid=(builds + tiles,),
            in_specs=[
                pl.BlockSpec(memory_space=pltpu.SMEM),
                pl.BlockSpec((OBS, block), source),
                pl.BlockSpec((OBS, block), source),
                pl.BlockSpec((ACT, block), source),
                pl.BlockSpec((8, block), source),
                pl.BlockSpec((features, own), own_source),
                pl.BlockSpec((8, own), own_source),
                pl.BlockSpec(memory_space=pl.ANY),
                pl.BlockSpec(memory_space=pl.ANY),
                pl.BlockSpec(memory_space=pl.ANY),
                pl.BlockSpec(memory_space=pl.ANY),
            ],
            out_specs=(
                pl.BlockSpec((buffer_rows // 2, LANES), fixed),
                pl.BlockSpec((buffer_rows // 2, LANES), fixed),
            ),
            scratch_shapes=[
                f32(A_FLAT, LANES), f32(A_FLAT, LANES), f32(C_FLAT, LANES), f32(C_FLAT, LANES),
                bf(512, 384), bf(HID, 768), bf(HID, 896),
                bf(HID, LANES), bf(HID, LANES), bf(64, HID),
                bf(HID, HID), bf(HID, HID),
                bf(HID, 512), bf(HID, 512), bf(HID, 512), bf(HID, 512), bf(HID, 512),
                f32(HID, 4 * LANES), bf(96, HID), bf(96, HID), bf(32, HID), bf(32, HID),
                bf(HID, 144), f32(HID, 2 * LANES),
                f32(48, LANES), f32(48, LANES), f32(8, LANES), f32(8, LANES),
                f32(32, HID),
                f32(HID, 384), f32(HID, 512), f32(HID, HID), f32(HID, HID),
                f32(48, HID), f32(16, HID), f32(HID, LANES), f32(HID, LANES),
                f32(48, LANES), f32(16, LANES), f32(8, LANES), f32(buffer_rows, LANES),
                f32(2 * HID, TILE), f32(HID, TILE), f32(HID, TILE),
                bf(HID, TILE), bf(HID, TILE), bf(HID, TILE), bf(HID, TILE), bf(16, TILE),
                bf(HID, TILE), bf(HID, TILE), bf(HID, TILE), bf(HID, TILE), bf(48, TILE),
                f32((rows + 8) * CHUNKS, LANES), f32(TILE * 8, LANES), f32(LANES, block),
                bf(TILE, 512), bf(TILE, 512), bf(TILE, 512), bf(TILE, 384),
                f32(AUX_ROWS, TILE), f32(AUX_ROWS, TILE),
                f32(list_rows, OWN_ROWS, LANES),
                pltpu.VMEM((list_rows, LANES), jnp.int32),
                pltpu.SMEM((list_rows, LANES), jnp.int32),
                pltpu.SMEM((1,), jnp.int32), f32(8, LANES), pltpu.SemaphoreType.DMA,
                f32(1, A_SIZE), f32(1, A_SIZE), f32(1, C_SIZE), f32(1, C_SIZE),
                pltpu.SemaphoreType.DMA((4,)),
            ],
        ),
        compiler_params=pltpu.CompilerParams(
            dimension_semantics=("arbitrary",), vmem_limit_bytes=VMEM_BYTES
        ),
        name="losses",
    )(meta, log_alpha, obs, nxt, act, misc, noise, misc, own_a, other_a, own_c, other_c)


def stat_pieces(width_in, width_out):
    sizes = [width_in, HID, HID, HID, HID, width_out, HID, HID, width_out]
    starts = [sum(sizes[:k]) for k in range(len(sizes))]
    rows = [-(-size // LANES) for size in sizes]
    return sizes, starts, [sum(rows[:k]) for k in range(len(rows))], sum(rows)


def aligned_stats(statistics, width_in, width_out):
    sizes, starts, _, rows = stat_pieces(width_in, width_out)
    pieces = [
        jnp.pad(statistics[start : start + size], (0, -size % LANES))
        for size, start in zip(sizes, starts)
    ]
    pieces.append(jnp.zeros((-rows % 8 * LANES,), F32))
    return jnp.concatenate(pieces).reshape(-1, LANES)


def blend(old, new):
    return DECAY_RATE * old + (1.0 - DECAY_RATE) * new


def clip_scale(square_sum, number):
    return 1.0 / jnp.maximum(1.0, jnp.sqrt(square_sum / number) / CLIP_LEVEL)


def whole_sum(value):
    return jnp.sum(jnp.sum(value, axis=0, keepdims=True), axis=1, keepdims=True)


def large_layers(total, scale, old_row, width_in, places, rows, fg, fu, lines):
    for layer, (height, flat_at) in enumerate(((width_in, 0), (HID, rows[0]))):
        parts = [total[at : at + height, :] * scale for at in places[layer]]
        squares = [g * g + TINY_TERM for g in parts]
        yield
        blocks = -(-height // LANES)
        old = jnp.concatenate([column(old_row(layer, k)) for k in range(blocks)], axis=0)
        old = old[0:height, :]
        mean = jnp.sum(squares[0] + squares[1], axis=1, keepdims=True) * (1.0 / HID)
        row_stat = blend(old, jnp.broadcast_to(mean, (height, LANES)))
        yield
        for k in range(blocks):
            block = row_stat[k * LANES : min(height, (k + 1) * LANES), :]
            if block.shape[0] < LANES:
                block = jnp.concatenate(
                    [block, jnp.zeros((LANES - block.shape[0], LANES), F32)], axis=0
                )
            lines[layer].append(block.T[0:1, :])
        mean_row = jnp.sum(row_stat, axis=0, keepdims=True) * (1.0 / height)
        row_root = lax.rsqrt(row_stat)
        yield
        steps = []
        square_sum = 0.0
        for side in (0, 1):
            col_stat = blend(
                old_row(3 + layer, side),
                jnp.sum(squares[side], axis=0, keepdims=True) * (1.0 / height),
            )
            lines[3 + layer].append(col_stat)
            step = (parts[side] * row_root) * (lax.rsqrt(col_stat) * jnp.sqrt(mean_row))
            square_sum = square_sum + jnp.sum(step * step, axis=0, keepdims=True)
            steps.append(step)
            fg[pl.ds(flat_at + side, height, stride=2), :] = parts[side]
            yield
        square_sum = jnp.sum(square_sum, axis=1, keepdims=True)
        factor = clip_scale(square_sum, float(height * HID))
        for side in (0, 1):
            fu[pl.ds(flat_at + side, height, stride=2), :] = steps[side] * factor
            yield


def last_layer(total, scale, old_row, width_out, place, rows, fg, fu, lines):
    tall = -(-width_out // 8) * 8
    parts = [total[at : at + tall, :] * scale for at in place]
    real = rows_of(tall) < width_out
    squares = [jnp.where(real, g * g + TINY_TERM, 0.0) for g in parts]
    old = column(old_row(5, 0))[0:tall, :]
    mean = jnp.sum(squares[0] + squares[1], axis=1, keepdims=True) * (1.0 / HID)
    col_stat = blend(old, jnp.broadcast_to(mean, (tall, LANES)))
    pad = jnp.zeros((LANES - tall, LANES), F32)
    lines[5].append(jnp.concatenate([col_stat, pad], axis=0).T[0:1, :])
    yield
    row_stats = []
    for side in (0, 1):
        row_stats.append(
            blend(
                old_row(2, side),
                jnp.sum(squares[side], axis=0, keepdims=True) * (1.0 / width_out),
            )
        )
        lines[2].append(row_stats[side])
    mean_row = jnp.sum(row_stats[0] + row_stats[1], axis=1, keepdims=True) * (1.0 / HID)
    col_root = jnp.where(real, lax.rsqrt(col_stat), 0.0)
    steps = [
        (parts[side] * lax.rsqrt(row_stats[side])) * (col_root * jnp.sqrt(mean_row))
        for side in (0, 1)
    ]
    factor = clip_scale(
        whole_sum(steps[0] * steps[0] + steps[1] * steps[1]), float(HID * width_out)
    )
    yield
    size = rows[2] - rows[1]
    turned = [
        jnp.concatenate(
            [jnp.concatenate([jnp.where(real, part, 0.0), pad], axis=0).T for part in pair], axis=0
        )
        for pair in (parts, [u * factor for u in steps])
    ]
    yield
    flat_parts = yield from flatten(turned, width_out, -(-size // 8) * 8)
    for flat, part in zip((fg, fu), flat_parts):
        flat[rows[1] : rows[1] + size, :] = part[0:size, :]


def biases(total, scale, old, width_out, bias_at, rows, fg, fu, lines):
    grad = total[bias_at : bias_at + 8, :] * scale
    line = rows_of(8)
    lane = lanes_of(8)
    real = (line < 4) | ((line == 4) & (lane < width_out))
    grad = jnp.where(real, grad, 0.0)
    stat = blend(old, grad[0:5, :] * grad[0:5, :] + TINY_TERM)
    step = jnp.where(real[0:5, :], grad[0:5, :] * lax.rsqrt(stat), 0.0)
    yield
    factor = clip_scale(whole_sum(step * step), float(2 * HID + width_out))
    fg[rows[2] : rows[2] + 5, :] = grad[0:5, :]
    fu[rows[2] : rows[2] + 5, :] = step * factor
    for k in range(5):
        lines[6 + k // 2].append(stat[k : k + 1, :])


def store_statistics(lines, width_in, width_out, stats_out):
    sizes, starts, _, _ = stat_pieces(width_in, width_out)
    size = stats_out.shape[0]
    count = -(-size // LANES)
    made = [jnp.zeros((1, LANES), F32) for _ in range(count + 1)]
    lane = lanes_of(1)
    for piece, pieces in enumerate(lines):
        for k, value in enumerate(pieces):
            start = starts[piece] + k * LANES
            width = min(LANES, sizes[piece] - k * LANES)
            value = jnp.where(lane < width, value, 0.0)
            shift = start % LANES
            at = start // LANES
            if shift:
                value = pltpu.roll(value, shift, 1)
            made[at] = made[at] + jnp.where(lane >= shift, value, 0.0)
            if shift:
                made[at + 1] = made[at + 1] + jnp.where(lane < shift, value, 0.0)
    for k in range(count):
        width = min(LANES, size - k * LANES)
        stats_out[pl.ds(k * LANES, width)] = made[k][:, 0:width].reshape(width)


def in_turn(stages):
    while stages:
        stages = [stage for stage in stages if next(stage, True) is None]


def net_update(total, scale, old_stats, width_in, width_out, places, rows, fg, fu):
    sizes, _, first, _ = stat_pieces(width_in, width_out)
    lines = [[] for _ in sizes]

    def old_row(piece, k):
        return old_stats[first[piece] + k : first[piece] + k + 1, :]

    old_bias = old_stats[first[6] : first[6] + 5, :]
    large = large_layers(total, scale, old_row, width_in, places, rows, fg, fu, lines)
    small = [
        last_layer(total, scale, old_row, width_out, places[2], rows, fg, fu, lines),
        biases(total, scale, old_bias, width_out, places[3], rows, fg, fu, lines),
    ]
    return large, small, lines


def write_net(side, own, other, fg, fu, slot, copy, grad):
    size = own.shape[1]
    whole = size // 2048

    def piece(at, row, width, count):
        mine = own[0:1, pl.ds(at, width)].reshape(count, width // count)
        theirs = other[0:1, pl.ds(at, width)].reshape(count, width // count)
        wide = width // count
        step = fu[pl.ds(row, count), 0:wide]
        online = jnp.where(side == 0, theirs, mine)
        new = online - LEARN_RATE * step
        held = jnp.where(side == 0, POLYAK_RATE * new + (1.0 - POLYAK_RATE) * mine, new)
        slot[0:1, pl.ds(at, width)] = held.reshape(1, width)
        copy[0:1, pl.ds(at, width)] = held.astype(BF16).reshape(1, width)
        grad[pl.ds(at, width)] = fg[pl.ds(row, count), 0:wide].reshape(width)

    for k in range(whole):
        piece(k * 2048, k * 16, 2048, 16)
    full = size // LANES
    for row in range(whole * 16, full):
        piece(row * LANES, row, LANES, 1)
    piece(full * LANES, full, size - full * LANES, 1)


def update_kernel(
    chunk, devices,
    meta, log_alpha, mine, theirs, own_a, other_a, own_c, other_c, stats_a, stats_c,
    slot_a, slot_c, copy_a, copy_c, grad_a, grad_c, new_a, new_c, summary, alpha_out,
    total, fg_a, fu_a, fg_c, fu_c,
):
    count = devices // 2
    for p in range(count):
        at = pl.multiple_of((meta[1] ^ p) * chunk, 8)
        total[pl.ds(at, chunk), :] = mine[p * chunk : (p + 1) * chunk, :]
        at = pl.multiple_of((meta[2] ^ p) * chunk, 8)
        total[pl.ds(at, chunk), :] = theirs[p * chunk : (p + 1) * chunk, :]

    sums = jnp.sum(total[EXTRA : EXTRA + 8, :], axis=1, keepdims=True)
    peak = jnp.max(total[EXTRA_SLOTS : EXTRA + 8, :], axis=1, keepdims=True)
    peak = jnp.max(peak, axis=0, keepdims=True)
    counted = sums[0:1, :]
    scale_a = 1.0 / counted
    scale_c = scale_a / peak
    lane = lanes_of(1)
    line = jnp.where(
        lane == 0,
        jnp.broadcast_to(sums[2:3, :] / peak, (1, LANES)),
        jnp.where(
            lane == 1,
            jnp.broadcast_to(sums[3:4, :], (1, LANES)),
            jnp.broadcast_to(counted, (1, LANES)),
        ),
    )
    summary[...] = line[:, 0:3].reshape(3)
    new_alpha = log_alpha[0] + ALPHA_STEP * (
        jnp.broadcast_to(sums[1:2, :] / counted, (1, LANES)) - ACT
    )
    alpha_out[...] = new_alpha[:, 0:1].reshape(1)
    large_a, small_a, lines_a = net_update(
        total, scale_a, stats_a, OBS, 2 * ACT, (A_W1, A_W2, A_W3, A_B), A_ROWS, fg_a, fu_a
    )
    large_c, small_c, lines_c = net_update(
        total, scale_c, stats_c, OBS + ACT, 2, (C_W1, C_W2, C_W3, C_B), C_ROWS, fg_c, fu_c
    )
    in_turn([large_a] + small_a)
    in_turn([large_c] + small_c)
    store_statistics(lines_a, OBS, 2 * ACT, new_a)
    store_statistics(lines_c, OBS + ACT, 2, new_c)
    write_net(meta[0], own_a, other_a, fg_a, fu_a, slot_a, copy_a, grad_a)
    write_net(meta[0], own_c, other_c, fg_c, fu_c, slot_c, copy_c, grad_c)


def update(meta, log_alpha, mine, theirs, own_a, other_a, own_c, other_c, stats_a, stats_c, sizes, devices):
    chunk = chunk_rows(devices)

    def body(*refs):
        update_kernel(chunk, devices, *refs)

    def f32(*shape):
        return jax.ShapeDtypeStruct(shape, F32)

    smem = pl.BlockSpec(memory_space=pltpu.SMEM)
    vmem = pl.BlockSpec(memory_space=pltpu.VMEM)
    return pl.pallas_call(
        body,
        out_shape=(
            f32(1, A_SIZE), f32(1, C_SIZE),
            jax.ShapeDtypeStruct((1, A_SIZE), BF16), jax.ShapeDtypeStruct((1, C_SIZE), BF16),
            f32(A_SIZE), f32(C_SIZE), f32(sizes[0]), f32(sizes[1]), f32(3), f32(1),
        ),
        in_specs=[smem, smem] + [vmem] * 8,
        out_specs=tuple([vmem] * 10),
        scratch_shapes=[
            pltpu.VMEM((chunk * devices, LANES), F32),
            pltpu.VMEM((A_FLAT, LANES), F32), pltpu.VMEM((A_FLAT, LANES), F32),
            pltpu.VMEM((C_FLAT, LANES), F32), pltpu.VMEM((C_FLAT, LANES), F32),
        ],
        compiler_params=pltpu.CompilerParams(vmem_limit_bytes=UPDATE_VMEM_BYTES),
        name="optimizer",
    )(meta, log_alpha, mine, theirs, own_a, other_a, own_c, other_c, stats_a, stats_c)


def chunk_rows(devices):
    return -(-DATA_ROWS // (8 * devices)) * 8


def stage_bits(count, group):
    number = count.bit_length() - 1
    bits = [(bit + 2 * group) % number for bit in range(number)]
    return [bits[k : k + 2] for k in range(0, number, 2)]


def swap_groups(value):
    return lax.ppermute(value, "grp", [(0, 1), (1, 0)])


def exchange(value, stage, digit):
    count = lax.axis_size("dp")
    pairs = []
    for group in (0, 1):
        bits = stage_bits(count, group)[stage]
        mask = sum(1 << bit for k, bit in enumerate(bits) if digit >> k & 1)
        pairs += [(group * count + i, group * count + (i ^ mask)) for i in range(count)]
    return lax.ppermute(value, ("grp", "dp"), pairs)


def buffer_place(group, count):
    index = lax.axis_index("dp")
    place = group
    for bits in stage_bits(count, group):
        for bit in reversed(bits):
            place = place * 2 + (index >> bit & 1)
    return place


def all_sum(keep, send):
    count = lax.axis_size("dp")
    sizes = [1 << len(bits) for bits in stage_bits(count, 0)]
    value = keep + swap_groups(send)
    for stage, size in enumerate(sizes):
        rows = value.shape[0] // size
        parts = [value[k * rows : (k + 1) * rows] for k in range(size)]
        came = [exchange(parts[k], stage, k) for k in range(1, size)]
        value = parts[0]
        for part in came:
            value = value + part
    for stage, size in reversed(list(enumerate(sizes))):
        value = jnp.concatenate(
            [value] + [exchange(value, stage, k) for k in range(1, size)], axis=0
        )
    return value, swap_groups(value)


def shards(
    obs_rows,
    next_rows,
    action_rows,
    reward_rows,
    batch_index,
    valid_mask,
    noise,
    importance,
    actor_params,
    critic_params,
    actor_stats,
    critic_stats,
    log_alpha,
):
    devices = lax.axis_size("dp") * lax.axis_size("grp")
    group_side = lax.axis_index("grp")
    other_a = swap_groups(actor_params)
    other_c = swap_groups(critic_params)
    places = [buffer_place(group, lax.axis_size("dp")) for group in (0, 1)]
    number = jnp.arange(3)
    meta = jnp.where((number == 1) == (group_side == 0), places[0], places[1])
    meta = jnp.where(number == 0, group_side, meta).astype(jnp.int32)
    row = lax.broadcasted_iota(jnp.int32, (8, batch_index.shape[0]), 0)
    misc = jnp.where(row == MISC_VALID, valid_mask[None], batch_index[None]).astype(F32)
    misc = jnp.where(row == MISC_WEIGHT, importance[None], misc)
    misc = jnp.where(row == 0, reward_rows[None], misc)
    keep, send = losses(
        meta, log_alpha, obs_rows.T, next_rows.T, action_rows.T, noise.T, misc,
        actor_params, other_a, critic_params, other_c, devices,
    )
    keep, send, actor_stats, critic_stats = lax.optimization_barrier(
        (keep, send, actor_stats, critic_stats)
    )
    mine, theirs = all_sum(keep, send)
    (
        slot_a, slot_c, copy_a, copy_c, grad_a, grad_c, new_a, new_c, summary, alpha
    ) = update(
        meta, log_alpha, mine, theirs, actor_params, other_a, critic_params, other_c,
        aligned_stats(actor_stats, OBS, 2 * ACT), aligned_stats(critic_stats, OBS + ACT, 2),
        (actor_stats.shape[0], critic_stats.shape[0]), devices,
    )
    return (
        slot_a, slot_c, copy_a, copy_c, grad_a, grad_c, new_a, new_c,
        summary, alpha,
    )


def solution(mesh):
    return jax.shard_map(
        shards,
        mesh=mesh,
        in_specs=(
            P("dp", None),
            P("dp", None),
            P("dp", None),
            P("dp"),
            P("dp"),
            P("dp"),
            P("dp", None),
            P("dp"),
            P("grp", None),
            P("grp", None),
            P(),
            P(),
            P(),
        ),
        out_specs=(
            P("grp", None),
            P("grp", None),
            P("grp", None),
            P("grp", None),
            P(),
            P(),
            P(),
            P(),
            P(),
            P(),
        ),
        check_vma=False,
    )
```

```python
import jax
import jax.numpy as jnp
from jax import lax
from jax.experimental import pallas as pl
from jax.experimental.pallas import tpu as pltpu
from jax.sharding import PartitionSpec as P

OBS = 376
ACT = 17
HID = 256
LANES = 128
TILE = 512
SUB = 256

DISCOUNT = 0.99
POLYAK_RATE = 0.1
DECAY_RATE = 0.5
LEARN_RATE = 0.1
CLIP_LEVEL = 0.1
ALPHA_STEP = 0.01
TINY_TERM = 1e-30
HALF_LOG_TWO_PI = 0.9189385332046727
LOG_TWO = 0.6931471805599453
ROOT_HALF = 0.7071067811865476
ROOT_TWO = 1.4142135623730951
LOG2_E = 1.4426950408889634
LOG2_TWO_OVER_ROOT_PI = 0.17425193548825

F32 = jnp.float32
BF16 = jnp.bfloat16
VMEM_BYTES = 57 * 2**20
UPDATE_VMEM_BYTES = 24 * 2**20

ONE_LANE = OBS
AUX_LOW = 32
AUX_REWARD = 64
AUX_AGAIN = 96
AUX_ROWS = 72
CHUNKS = 7
OWN_WEIGHT = 40
OWN_ROWS = 48
MISC_WEIGHT = 1
MISC_VALID = 2
MISC_INDEX = 3


def flat_rows(width_in, width_out):
    w2 = width_in * HID // LANES
    w3 = w2 + HID * HID // LANES
    b1 = w3 + HID * width_out // LANES
    return w2, w3, b1, b1 + 2, b1 + 4


A_ROWS = flat_rows(OBS, 2 * ACT)
C_ROWS = flat_rows(OBS + ACT, 2)
A_SIZE = A_ROWS[4] * LANES + 2 * ACT
C_SIZE = C_ROWS[4] * LANES + 2
A_FLAT = -(-A_SIZE // 1024) * 8
C_FLAT = -(-C_SIZE // 1024) * 8

A_W1 = (0, OBS)
A_W2 = (2 * OBS, 2 * OBS + HID)
A_W3 = (2 * OBS + 2 * HID, 2 * OBS + 2 * HID + 40)
A_B = A_W3[1] + 40
C_W1 = (A_B + 8, A_B + 8 + 400)
C_W2 = (C_W1[1] + 400, C_W1[1] + 400 + HID)
C_W3 = (C_W2[1] + HID, C_W2[1] + HID + 8)
C_B = C_W3[1] + 8
EXTRA = C_B + 8
EXTRA_SLOTS = EXTRA + 4
DATA_ROWS = EXTRA + 8


def nn(left, right):
    return lax.dot_general(
        left, right, (((1,), (0,)), ((), ())), preferred_element_type=F32
    )


def nt(left, right):
    return lax.dot_general(
        left, right, (((1,), (1,)), ((), ())), preferred_element_type=F32
    )


def split(value):
    high = value.astype(BF16)
    return high, (value - high.astype(F32)).astype(BF16)


def twice(value):
    return jnp.concatenate([value, value], axis=0)


def gelu(t):
    return (t * (1.0 + lax.erf(t))).astype(BF16)


def gelu_pair(t):
    double_cdf = 1.0 + lax.erf(t)
    bell = jnp.exp2(LOG2_TWO_OVER_ROOT_PI - LOG2_E * (t * t))
    return (t * double_cdf).astype(BF16), double_cdf + t * bell


def softplus(x):
    return jnp.maximum(x, 0.0) + jnp.log(1.0 + jnp.exp(-jnp.abs(x)))


def softplus_pair(x):
    decay = jnp.exp(-jnp.abs(x))
    inverse = 1.0 / (1.0 + decay)
    return jnp.maximum(x, 0.0) + jnp.log(1.0 + decay), jnp.where(x >= 0.0, inverse, decay * inverse)


def column(row):
    return jnp.broadcast_to(row, (LANES, LANES)).T


def rows_of(count):
    return lax.broadcasted_iota(jnp.int32, (count, LANES), 0)


def lanes_of(count):
    return lax.broadcasted_iota(jnp.int32, (count, LANES), 1)


def square_eye(reverse=False):
    row = lax.broadcasted_iota(jnp.int32, (HID, HID), 0)
    lane = lax.broadcasted_iota(jnp.int32, (HID, HID), 1)
    return (row == (HID - 1 - lane if reverse else lane)).astype(F32).astype(BF16)


def two_pieces(value):
    return jnp.concatenate(split(value), axis=1)


def turns(value, shift, stride):
    turn = (rows_of(HID) * stride + shift) % LANES
    for step in (2, 4, 8, 16, 32, 64):
        value = jnp.where((turn & step) != 0, pltpu.roll(value, step, 1), value)
        yield value


def unflatten(flat, width):
    rows = flat.shape[0]
    first = (HID - 1 - rows_of(HID)) * width
    lane = lanes_of(HID)
    owner = first // LANES
    picks = jnp.concatenate([(owner == lane), (owner + 1 == lane)], axis=0).astype(F32).astype(BF16)
    found = nn(picks[:, 0:rows], two_pieces(flat))
    yield
    found = found[:, 0:LANES] + found[:, LANES:]
    mixed = jnp.where(lane >= first % LANES, found[0:HID, :], found[HID:, :])
    for turned in turns(mixed, -(HID - 1) * width % LANES, width):
        yield
    pieces = nn(square_eye(True), two_pieces(turned)).astype(BF16)
    yield
    return pieces


def flatten(values, width, rows):
    first = rows_of(HID) * width % LANES
    lane = lanes_of(HID)
    for turned in turns(values[0] + pltpu.roll(values[1], 64, 1), 0, width):
        yield
    swapped = pltpu.roll(turned, 64, 1)
    begun = (lane >= first) & (lane < first + width)
    wrapped = lane < first + width - LANES
    parts = []
    for value in (turned, swapped):
        parts.append(
            jnp.concatenate([jnp.where(begun, value, 0.0), jnp.where(wrapped, value, 0.0)], axis=0)
        )
    both = jnp.concatenate(parts, axis=1)
    high, low = split(both)
    least = (both - high.astype(F32) - low.astype(F32)).astype(BF16)
    owner = lax.broadcasted_iota(jnp.int32, (rows, HID), 1) * width // LANES
    row = lax.broadcasted_iota(jnp.int32, (rows, HID), 0)
    places = jnp.concatenate([owner == row, owner + 1 == row], axis=1).astype(F32).astype(BF16)
    yield
    found = nn(places, jnp.concatenate([high, low, least], axis=1))
    yield
    found = found[:, 0:HID] + found[:, HID : 2 * HID] + found[:, 2 * HID :]
    return found[:, 0:LANES], found[:, LANES:]


def build_table(step, block, obs, nxt, act, misc, table, wide):
    groups = block // 8
    table3 = table.reshape(table.shape[0] // (8 * CHUNKS), 8 * CHUNKS, LANES)
    at = pl.multiple_of(step * groups, groups)

    def put(value, first):
        for c in range(value.shape[1] // LANES):
            table3[pl.ds(at, groups), 8 * (first + c) : 8 * (first + c) + 8, :] = value[
                :, LANES * c : LANES * (c + 1)
            ].reshape(groups, 8, LANES)

    ones = (lax.broadcasted_iota(jnp.int32, (8, block), 0) == 0).astype(F32)
    whole = OBS // 16 * 16

    def padded(source):
        value = source[...]
        rest = jnp.concatenate([value[whole:, :].astype(F32), ones], axis=0).astype(BF16)
        return jnp.concatenate([value[0:whole, :], rest], axis=0)

    value = padded(obs)
    eye = square_eye()
    turned = [nt(eye, value[:, k : k + HID]) for k in range(0, block, HID)]
    put(jnp.concatenate(turned, axis=0), 0)
    put(padded(nxt).T.astype(F32), 3)
    action = act[...]
    high = action.astype(BF16).astype(F32)
    wide[0:ACT, :] = high
    wide[AUX_LOW : AUX_LOW + ACT, :] = action - high
    wide[AUX_AGAIN : AUX_AGAIN + ACT, :] = high
    wide[AUX_REWARD : AUX_REWARD + 8, :] = misc[...]
    put(wide[...].T, 6)


def choose(size, noise, misc, listed, gathered, count):
    lane = lanes_of(1)
    wide_lane = lanes_of(OWN_ROWS)
    parts = size // LANES
    counted = misc[MISC_VALID : MISC_VALID + 1, :]
    flags = [counted[:, LANES * k : LANES * (k + 1)] for k in range(parts)]
    stacked = jnp.concatenate(flags + [jnp.zeros((-parts % 16, LANES), F32)], axis=0).astype(BF16)
    before = nn(stacked, (rows_of(LANES) < lanes_of(LANES)).astype(F32).astype(BF16))
    before = before.astype(jnp.int32)
    index = misc[MISC_INDEX : MISC_INDEX + 1, :].astype(jnp.int32)
    spot = (index >> 3) * (8 * CHUNKS) + (index & 7)
    digits = jnp.concatenate([spot >> 8, spot & 255] + [jnp.zeros_like(spot)] * 14, axis=0)
    gap = jnp.zeros((OWN_WEIGHT - 2 * ACT - 1, size), F32)
    high, low = split(jnp.concatenate([noise[...], gap, misc[...]], axis=0))
    value = jnp.concatenate([digits.astype(F32).astype(BF16), high, low], axis=0)
    place = count[0]
    for k in range(parts):
        where = (before[k : k + 1, :] + place) & (LANES - 1)
        where = jnp.where(flags[k] > 0.0, where, -1)
        hit = (jnp.broadcast_to(where, (LANES, LANES)) == rows_of(LANES)).astype(F32).astype(BF16)
        moved = nt(value[:, LANES * k : LANES * (k + 1)], hit)
        spots = moved[0:2, :].astype(jnp.int32)
        spots = (spots[0:1, :] << 8) + spots[1:2, :]
        values = moved[16 : 16 + OWN_ROWS, :] + moved[16 + OWN_ROWS :, :]
        row = place >> 7
        start = place & (LANES - 1)
        listed[pl.ds(row, 1), :] += jnp.where(lane >= start, spots, 0)
        listed[pl.ds(row + 1, 1), :] += jnp.where(lane >= start, 0, spots)
        gathered[row] += jnp.where(wide_lane >= start, values, 0.0)
        gathered[row + 1] += jnp.where(wide_lane >= start, 0.0, values)
        place = place + jnp.sum(flags[k]).astype(jnp.int32)
    count[0] = place


def fetch_rows(chosen, first, table, got, start, stop, batch=16):
    for base in range(start, stop, batch):
        found = [
            table[pl.ds(chosen[first + j // LANES, j % LANES], 8, stride=8), :]
            for j in range(base, base + batch)
        ]
        for j in range(base, base + batch):
            got[pl.ds((j // 8) * 64 + j % 8, 8, stride=8), :] = found[j - base]


def turn_rows(got, states, nexts, aux):
    got3 = got.reshape(TILE // 8, 64, LANES)

    def chunk(c):
        return got3[:, 8 * c : 8 * c + 8, :].reshape(TILE, LANES)

    for c in range(3):
        states[:, LANES * c : LANES * (c + 1)] = chunk(c).astype(BF16)
        nexts[:, LANES * c : LANES * (c + 1)] = chunk(3 + c).astype(BF16)
    extra = chunk(6)
    states[:, 3 * LANES :] = extra.astype(BF16)
    aux[...] = extra.T[0:AUX_ROWS, :]


def copy_flat(flat, source):
    size = source.shape[1]
    whole = size // 1024

    for k in range(whole):
        flat[8 * k : 8 * k + 8, :] = source[0:1, 1024 * k : 1024 * (k + 1)].reshape(8, LANES)
    flat[8 * whole : 8 * whole + 8, :] = jnp.zeros((8, LANES), F32)
    full = (size - whole * 1024) // LANES
    for k in range(full):
        flat[8 * whole + k : 8 * whole + k + 1, :] = source[
            0:1, whole * 1024 + k * LANES : whole * 1024 + (k + 1) * LANES
        ]
    rest = size - whole * 1024 - full * LANES
    flat[8 * whole + full : 8 * whole + full + 1, 0:rest] = source[0:1, size - rest : size]


def halves(flat, start, height):
    return [flat[pl.ds(start + side, height, stride=2), :] for side in (0, 1)]


def natural(flat, start, height):
    return jnp.concatenate([flat[pl.ds(start + side, height, stride=2), :] for side in (0, 1)], axis=1)


def bias_row(flat, at):
    return jnp.concatenate([flat[at : at + 1, :], flat[at + 1 : at + 2, :]], axis=1)


def first_layer(flat, rows, eye, dst, pieces, base):
    tile = lax.broadcasted_iota(jnp.int32, (8, HID), 0)
    bias = jnp.where(tile == 0, jnp.broadcast_to(bias_row(flat, rows[2]), (8, HID)), 0.0)
    parts = split(jnp.concatenate([natural(flat, 0, OBS), bias], axis=0) * ROOT_HALF)
    for k in range(pieces):
        dst[base : base + HID, 384 * k : 384 * (k + 1)] = nt(eye, parts[k]).astype(BF16)


def action_layer(flat, eye, square, stack, first, back):
    square[0:ACT, :] = natural(flat, 2 * OBS, ACT)
    square[ACT:, :] = jnp.zeros((32 - ACT, HID), F32)
    value = square[...]
    high, low = split(value * ROOT_HALF)
    none = jnp.zeros_like(high)
    stack[...] = nt(eye, jnp.concatenate([high, high, low, none], axis=0)).astype(BF16)
    if first is not None:
        first[:, 768:896] = nt(eye, jnp.concatenate([high, high, none, low], axis=0)).astype(BF16)
        high, low = split(0.5 * value)
        back[0:32, :] = high
        back[32:64, :] = low


def second_layer(flat, rows, eye, forward, back, back_q=None, head=None):
    value = 0.5 * natural(flat, rows[0], HID)
    high, low = split(value)
    forward[:, 0:HID] = nt(eye, high).astype(BF16)
    if back is not None:
        forward[:, HID : 2 * HID] = nt(eye, low).astype(BF16)
        back[:, 0:HID] = high
        back[:, HID : 2 * HID] = low
    if back_q is not None:
        high, low = split(value * head)
        back_q[:, 0:HID] = high
        back_q[:, HID : 2 * HID] = low


def second_biases(flats, eye, bias):
    rows = [
        jnp.broadcast_to(bias_row(flat, rows[3]) * ROOT_HALF, (LANES, HID)) for flat, rows in flats
    ]
    both = jnp.concatenate([two_pieces(row) for row in rows], axis=0)
    bias[...] = nt(jnp.concatenate([eye, eye], axis=1), both)


def selector(rows, chosen):
    return chosen(rows_of(rows), lanes_of(rows)).astype(F32)


def block_pair(value):
    none = jnp.zeros_like(value)
    return jnp.concatenate(
        [jnp.concatenate([value, none], axis=1), jnp.concatenate([none, value], axis=1)], axis=0
    ).astype(BF16)


def actor_place(row, lane):
    return ((row == lane) & (row < ACT)) | ((row - 24 == lane - ACT) & (row >= 24) & (row < 24 + ACT))


def actor_head(flat, rows, forward, bias, back):
    pieces = yield from unflatten(flat[rows[1] : rows[1] + 72, :] * ROOT_HALF, 2 * ACT)
    place = selector(48, actor_place)
    forward[...] = nt(block_pair(place), pieces).astype(BF16)
    if back is not None:
        none = jnp.zeros((48, LANES), F32)
        high = jnp.concatenate([place, none], axis=1)
        low = jnp.concatenate([none, place], axis=1)
        back[...] = nt(pieces, jnp.concatenate([high, high, low], axis=0).astype(BF16)).astype(BF16)
    heads = column(flat[rows[4] : rows[4] + 1, :])
    bias[0:24, :] = heads[0:24, :]
    bias[24:48, :] = heads[ACT : ACT + 24, :]


def critic_head(flat, rows, eye, forward, bias, back, use_mean_row=None):
    pieces = yield from unflatten(flat[rows[1] : rows[1] + 8, :] * ROOT_HALF, 2)
    place = selector(16, lambda row, lane: (row == lane) & (row < 2))
    both = nt(block_pair(place), pieces)
    forward[...] = both.astype(BF16)
    bias[...] = column(flat[rows[4] : rows[4] + 1, :])[0:8, :]
    if back is None:
        return
    yield
    spread = [
        jnp.concatenate(
            [jnp.broadcast_to(both[16 * part + k : 16 * part + k + 1, :], (LANES, HID)) for part in (0, 1)],
            axis=1,
        )
        for k in (0, 1)
    ]
    columns = nt(jnp.concatenate([eye, eye], axis=1), jnp.concatenate(spread, axis=0).astype(BF16))
    back[...] = ROOT_TWO * columns
    yield
    use_mean_row(ROOT_TWO * (both[0:1, :] + both[16:17, :]))


def spread_lanes(bias):
    return jnp.concatenate([bias] * (SUB // LANES), axis=1)


def fold(value):
    parts = [value[:, k : k + LANES] for k in range(0, value.shape[1], LANES)]
    total = parts[0]
    for part in parts[1:]:
        total = total + part
    return total


def policy_parts(out, shocks):
    centre = out[0:ACT, :]
    raw = out[24 : 24 + ACT, :]
    soft, slope = softplus_pair(raw)
    spread = soft + 0.05
    pre = centre + spread * shocks
    terms = (
        -0.5 * shocks * shocks
        - jnp.log(spread)
        - HALF_LOG_TWO_PI
        - 2.0 * (LOG_TWO - pre - softplus(-2.0 * pre))
    )
    return jnp.tanh(pre), jnp.sum(terms, axis=0, keepdims=True), spread, slope


def stacked_action(value, pad):
    tall = jnp.concatenate([value, pad], axis=0)
    high, low = split(tall)
    return jnp.concatenate([high, low, high, jnp.zeros_like(high)], axis=0)


def loss_kernel(
    builds, tiles, half, chunk, block,
    meta, log_alpha, obs, nxt, act, misc_wide, noise_own, misc_own,
    own_actor, other_actor, own_critic, other_critic,
    keep, send,
    flat_ta, flat_oa, flat_tc, flat_oc,
    w1_t, w1a, w1c, wa_t, wa_o, wa_back, w2_ta, w2_tc, w2a, w2c, w2a_back, w2c_back, w2q_back,
    bias2, w3_ta, w3_oa, w3_tc, w3_oc, w3a_back, w3c_back, bias3_ta, bias3_oa, bias3_tc, bias3_oc,
    square,
    g1a, g1c, g2a, g2c, g3a, g3c, gb2a, gb2c, gb3a, gb3c, sums, total,
    z1_t, z1_a, z1_c, h1c, h2c, dz1c, dz2c, doc, h1a, h2a, dz1a, dz2a, doa,
    table, got, wide, states_before, states, states_after, nexts_after, aux, aux_after,
    gathered, listed, chosen, count, peaks, done, raw_ta, raw_oa, raw_tc, raw_oc, arrived,
):
    grid_step = pl.program_id(0)
    step = grid_step - builds

    def first_products(rows, next_rows, which=(0, 1, 2)):
        x = rows[...]
        x3 = x[:, 0:384]
        if 0 in which:
            z1_c[...] = nt(w1c[...], jnp.concatenate([x3, x], axis=1))
        if 1 in which:
            z1_a[...] = nt(w1a[...], jnp.concatenate([x3, x3], axis=1))
        if 2 in which:
            z1_t[...] = nt(w1_t[...], next_rows[...])

    def gradients(rows, which=range(6)):
        x = rows[...]
        if 0 in which:
            g2c[...] += nt(h1c[...], dz2c[...])
        if 1 in which:
            g3c[...] += nt(doc[...], h2c[...])
        if 2 in which:
            g1c[...] += nn(dz1c[...], x)
        if 3 in which:
            g2a[...] += nt(h1a[...], dz2a[...])
        if 4 in which:
            g3a[...] += nt(doa[...], h2a[...])
        if 5 in which:
            g1a[...] += nn(dz1a[...], x[:, 0:384])

    raws = (raw_ta, raw_oa, raw_tc, raw_oc)

    def parameter_copies(first):
        sources = (own_actor, other_actor, own_critic, other_critic)
        if not first:
            sources = (other_actor, own_actor, other_critic, own_critic)
        return [
            pltpu.make_async_copy(source, raw, arrived.at[k])
            for k, (source, raw) in enumerate(zip(sources, raws))
        ]

    @pl.when((grid_step == 0) & (meta[0] == 0))
    def _():
        for copy in parameter_copies(True):
            copy.start()

    @pl.when((grid_step == 0) & (meta[0] != 0))
    def _():
        for copy in parameter_copies(False):
            copy.start()

    @pl.when(grid_step == 0)
    def _():
        wide[...] = jnp.zeros_like(wide)
        gathered[...] = jnp.zeros_like(gathered)
        peaks[...] = jnp.zeros_like(peaks)
        listed[...] = jnp.zeros_like(listed)
        count[0] = 0

    @pl.when(grid_step < builds)
    def _():
        build_table(grid_step, block, obs, nxt, act, misc_wide, table, wide)
        choose(half // builds, noise_own, misc_own, listed, gathered, count)
        for k in range(0, half // builds, LANES):
            peaks[0:1, :] = jnp.maximum(peaks[0:1, :], misc_own[MISC_WEIGHT : MISC_WEIGHT + 1, k : k + LANES])

    @pl.when(grid_step == builds - 1)
    def _():
        for copy in parameter_copies(True):
            copy.wait()
        for flat, raw in zip((flat_ta, flat_oa, flat_tc, flat_oc), raws):
            copy_flat(flat, raw)
        copy = pltpu.make_async_copy(listed, chosen, done)
        copy.start()
        eye = square_eye()
        running = [
            actor_head(flat_ta, A_ROWS, w3_ta, bias3_ta, None),
            actor_head(flat_oa, A_ROWS, w3_oa, bias3_oa, w3a_back),
            critic_head(flat_tc, C_ROWS, eye, w3_tc, bias3_tc, None),
            critic_head(
                flat_oc, C_ROWS, eye, w3_oc, bias3_oc, w3c_back,
                lambda row: second_layer(flat_oc, C_ROWS, eye, w2c, w2c_back, w2q_back, row),
            ),
        ]
        flats = ((flat_ta, A_ROWS), (flat_tc, C_ROWS), (flat_oa, A_ROWS), (flat_oc, C_ROWS))
        beside = [
            lambda: first_layer(flat_oc, C_ROWS, eye, w1c, 2, 0),
            lambda: first_layer(flat_oa, A_ROWS, eye, w1a, 2, 0),
            lambda: first_layer(flat_ta, A_ROWS, eye, w1_t, 1, 0),
            lambda: first_layer(flat_tc, C_ROWS, eye, w1_t, 1, HID),
            lambda: action_layer(flat_oc, eye, square, wa_o, w1c, wa_back),
            lambda: action_layer(flat_tc, eye, square, wa_t, None, None),
            lambda: second_layer(flat_oa, A_ROWS, eye, w2a, w2a_back),
            lambda: second_layer(flat_ta, A_ROWS, eye, w2_ta, None),
            lambda: second_layer(flat_tc, C_ROWS, eye, w2_tc, None),
            lambda: second_biases(flats, eye, bias2),
            copy.wait,
        ]
        zeros = [g1a, g1c, g2a, g2c, g3a, g3c, gb2a, gb2c, gb3a, gb3c, sums]
        zeros += [h1c, h2c, dz1c, dz2c, doc, h1a, h2a, dz1a, dz2a, doa]
        fetched = 0
        while running or beside:
            running = [piece for piece in running if next(piece, True) is None]
            if beside:
                task = beside.pop(0)
                task()
                waited = task == copy.wait or fetched > 0
            for ref in zeros[:2]:
                ref[...] = jnp.zeros_like(ref)
            zeros = zeros[2:]
            if waited and fetched < TILE:
                fetch_rows(chosen, 0, table, got, fetched, fetched + 64)
                fetched += 64
        for ref in zeros:
            ref[...] = jnp.zeros_like(ref)
        fetch_rows(chosen, 0, table, got, fetched, TILE)
        turn_rows(got, states, nexts_after, aux)
        first_products(states, nexts_after)
        states_before[...] = states[...]

    @pl.when((grid_step >= builds) & (step * TILE < count[0]))
    def _():
        alpha = jnp.exp(jnp.full((1, SUB), log_alpha[0], F32))
        col0 = spread_lanes(w3c_back[:, 0:LANES])
        col1 = spread_lanes(w3c_back[:, LANES : 2 * LANES])
        pad = jnp.zeros((32 - ACT, SUB), F32)
        gap = jnp.zeros((24 - ACT, SUB), F32)
        row16 = lax.broadcasted_iota(jnp.int32, (16, SUB), 0)

        def head(weights, hidden, bias, size):
            tick()
            both = nn(weights[...], hidden)
            return both[0:size, :] + both[size : 2 * size, :] + spread_lanes(bias)

        def tick():
            task = beside.pop(0) if beside else None
            if task is not None:
                task()

        def gelu_t(t):
            tick()
            return gelu(t)

        def pair_t(t):
            tick()
            return gelu_pair(t)

        def nn_t(left, right):
            tick()
            return nn(left, right)

        def part(sub):
            lanes = slice(sub * SUB, (sub + 1) * SUB)
            per = SUB // LANES
            blocks = [gathered[step * (TILE // LANES) + sub * per + k] for k in range(per)]
            own = jnp.concatenate(blocks, axis=1)
            noise = own[0 : 2 * ACT + 1, :]
            place = step * TILE + sub * SUB + lax.broadcasted_iota(jnp.int32, (1, SUB), 1)
            counted = (place < count[0]).astype(F32)
            importance = own[OWN_WEIGHT + MISC_WEIGHT : OWN_WEIGHT + MISC_WEIGHT + 1, :]
            weight = counted * importance
            h1 = gelu_t(z1_t[0:HID, lanes])
            z2_t = nn_t(w2_ta[...], h1) + spread_lanes(bias2[:, 0 * LANES : 1 * LANES])
            hidden_a, s1a = pair_t(z1_a[:, lanes])
            z2_a = nn_t(w2a[...], twice(hidden_a)) + spread_lanes(bias2[:, 2 * LANES : 3 * LANES])
            hidden_c, s1c = pair_t(z1_c[:, lanes])
            z2_c = nn_t(w2c[...], twice(hidden_c)) + spread_lanes(bias2[:, 3 * LANES : 4 * LANES])
            yield
            h2 = gelu_t(z2_t)
            out = head(w3_ta, h2, bias3_ta[...], 48)
            last_a, s2a = pair_t(z2_a)
            out_a = head(w3_oa, last_a, bias3_oa[...], 48)
            last_c, s2c = pair_t(z2_c)
            both = nn_t(w3_oc[...], last_c)
            out_c = both[0:8, :] + both[16:24, :] + spread_lanes(bias3_oc[...])
            yield
            next_action, next_logp, _, _ = policy_parts(out, noise[0:ACT, :])
            z1_n = z1_t[HID:, lanes] + nn_t(wa_t[...], stacked_action(next_action, pad))
            shocks = noise[ACT : 2 * ACT, :]
            action, logp, spread_a, slope_a = policy_parts(out_a, shocks)
            old_action = aux[0:ACT, lanes] + aux[AUX_LOW : AUX_LOW + ACT, lanes]
            z1_q = z1_c[:, lanes] + nn_t(wa_o[...], stacked_action(action - old_action, pad))
            yield
            h1 = gelu_t(z1_n)
            z2_n = nn_t(w2_tc[...], h1) + spread_lanes(bias2[:, 1 * LANES : 2 * LANES])
            h1q, s1q = pair_t(z1_q)
            z2_q = nn_t(w2c[...], twice(h1q)) + spread_lanes(bias2[:, 3 * LANES : 4 * LANES])
            yield
            h2 = gelu_t(z2_n)
            both = nn_t(w3_tc[...], h2)
            out_t = both[0:8, :] + both[16:24, :] + spread_lanes(bias3_tc[...])
            h2q, s2q = pair_t(z2_q)
            both = nn_t(w3_oc[...], h2q)
            value_now = both[0:1, :] + both[16:17, :] + spread_lanes(bias3_oc[0:1, :])
            dz1q = nn_t(w2q_back[...], twice(s2q.astype(BF16))) * s1q
            yield
            both = nn_t(wa_back[...], dz1q.astype(BF16))
            value_back = both[0:ACT, :] + both[32 : 32 + ACT, :]
            next_spread = softplus(out_t[1:2, :]) + 0.1
            reward = aux[AUX_REWARD : AUX_REWARD + 1, lanes]
            goal = reward + DISCOUNT * (
                out_t[0:1, :] + next_spread * noise[2 * ACT : 2 * ACT + 1, :] - alpha * next_logp
            )
            q_value = out_c[0:1, :]
            soft, slope = softplus_pair(out_c[1:2, :])
            spread = soft + 0.1
            inverse = 1.0 / spread
            square_inverse = inverse * inverse
            miss = goal - q_value
            bound = jnp.minimum(jnp.maximum(miss, -3.0 * spread), 3.0 * spread)
            critic_loss = weight * (
                0.5 * miss * miss * square_inverse
                + 0.5 * bound * bound * square_inverse
                + jnp.log(spread)
            )
            mean_back = -weight * miss * square_inverse
            spread_back = weight * (1.0 - bound * bound * square_inverse) * inverse * slope
            dz2 = (col0 * mean_back + col1 * spread_back) * s2c
            back = dz2.astype(BF16)
            gb2c[...] += fold(dz2)
            dz1 = nn_t(w2c_back[...], twice(back)) * s1c
            do_c = jnp.where(
                row16 == 0,
                jnp.broadcast_to(mean_back, (16, SUB)),
                jnp.where(row16 == 1, jnp.broadcast_to(spread_back, (16, SUB)), 0.0),
            )
            gb3c[...] += fold(do_c)
            dz2c[:, lanes] = back
            dz1c[:, lanes] = dz1.astype(BF16)
            doc[:, lanes] = do_c.astype(BF16)
            h1c[:, lanes] = hidden_c
            h2c[:, lanes] = last_c
            yield
            counted_alpha = counted * alpha
            d_pre = counted_alpha * 2.0 * action - counted * value_back * (1.0 - action * action)
            d_raw = (d_pre * shocks - counted_alpha / spread_a) * slope_a
            do_a = jnp.concatenate([d_pre, gap, d_raw, gap], axis=0)
            high, low = split(ROOT_TWO * do_a)
            dz2 = nn_t(w3a_back[...], jnp.concatenate([high, low, high], axis=0)) * s2a
            back = dz2.astype(BF16)
            gb2a[...] += fold(dz2)
            gb3a[...] += fold(do_a)
            sums[0:1, :] += fold(counted)
            sums[1:2, :] += fold(counted * logp)
            sums[2:3, :] += fold(critic_loss)
            sums[3:4, :] += fold(counted * (alpha * logp - value_now))
            yield
            dz1 = nn_t(w2a_back[...], twice(back)) * s1a
            dz2a[:, lanes] = back
            dz1a[:, lanes] = dz1.astype(BF16)
            doa[:, lanes] = high
            h1a[:, lanes] = hidden_a
            h2a[:, lanes] = last_a

        first_pick = jnp.minimum(step + 1, tiles - 1) * (TILE // LANES)

        fetches = [
            lambda k=k: fetch_rows(chosen, first_pick, table, got, k, k + 16)
            for k in range(0, TILE, 16)
        ]
        sums_before = [
            lambda which=which: gradients(states_before, (which,)) for which in range(6)
        ]
        products_after = [
            lambda: turn_rows(got, states_after, nexts_after, aux_after),
            lambda: first_products(states_after, nexts_after, (0,)),
            lambda: first_products(states_after, nexts_after, (1,)),
            lambda: first_products(states_after, nexts_after, (2,)),
        ]
        beside = []
        for k, fetch in enumerate(fetches):
            beside.append(fetch)
            if k % 5 == 2 and sums_before:
                beside.append(sums_before.pop(0))
        for product in products_after:
            beside += [product, None, None, None, None]

        running = [part(sub) for sub in range(TILE // SUB)]
        while running:
            running = [piece for piece in running if next(piece, True) is None]
        while beside:
            tick()
        states_before[...] = states[...]
        states[...] = states_after[...]
        aux[...] = aux_after[...]

    @pl.when(step == tiles - 1)
    def _():
        gradients(states_before)
        total[...] = jnp.zeros_like(total)

        def sum_row(block):
            return jnp.sum(block.T, axis=0, keepdims=True)

        for side in (0, 1):
            at = side * LANES
            turned = 0.5 * g1a[at : at + LANES, :].T
            total[A_W1[side] : A_W1[side] + OBS, :] = turned[0:OBS, :]
            total[A_B + side : A_B + side + 1, :] = turned[ONE_LANE : ONE_LANE + 1, :]
            total[A_W2[side] : A_W2[side] + HID, :] = (0.5 * ROOT_HALF) * g2a[:, at : at + LANES]
            total[A_W3[side] : A_W3[side] + ACT, :] = 0.5 * g3a[0:ACT, at : at + LANES]
            total[A_W3[side] + ACT : A_W3[side] + 2 * ACT, :] = (
                0.5 * g3a[24 : 24 + ACT, at : at + LANES]
            )
            total[A_B + 2 + side : A_B + 3 + side, :] = 0.5 * sum_row(gb2a[at : at + LANES, :])
            turned = 0.5 * g1c[at : at + LANES, :].T
            total[C_W1[side] : C_W1[side] + OBS, :] = turned[0:OBS, :]
            total[C_W1[side] + OBS : C_W1[side] + OBS + ACT, :] = (
                turned[384 : 384 + ACT, :] + turned[384 + AUX_LOW : 384 + AUX_LOW + ACT, :]
            )
            total[C_B + side : C_B + side + 1, :] = turned[ONE_LANE : ONE_LANE + 1, :]
            total[C_W2[side] : C_W2[side] + HID, :] = (0.5 * ROOT_HALF) * g2c[:, at : at + LANES]
            total[C_W3[side] : C_W3[side] + 2, :] = ROOT_HALF * g3c[0:2, at : at + LANES]
            total[C_B + 2 + side : C_B + 3 + side, :] = 0.5 * sum_row(gb2c[at : at + LANES, :])
        none = jnp.zeros((LANES - 2 * ACT, LANES), F32)
        total[A_B + 4 : A_B + 5, :] = sum_row(
            jnp.concatenate([gb3a[0:ACT, :], gb3a[24 : 24 + ACT, :], none], axis=0)
        )
        none = jnp.zeros((LANES - 16, LANES), F32)
        total[C_B + 4 : C_B + 5, :] = sum_row(jnp.concatenate([gb3c[...], none], axis=0))
        total[EXTRA : EXTRA + 4, :] = sums[0:4, :]
        peak = jnp.max(peaks[0:1, :], axis=1, keepdims=True)
        for k in range(EXTRA + 8 - EXTRA_SLOTS):
            total[EXTRA_SLOTS + k : EXTRA_SLOTS + k + 1, :] = jnp.where(
                lanes_of(1) + k * LANES == meta[1], jnp.broadcast_to(peak, (1, LANES)), 0.0
            )
        count = keep.shape[0] // chunk
        for p in range(count):
            at = pl.multiple_of((meta[1] ^ p) * chunk, 8)
            keep[p * chunk : (p + 1) * chunk, :] = total[pl.ds(at, chunk), :]
            at = pl.multiple_of((meta[2] ^ p) * chunk, 8)
            send[p * chunk : (p + 1) * chunk, :] = total[pl.ds(at, chunk), :]


def losses(
    meta, log_alpha, obs, nxt, act, noise, misc, own_a, other_a, own_c, other_c, devices
):
    rows = obs.shape[1]
    half = noise.shape[1] // 2
    tiles = -(-half // TILE)
    block = next(size for size in (1280, 640, 512, 256, 128) if rows % size == 0)
    builds = rows // block
    own = half // builds
    list_rows = -(-(tiles * (TILE // LANES) + 1) // 8) * 8
    chunk = chunk_rows(devices)
    buffer_rows = chunk * devices

    def fixed(i, meta):
        return (0, 0)

    def source(i, meta):
        return (0, jnp.minimum(i, builds - 1))

    def own_source(i, meta):
        return (0, meta[0] * builds + jnp.minimum(i, builds - 1))

    def body(*refs):
        loss_kernel(builds, tiles, half, chunk, block, *refs)

    def bf(*shape):
        return pltpu.VMEM(shape, BF16)

    def f32(*shape):
        return pltpu.VMEM(shape, F32)

    features = noise.shape[0]
    return pl.pallas_call(
        body,
        out_shape=(
            jax.ShapeDtypeStruct((buffer_rows // 2, LANES), F32),
            jax.ShapeDtypeStruct((buffer_rows // 2, LANES), F32),
        ),
        grid_spec=pltpu.PrefetchScalarGridSpec(
            num_scalar_prefetch=1,
            grid=(builds + tiles,),
            in_specs=[
                pl.BlockSpec(memory_space=pltpu.SMEM),
                pl.BlockSpec((OBS, block), source),
                pl.BlockSpec((OBS, block), source),
                pl.BlockSpec((ACT, block), source),
                pl.BlockSpec((8, block), source),
                pl.BlockSpec((features, own), own_source),
                pl.BlockSpec((8, own), own_source),
                pl.BlockSpec(memory_space=pl.ANY),
                pl.BlockSpec(memory_space=pl.ANY),
                pl.BlockSpec(memory_space=pl.ANY),
                pl.BlockSpec(memory_space=pl.ANY),
            ],
            out_specs=(
                pl.BlockSpec((buffer_rows // 2, LANES), fixed),
                pl.BlockSpec((buffer_rows // 2, LANES), fixed),
            ),
            scratch_shapes=[
                f32(A_FLAT, LANES), f32(A_FLAT, LANES), f32(C_FLAT, LANES), f32(C_FLAT, LANES),
                bf(512, 384), bf(HID, 768), bf(HID, 896),
                bf(HID, LANES), bf(HID, LANES), bf(64, HID),
                bf(HID, HID), bf(HID, HID),
                bf(HID, 512), bf(HID, 512), bf(HID, 512), bf(HID, 512), bf(HID, 512),
                f32(HID, 4 * LANES), bf(96, HID), bf(96, HID), bf(32, HID), bf(32, HID),
                bf(HID, 144), f32(HID, 2 * LANES),
                f32(48, LANES), f32(48, LANES), f32(8, LANES), f32(8, LANES),
                f32(32, HID),
                f32(HID, 384), f32(HID, 512), f32(HID, HID), f32(HID, HID),
                f32(48, HID), f32(16, HID), f32(HID, LANES), f32(HID, LANES),
                f32(48, LANES), f32(16, LANES), f32(8, LANES), f32(buffer_rows, LANES),
                f32(2 * HID, TILE), f32(HID, TILE), f32(HID, TILE),
                bf(HID, TILE), bf(HID, TILE), bf(HID, TILE), bf(HID, TILE), bf(16, TILE),
                bf(HID, TILE), bf(HID, TILE), bf(HID, TILE), bf(HID, TILE), bf(48, TILE),
                f32((rows + 8) * CHUNKS, LANES), f32(TILE * 8, LANES), f32(LANES, block),
                bf(TILE, 512), bf(TILE, 512), bf(TILE, 512), bf(TILE, 384),
                f32(AUX_ROWS, TILE), f32(AUX_ROWS, TILE),
                f32(list_rows, OWN_ROWS, LANES),
                pltpu.VMEM((list_rows, LANES), jnp.int32),
                pltpu.SMEM((list_rows, LANES), jnp.int32),
                pltpu.SMEM((1,), jnp.int32), f32(8, LANES), pltpu.SemaphoreType.DMA,
                f32(1, A_SIZE), f32(1, A_SIZE), f32(1, C_SIZE), f32(1, C_SIZE),
                pltpu.SemaphoreType.DMA((4,)),
            ],
        ),
        compiler_params=pltpu.CompilerParams(
            dimension_semantics=("arbitrary",), vmem_limit_bytes=VMEM_BYTES
        ),
        name="losses",
    )(meta, log_alpha, obs, nxt, act, misc, noise, misc, own_a, other_a, own_c, other_c)


def stat_pieces(width_in, width_out):
    sizes = [width_in, HID, HID, HID, HID, width_out, HID, HID, width_out]
    starts = [sum(sizes[:k]) for k in range(len(sizes))]
    rows = [-(-size // LANES) for size in sizes]
    return sizes, starts, [sum(rows[:k]) for k in range(len(rows))], sum(rows)


def aligned_stats(statistics, width_in, width_out):
    sizes, starts, _, rows = stat_pieces(width_in, width_out)
    pieces = [
        jnp.pad(statistics[start : start + size], (0, -size % LANES))
        for size, start in zip(sizes, starts)
    ]
    pieces.append(jnp.zeros((-rows % 8 * LANES,), F32))
    return jnp.concatenate(pieces).reshape(-1, LANES)


def blend(old, new):
    return DECAY_RATE * old + (1.0 - DECAY_RATE) * new


def clip_scale(square_sum, number):
    return 1.0 / jnp.maximum(1.0, jnp.sqrt(square_sum / number) / CLIP_LEVEL)


def whole_sum(value):
    return jnp.sum(jnp.sum(value, axis=0, keepdims=True), axis=1, keepdims=True)


def large_layers(total, scale, old_row, width_in, places, rows, fg, fu, lines):
    for layer, (height, flat_at) in enumerate(((width_in, 0), (HID, rows[0]))):
        parts = [total[at : at + height, :] * scale for at in places[layer]]
        squares = [g * g + TINY_TERM for g in parts]
        yield
        blocks = -(-height // LANES)
        old = jnp.concatenate([column(old_row(layer, k)) for k in range(blocks)], axis=0)
        old = old[0:height, :]
        mean = jnp.sum(squares[0] + squares[1], axis=1, keepdims=True) * (1.0 / HID)
        row_stat = blend(old, jnp.broadcast_to(mean, (height, LANES)))
        yield
        for k in range(blocks):
            block = row_stat[k * LANES : min(height, (k + 1) * LANES), :]
            if block.shape[0] < LANES:
                block = jnp.concatenate(
                    [block, jnp.zeros((LANES - block.shape[0], LANES), F32)], axis=0
                )
            lines[layer].append(block.T[0:1, :])
        mean_row = jnp.sum(row_stat, axis=0, keepdims=True) * (1.0 / height)
        row_root = lax.rsqrt(row_stat)
        yield
        steps = []
        square_sum = 0.0
        for side in (0, 1):
            col_stat = blend(
                old_row(3 + layer, side),
                jnp.sum(squares[side], axis=0, keepdims=True) * (1.0 / height),
            )
            lines[3 + layer].append(col_stat)
            step = (parts[side] * row_root) * (lax.rsqrt(col_stat) * jnp.sqrt(mean_row))
            square_sum = square_sum + jnp.sum(step * step, axis=0, keepdims=True)
            steps.append(step)
            fg[pl.ds(flat_at + side, height, stride=2), :] = parts[side]
            yield
        square_sum = jnp.sum(square_sum, axis=1, keepdims=True)
        factor = clip_scale(square_sum, float(height * HID))
        for side in (0, 1):
            fu[pl.ds(flat_at + side, height, stride=2), :] = steps[side] * factor
            yield


def last_layer(total, scale, old_row, width_out, place, rows, fg, fu, lines):
    tall = -(-width_out // 8) * 8
    parts = [total[at : at + tall, :] * scale for at in place]
    real = rows_of(tall) < width_out
    squares = [jnp.where(real, g * g + TINY_TERM, 0.0) for g in parts]
    old = column(old_row(5, 0))[0:tall, :]
    mean = jnp.sum(squares[0] + squares[1], axis=1, keepdims=True) * (1.0 / HID)
    col_stat = blend(old, jnp.broadcast_to(mean, (tall, LANES)))
    pad = jnp.zeros((LANES - tall, LANES), F32)
    lines[5].append(jnp.concatenate([col_stat, pad], axis=0).T[0:1, :])
    yield
    row_stats = []
    for side in (0, 1):
        row_stats.append(
            blend(
                old_row(2, side),
                jnp.sum(squares[side], axis=0, keepdims=True) * (1.0 / width_out),
            )
        )
        lines[2].append(row_stats[side])
    mean_row = jnp.sum(row_stats[0] + row_stats[1], axis=1, keepdims=True) * (1.0 / HID)
    col_root = jnp.where(real, lax.rsqrt(col_stat), 0.0)
    steps = [
        (parts[side] * lax.rsqrt(row_stats[side])) * (col_root * jnp.sqrt(mean_row))
        for side in (0, 1)
    ]
    factor = clip_scale(
        whole_sum(steps[0] * steps[0] + steps[1] * steps[1]), float(HID * width_out)
    )
    yield
    size = rows[2] - rows[1]
    turned = [
        jnp.concatenate(
            [jnp.concatenate([jnp.where(real, part, 0.0), pad], axis=0).T for part in pair], axis=0
        )
        for pair in (parts, [u * factor for u in steps])
    ]
    yield
    flat_parts = yield from flatten(turned, width_out, -(-size // 8) * 8)
    for flat, part in zip((fg, fu), flat_parts):
        flat[rows[1] : rows[1] + size, :] = part[0:size, :]


def biases(total, scale, old, width_out, bias_at, rows, fg, fu, lines):
    grad = total[bias_at : bias_at + 8, :] * scale
    line = rows_of(8)
    lane = lanes_of(8)
    real = (line < 4) | ((line == 4) & (lane < width_out))
    grad = jnp.where(real, grad, 0.0)
    stat = blend(old, grad[0:5, :] * grad[0:5, :] + TINY_TERM)
    step = jnp.where(real[0:5, :], grad[0:5, :] * lax.rsqrt(stat), 0.0)
    yield
    factor = clip_scale(whole_sum(step * step), float(2 * HID + width_out))
    fg[rows[2] : rows[2] + 5, :] = grad[0:5, :]
    fu[rows[2] : rows[2] + 5, :] = step * factor
    for k in range(5):
        lines[6 + k // 2].append(stat[k : k + 1, :])


def store_statistics(lines, width_in, width_out, stats_out):
    sizes, starts, _, _ = stat_pieces(width_in, width_out)
    size = stats_out.shape[0]
    count = -(-size // LANES)
    made = [jnp.zeros((1, LANES), F32) for _ in range(count + 1)]
    lane = lanes_of(1)
    for piece, pieces in enumerate(lines):
        for k, value in enumerate(pieces):
            start = starts[piece] + k * LANES
            width = min(LANES, sizes[piece] - k * LANES)
            value = jnp.where(lane < width, value, 0.0)
            shift = start % LANES
            at = start // LANES
            if shift:
                value = pltpu.roll(value, shift, 1)
            made[at] = made[at] + jnp.where(lane >= shift, value, 0.0)
            if shift:
                made[at + 1] = made[at + 1] + jnp.where(lane < shift, value, 0.0)
    for k in range(count):
        width = min(LANES, size - k * LANES)
        stats_out[pl.ds(k * LANES, width)] = made[k][:, 0:width].reshape(width)


def in_turn(stages):
    while stages:
        stages = [stage for stage in stages if next(stage, True) is None]


def net_update(total, scale, old_stats, width_in, width_out, places, rows, fg, fu):
    sizes, _, first, _ = stat_pieces(width_in, width_out)
    lines = [[] for _ in sizes]

    def old_row(piece, k):
        return old_stats[first[piece] + k : first[piece] + k + 1, :]

    old_bias = old_stats[first[6] : first[6] + 5, :]
    large = large_layers(total, scale, old_row, width_in, places, rows, fg, fu, lines)
    small = [
        last_layer(total, scale, old_row, width_out, places[2], rows, fg, fu, lines),
        biases(total, scale, old_bias, width_out, places[3], rows, fg, fu, lines),
    ]
    return large, small, lines


def write_net(side, own, other, fg, fu, slot, copy, grad):
    size = own.shape[1]
    whole = size // 2048

    def piece(at, row, width, count):
        mine = own[0:1, pl.ds(at, width)].reshape(count, width // count)
        theirs = other[0:1, pl.ds(at, width)].reshape(count, width // count)
        wide = width // count
        step = fu[pl.ds(row, count), 0:wide]
        online = jnp.where(side == 0, theirs, mine)
        new = online - LEARN_RATE * step
        held = jnp.where(side == 0, POLYAK_RATE * new + (1.0 - POLYAK_RATE) * mine, new)
        slot[0:1, pl.ds(at, width)] = held.reshape(1, width)
        copy[0:1, pl.ds(at, width)] = held.astype(BF16).reshape(1, width)
        grad[pl.ds(at, width)] = fg[pl.ds(row, count), 0:wide].reshape(width)

    for k in range(whole):
        piece(k * 2048, k * 16, 2048, 16)
    full = size // LANES
    for row in range(whole * 16, full):
        piece(row * LANES, row, LANES, 1)
    piece(full * LANES, full, size - full * LANES, 1)


def update_kernel(
    chunk, devices,
    meta, log_alpha, mine, theirs, own_a, other_a, own_c, other_c, stats_a, stats_c,
    slot_a, slot_c, copy_a, copy_c, grad_a, grad_c, new_a, new_c, summary, alpha_out,
    total, fg_a, fu_a, fg_c, fu_c,
):
    count = devices // 2
    for p in range(count):
        at = pl.multiple_of((meta[1] ^ p) * chunk, 8)
        total[pl.ds(at, chunk), :] = mine[p * chunk : (p + 1) * chunk, :]
        at = pl.multiple_of((meta[2] ^ p) * chunk, 8)
        total[pl.ds(at, chunk), :] = theirs[p * chunk : (p + 1) * chunk, :]

    sums = jnp.sum(total[EXTRA : EXTRA + 8, :], axis=1, keepdims=True)
    peak = jnp.max(total[EXTRA_SLOTS : EXTRA + 8, :], axis=1, keepdims=True)
    peak = jnp.max(peak, axis=0, keepdims=True)
    counted = sums[0:1, :]
    scale_a = 1.0 / counted
    scale_c = scale_a / peak
    lane = lanes_of(1)
    line = jnp.where(
        lane == 0,
        jnp.broadcast_to(sums[2:3, :] / peak, (1, LANES)),
        jnp.where(
            lane == 1,
            jnp.broadcast_to(sums[3:4, :], (1, LANES)),
            jnp.broadcast_to(counted, (1, LANES)),
        ),
    )
    summary[...] = line[:, 0:3].reshape(3)
    new_alpha = log_alpha[0] + ALPHA_STEP * (
        jnp.broadcast_to(sums[1:2, :] / counted, (1, LANES)) - ACT
    )
    alpha_out[...] = new_alpha[:, 0:1].reshape(1)
    large_a, small_a, lines_a = net_update(
        total, scale_a, stats_a, OBS, 2 * ACT, (A_W1, A_W2, A_W3, A_B), A_ROWS, fg_a, fu_a
    )
    large_c, small_c, lines_c = net_update(
        total, scale_c, stats_c, OBS + ACT, 2, (C_W1, C_W2, C_W3, C_B), C_ROWS, fg_c, fu_c
    )
    in_turn([large_a] + small_a)
    in_turn([large_c] + small_c)
    store_statistics(lines_a, OBS, 2 * ACT, new_a)
    store_statistics(lines_c, OBS + ACT, 2, new_c)
    write_net(meta[0], own_a, other_a, fg_a, fu_a, slot_a, copy_a, grad_a)
    write_net(meta[0], own_c, other_c, fg_c, fu_c, slot_c, copy_c, grad_c)


def update(meta, log_alpha, mine, theirs, own_a, other_a, own_c, other_c, stats_a, stats_c, sizes, devices):
    chunk = chunk_rows(devices)

    def body(*refs):
        update_kernel(chunk, devices, *refs)

    def f32(*shape):
        return jax.ShapeDtypeStruct(shape, F32)

    smem = pl.BlockSpec(memory_space=pltpu.SMEM)
    vmem = pl.BlockSpec(memory_space=pltpu.VMEM)
    return pl.pallas_call(
        body,
        out_shape=(
            f32(1, A_SIZE), f32(1, C_SIZE),
            jax.ShapeDtypeStruct((1, A_SIZE), BF16), jax.ShapeDtypeStruct((1, C_SIZE), BF16),
            f32(A_SIZE), f32(C_SIZE), f32(sizes[0]), f32(sizes[1]), f32(3), f32(1),
        ),
        in_specs=[smem, smem] + [vmem] * 8,
        out_specs=tuple([vmem] * 10),
        scratch_shapes=[
            pltpu.VMEM((chunk * devices, LANES), F32),
            pltpu.VMEM((A_FLAT, LANES), F32), pltpu.VMEM((A_FLAT, LANES), F32),
            pltpu.VMEM((C_FLAT, LANES), F32), pltpu.VMEM((C_FLAT, LANES), F32),
        ],
        compiler_params=pltpu.CompilerParams(vmem_limit_bytes=UPDATE_VMEM_BYTES),
        name="optimizer",
    )(meta, log_alpha, mine, theirs, own_a, other_a, own_c, other_c, stats_a, stats_c)


def chunk_rows(devices):
    return -(-DATA_ROWS // (8 * devices)) * 8


def stage_bits(count, group):
    number = count.bit_length() - 1
    bits = [(bit + 2 * group) % number for bit in range(number)]
    return [bits[k : k + 2] for k in range(0, number, 2)]


def swap_groups(value):
    return lax.ppermute(value, "grp", [(0, 1), (1, 0)])


def exchange(value, stage, digit):
    count = lax.axis_size("dp")
    pairs = []
    for group in (0, 1):
        bits = stage_bits(count, group)[stage]
        mask = sum(1 << bit for k, bit in enumerate(bits) if digit >> k & 1)
        pairs += [(group * count + i, group * count + (i ^ mask)) for i in range(count)]
    return lax.ppermute(value, ("grp", "dp"), pairs)


def buffer_place(group, count):
    index = lax.axis_index("dp")
    place = group
    for bits in stage_bits(count, group):
        for bit in reversed(bits):
            place = place * 2 + (index >> bit & 1)
    return place


def all_sum(keep, send):
    count = lax.axis_size("dp")
    sizes = [1 << len(bits) for bits in stage_bits(count, 0)]
    value = keep + swap_groups(send)
    for stage, size in enumerate(sizes):
        rows = value.shape[0] // size
        parts = [value[k * rows : (k + 1) * rows] for k in range(size)]
        came = [exchange(parts[k], stage, k) for k in range(1, size)]
        value = parts[0]
        for part in came:
            value = value + part
    for stage, size in reversed(list(enumerate(sizes))):
        value = jnp.concatenate(
            [value] + [exchange(value, stage, k) for k in range(1, size)], axis=0
        )
    return value, swap_groups(value)


def shards(
    obs_rows,
    next_rows,
    action_rows,
    reward_rows,
    batch_index,
    valid_mask,
    noise,
    importance,
    actor_params,
    critic_params,
    actor_stats,
    critic_stats,
    log_alpha,
):
    devices = lax.axis_size("dp") * lax.axis_size("grp")
    group_side = lax.axis_index("grp")
    other_a = swap_groups(actor_params)
    other_c = swap_groups(critic_params)
    places = [buffer_place(group, lax.axis_size("dp")) for group in (0, 1)]
    number = jnp.arange(3)
    meta = jnp.where((number == 1) == (group_side == 0), places[0], places[1])
    meta = jnp.where(number == 0, group_side, meta).astype(jnp.int32)
    row = lax.broadcasted_iota(jnp.int32, (8, batch_index.shape[0]), 0)
    misc = jnp.where(row == MISC_VALID, valid_mask[None], batch_index[None]).astype(F32)
    misc = jnp.where(row == MISC_WEIGHT, importance[None], misc)
    misc = jnp.where(row == 0, reward_rows[None], misc)
    keep, send = losses(
        meta, log_alpha, obs_rows.T, next_rows.T, action_rows.T, noise.T, misc,
        actor_params, other_a, critic_params, other_c, devices,
    )
    keep, send, actor_stats, critic_stats = lax.optimization_barrier(
        (keep, send, actor_stats, critic_stats)
    )
    mine, theirs = all_sum(keep, send)
    (
        slot_a, slot_c, copy_a, copy_c, grad_a, grad_c, new_a, new_c, summary, alpha
    ) = update(
        meta, log_alpha, mine, theirs, actor_params, other_a, critic_params, other_c,
        aligned_stats(actor_stats, OBS, 2 * ACT), aligned_stats(critic_stats, OBS + ACT, 2),
        (actor_stats.shape[0], critic_stats.shape[0]), devices,
    )
    return (
        slot_a, slot_c, copy_a, copy_c, grad_a, grad_c, new_a, new_c,
        summary, alpha,
    )


def solution(mesh):
    return jax.shard_map(
        shards,
        mesh=mesh,
        in_specs=(
            P("dp", None),
            P("dp", None),
            P("dp", None),
            P("dp"),
            P("dp"),
            P("dp"),
            P("dp", None),
            P("dp"),
            P("grp", None),
            P("grp", None),
            P(),
            P(),
            P(),
        ),
        out_specs=(
            P("grp", None),
            P("grp", None),
            P("grp", None),
            P("grp", None),
            P(),
            P(),
            P(),
            P(),
            P(),
            P(),
        ),
        check_vma=False,
    )
```

```python
import jax
import jax.numpy as jnp
from jax import lax
from jax.experimental import pallas as pl
from jax.experimental.pallas import tpu as pltpu
from jax.sharding import PartitionSpec as P

OBS = 376
ACT = 17
HID = 256
LANES = 128
TILE = 512
SUB = 256

DISCOUNT = 0.99
POLYAK_RATE = 0.1
DECAY_RATE = 0.5
LEARN_RATE = 0.1
CLIP_LEVEL = 0.1
ALPHA_STEP = 0.01
TINY_TERM = 1e-30
HALF_LOG_TWO_PI = 0.9189385332046727
LOG_TWO = 0.6931471805599453
ROOT_HALF = 0.7071067811865476
ROOT_TWO = 1.4142135623730951
LOG2_E = 1.4426950408889634
LOG2_TWO_OVER_ROOT_PI = 0.17425193548825

F32 = jnp.float32
BF16 = jnp.bfloat16
VMEM_BYTES = 57 * 2**20
UPDATE_VMEM_BYTES = 24 * 2**20

ONE_LANE = OBS
AUX_LOW = 32
AUX_REWARD = 64
AUX_AGAIN = 96
AUX_ROWS = 72
CHUNKS = 7
OWN_WEIGHT = 40
OWN_ROWS = 48
MISC_WEIGHT = 1
MISC_VALID = 2
MISC_INDEX = 3


def flat_rows(width_in, width_out):
    w2 = width_in * HID // LANES
    w3 = w2 + HID * HID // LANES
    b1 = w3 + HID * width_out // LANES
    return w2, w3, b1, b1 + 2, b1 + 4


A_ROWS = flat_rows(OBS, 2 * ACT)
C_ROWS = flat_rows(OBS + ACT, 2)
A_SIZE = A_ROWS[4] * LANES + 2 * ACT
C_SIZE = C_ROWS[4] * LANES + 2
A_FLAT = -(-A_SIZE // 1024) * 8
C_FLAT = -(-C_SIZE // 1024) * 8

A_W1 = (0, OBS)
A_W2 = (2 * OBS, 2 * OBS + HID)
A_W3 = (2 * OBS + 2 * HID, 2 * OBS + 2 * HID + 40)
A_B = A_W3[1] + 40
C_W1 = (A_B + 8, A_B + 8 + 400)
C_W2 = (C_W1[1] + 400, C_W1[1] + 400 + HID)
C_W3 = (C_W2[1] + HID, C_W2[1] + HID + 8)
C_B = C_W3[1] + 8
EXTRA = C_B + 8
EXTRA_SLOTS = EXTRA + 4
DATA_ROWS = EXTRA + 8


def nn(left, right):
    return lax.dot_general(
        left, right, (((1,), (0,)), ((), ())), preferred_element_type=F32
    )


def nt(left, right):
    return lax.dot_general(
        left, right, (((1,), (1,)), ((), ())), preferred_element_type=F32
    )


def split(value):
    high = value.astype(BF16)
    return high, (value - high.astype(F32)).astype(BF16)


def twice(value):
    return jnp.concatenate([value, value], axis=0)


def gelu(t):
    return (t * (1.0 + lax.erf(t))).astype(BF16)


def gelu_pair(t):
    double_cdf = 1.0 + lax.erf(t)
    bell = jnp.exp2(LOG2_TWO_OVER_ROOT_PI - LOG2_E * (t * t))
    return (t * double_cdf).astype(BF16), double_cdf + t * bell


def softplus(x):
    return jnp.maximum(x, 0.0) + jnp.log(1.0 + jnp.exp(-jnp.abs(x)))


def softplus_pair(x):
    decay = jnp.exp(-jnp.abs(x))
    inverse = 1.0 / (1.0 + decay)
    return jnp.maximum(x, 0.0) + jnp.log(1.0 + decay), jnp.where(x >= 0.0, inverse, decay * inverse)


def column(row):
    return jnp.broadcast_to(row, (LANES, LANES)).T


def rows_of(count):
    return lax.broadcasted_iota(jnp.int32, (count, LANES), 0)


def lanes_of(count):
    return lax.broadcasted_iota(jnp.int32, (count, LANES), 1)


def square_eye(reverse=False):
    row = lax.broadcasted_iota(jnp.int32, (HID, HID), 0)
    lane = lax.broadcasted_iota(jnp.int32, (HID, HID), 1)
    return (row == (HID - 1 - lane if reverse else lane)).astype(F32).astype(BF16)


def two_pieces(value):
    return jnp.concatenate(split(value), axis=1)


def turns(value, shift, stride):
    turn = (rows_of(HID) * stride + shift) % LANES
    for step in (2, 4, 8, 16, 32, 64):
        value = jnp.where((turn & step) != 0, pltpu.roll(value, step, 1), value)
        yield value


def unflatten(flat, width):
    rows = flat.shape[0]
    first = (HID - 1 - rows_of(HID)) * width
    lane = lanes_of(HID)
    owner = first // LANES
    picks = jnp.concatenate([(owner == lane), (owner + 1 == lane)], axis=0).astype(F32).astype(BF16)
    found = nn(picks[:, 0:rows], two_pieces(flat))
    yield
    found = found[:, 0:LANES] + found[:, LANES:]
    mixed = jnp.where(lane >= first % LANES, found[0:HID, :], found[HID:, :])
    for turned in turns(mixed, -(HID - 1) * width % LANES, width):
        yield
    pieces = nn(square_eye(True), two_pieces(turned)).astype(BF16)
    yield
    return pieces


def flatten(values, width, rows):
    first = rows_of(HID) * width % LANES
    lane = lanes_of(HID)
    for turned in turns(values[0] + pltpu.roll(values[1], 64, 1), 0, width):
        yield
    swapped = pltpu.roll(turned, 64, 1)
    begun = (lane >= first) & (lane < first + width)
    wrapped = lane < first + width - LANES
    parts = []
    for value in (turned, swapped):
        parts.append(
            jnp.concatenate([jnp.where(begun, value, 0.0), jnp.where(wrapped, value, 0.0)], axis=0)
        )
    both = jnp.concatenate(parts, axis=1)
    high, low = split(both)
    least = (both - high.astype(F32) - low.astype(F32)).astype(BF16)
    owner = lax.broadcasted_iota(jnp.int32, (rows, HID), 1) * width // LANES
    row = lax.broadcasted_iota(jnp.int32, (rows, HID), 0)
    places = jnp.concatenate([owner == row, owner + 1 == row], axis=1).astype(F32).astype(BF16)
    yield
    found = nn(places, jnp.concatenate([high, low, least], axis=1))
    yield
    found = found[:, 0:HID] + found[:, HID : 2 * HID] + found[:, 2 * HID :]
    return found[:, 0:LANES], found[:, LANES:]


def build_table(step, block, obs, nxt, act, misc, table, wide):
    groups = block // 8
    table3 = table.reshape(table.shape[0] // (8 * CHUNKS), 8 * CHUNKS, LANES)
    at = pl.multiple_of(step * groups, groups)

    def put(value, first):
        for c in range(value.shape[1] // LANES):
            table3[pl.ds(at, groups), 8 * (first + c) : 8 * (first + c) + 8, :] = value[
                :, LANES * c : LANES * (c + 1)
            ].reshape(groups, 8, LANES)

    ones = (lax.broadcasted_iota(jnp.int32, (8, block), 0) == 0).astype(F32)
    whole = OBS // 16 * 16

    def padded(source):
        value = source[...]
        rest = jnp.concatenate([value[whole:, :].astype(F32), ones], axis=0).astype(BF16)
        return jnp.concatenate([value[0:whole, :], rest], axis=0)

    follow = padded(nxt)
    value = jnp.concatenate([padded(obs), follow[0:LANES, :]], axis=0)
    eye = square_eye()
    turned = [nt(eye, value[:, k : k + HID]) for k in range(0, block, HID)]
    put(jnp.concatenate(turned, axis=0), 0)
    put(follow[LANES:, :].T.astype(F32), 4)
    action = act[...]
    high = action.astype(BF16).astype(F32)
    wide[0:ACT, :] = high
    wide[AUX_LOW : AUX_LOW + ACT, :] = action - high
    wide[AUX_AGAIN : AUX_AGAIN + ACT, :] = high
    wide[AUX_REWARD : AUX_REWARD + 8, :] = misc[...]
    put(wide[...].T, 6)


def choose(size, noise, misc, listed, gathered, count):
    lane = lanes_of(1)
    wide_lane = lanes_of(OWN_ROWS)
    parts = size // LANES
    counted = misc[MISC_VALID : MISC_VALID + 1, :]
    flags = [counted[:, LANES * k : LANES * (k + 1)] for k in range(parts)]
    stacked = jnp.concatenate(flags + [jnp.zeros((-parts % 16, LANES), F32)], axis=0).astype(BF16)
    before = nn(stacked, (rows_of(LANES) < lanes_of(LANES)).astype(F32).astype(BF16))
    before = before.astype(jnp.int32)
    index = misc[MISC_INDEX : MISC_INDEX + 1, :].astype(jnp.int32)
    spot = (index >> 3) * (8 * CHUNKS) + (index & 7)
    digits = jnp.concatenate([spot >> 8, spot & 255] + [jnp.zeros_like(spot)] * 14, axis=0)
    gap = jnp.zeros((OWN_WEIGHT - 2 * ACT - 1, size), F32)
    high, low = split(jnp.concatenate([noise[...], gap, misc[...]], axis=0))
    value = jnp.concatenate([digits.astype(F32).astype(BF16), high, low], axis=0)
    place = count[0]
    for k in range(parts):
        where = (before[k : k + 1, :] + place) & (LANES - 1)
        where = jnp.where(flags[k] > 0.0, where, -1)
        hit = (jnp.broadcast_to(where, (LANES, LANES)) == rows_of(LANES)).astype(F32).astype(BF16)
        moved = nt(value[:, LANES * k : LANES * (k + 1)], hit)
        spots = moved[0:2, :].astype(jnp.int32)
        spots = (spots[0:1, :] << 8) + spots[1:2, :]
        values = moved[16 : 16 + OWN_ROWS, :] + moved[16 + OWN_ROWS :, :]
        row = place >> 7
        start = place & (LANES - 1)
        listed[pl.ds(row, 1), :] += jnp.where(lane >= start, spots, 0)
        listed[pl.ds(row + 1, 1), :] += jnp.where(lane >= start, 0, spots)
        gathered[row] += jnp.where(wide_lane >= start, values, 0.0)
        gathered[row + 1] += jnp.where(wide_lane >= start, 0.0, values)
        place = place + jnp.sum(flags[k]).astype(jnp.int32)
    count[0] = place


def fetch_rows(chosen, first, table, got, start, stop, batch=16):
    for base in range(start, stop, batch):
        found = [
            table[pl.ds(chosen[first + j // LANES, j % LANES], 8, stride=8), :]
            for j in range(base, base + batch)
        ]
        for j in range(base, base + batch):
            got[pl.ds((j // 8) * 64 + j % 8, 8, stride=8), :] = found[j - base]


def turn_rows(got, states, nexts, aux):
    got3 = got.reshape(TILE // 8, 64, LANES)

    def chunk(c):
        return got3[:, 8 * c : 8 * c + 8, :].reshape(TILE, LANES)

    for c in range(3):
        states[:, LANES * c : LANES * (c + 1)] = chunk(c).astype(BF16)
        nexts[:, LANES * c : LANES * (c + 1)] = chunk(3 + c).astype(BF16)
    extra = chunk(6)
    states[:, 3 * LANES :] = extra.astype(BF16)
    aux[...] = extra.T[0:AUX_ROWS, :]


def copy_flat(flat, source):
    size = source.shape[1]
    whole = size // 1024

    for k in range(whole):
        flat[8 * k : 8 * k + 8, :] = source[0:1, 1024 * k : 1024 * (k + 1)].reshape(8, LANES)
    flat[8 * whole : 8 * whole + 8, :] = jnp.zeros((8, LANES), F32)
    full = (size - whole * 1024) // LANES
    for k in range(full):
        flat[8 * whole + k : 8 * whole + k + 1, :] = source[
            0:1, whole * 1024 + k * LANES : whole * 1024 + (k + 1) * LANES
        ]
    rest = size - whole * 1024 - full * LANES
    flat[8 * whole + full : 8 * whole + full + 1, 0:rest] = source[0:1, size - rest : size]


def halves(flat, start, height):
    return [flat[pl.ds(start + side, height, stride=2), :] for side in (0, 1)]


def natural(flat, start, height):
    return jnp.concatenate([flat[pl.ds(start + side, height, stride=2), :] for side in (0, 1)], axis=1)


def bias_row(flat, at):
    return jnp.concatenate([flat[at : at + 1, :], flat[at + 1 : at + 2, :]], axis=1)


def first_layer(flat, rows, eye, dst, pieces, base):
    tile = lax.broadcasted_iota(jnp.int32, (8, HID), 0)
    bias = jnp.where(tile == 0, jnp.broadcast_to(bias_row(flat, rows[2]), (8, HID)), 0.0)
    parts = split(jnp.concatenate([natural(flat, 0, OBS), bias], axis=0) * ROOT_HALF)
    for k in range(pieces):
        dst[base : base + HID, 384 * k : 384 * (k + 1)] = nt(eye, parts[k]).astype(BF16)


def action_layer(flat, eye, square, stack, first, back):
    square[0:ACT, :] = natural(flat, 2 * OBS, ACT)
    square[ACT:, :] = jnp.zeros((32 - ACT, HID), F32)
    value = square[...]
    high, low = split(value * ROOT_HALF)
    none = jnp.zeros_like(high)
    stack[...] = nt(eye, jnp.concatenate([high, high, low, none], axis=0)).astype(BF16)
    if first is not None:
        first[:, 768:896] = nt(eye, jnp.concatenate([high, high, none, low], axis=0)).astype(BF16)
        high, low = split(0.5 * value)
        back[0:32, :] = high
        back[32:64, :] = low


def second_layer(flat, rows, eye, forward, back, back_q=None, head=None):
    value = 0.5 * natural(flat, rows[0], HID)
    high, low = split(value)
    forward[:, 0:HID] = nt(eye, high).astype(BF16)
    if back is not None:
        forward[:, HID : 2 * HID] = nt(eye, low).astype(BF16)
        back[:, 0:HID] = high
        back[:, HID : 2 * HID] = low
    if back_q is not None:
        high, low = split(value * head)
        back_q[:, 0:HID] = high
        back_q[:, HID : 2 * HID] = low


def second_biases(flats, eye, bias):
    rows = [
        jnp.broadcast_to(bias_row(flat, rows[3]) * ROOT_HALF, (LANES, HID)) for flat, rows in flats
    ]
    both = jnp.concatenate([two_pieces(row) for row in rows], axis=0)
    bias[...] = nt(jnp.concatenate([eye, eye], axis=1), both)


def selector(rows, chosen):
    return chosen(rows_of(rows), lanes_of(rows)).astype(F32)


def block_pair(value):
    none = jnp.zeros_like(value)
    return jnp.concatenate(
        [jnp.concatenate([value, none], axis=1), jnp.concatenate([none, value], axis=1)], axis=0
    ).astype(BF16)


def actor_place(row, lane):
    return ((row == lane) & (row < ACT)) | ((row - 24 == lane - ACT) & (row >= 24) & (row < 24 + ACT))


def actor_head(flat, rows, forward, bias, back):
    pieces = yield from unflatten(flat[rows[1] : rows[1] + 72, :] * ROOT_HALF, 2 * ACT)
    place = selector(48, actor_place)
    forward[...] = nt(block_pair(place), pieces).astype(BF16)
    if back is not None:
        none = jnp.zeros((48, LANES), F32)
        high = jnp.concatenate([place, none], axis=1)
        low = jnp.concatenate([none, place], axis=1)
        back[...] = nt(pieces, jnp.concatenate([high, high, low], axis=0).astype(BF16)).astype(BF16)
    heads = column(flat[rows[4] : rows[4] + 1, :])
    bias[0:24, :] = heads[0:24, :]
    bias[24:48, :] = heads[ACT : ACT + 24, :]


def critic_head(flat, rows, eye, forward, bias, back, use_mean_row=None):
    pieces = yield from unflatten(flat[rows[1] : rows[1] + 8, :] * ROOT_HALF, 2)
    place = selector(16, lambda row, lane: (row == lane) & (row < 2))
    both = nt(block_pair(place), pieces)
    forward[...] = both.astype(BF16)
    bias[...] = column(flat[rows[4] : rows[4] + 1, :])[0:8, :]
    if back is None:
        return
    yield
    spread = [
        jnp.concatenate(
            [jnp.broadcast_to(both[16 * part + k : 16 * part + k + 1, :], (LANES, HID)) for part in (0, 1)],
            axis=1,
        )
        for k in (0, 1)
    ]
    columns = nt(jnp.concatenate([eye, eye], axis=1), jnp.concatenate(spread, axis=0).astype(BF16))
    back[...] = ROOT_TWO * columns
    yield
    use_mean_row(ROOT_TWO * (both[0:1, :] + both[16:17, :]))


def spread_lanes(bias):
    return jnp.concatenate([bias] * (SUB // LANES), axis=1)


def fold(value):
    parts = [value[:, k : k + LANES] for k in range(0, value.shape[1], LANES)]
    total = parts[0]
    for part in parts[1:]:
        total = total + part
    return total


def policy_parts(out, shocks):
    centre = out[0:ACT, :]
    raw = out[24 : 24 + ACT, :]
    soft, slope = softplus_pair(raw)
    spread = soft + 0.05
    pre = centre + spread * shocks
    terms = (
        -0.5 * shocks * shocks
        - jnp.log(spread)
        - HALF_LOG_TWO_PI
        - 2.0 * (LOG_TWO - pre - softplus(-2.0 * pre))
    )
    return jnp.tanh(pre), jnp.sum(terms, axis=0, keepdims=True), spread, slope


def stacked_action(value, pad):
    tall = jnp.concatenate([value, pad], axis=0)
    high, low = split(tall)
    return jnp.concatenate([high, low, high, jnp.zeros_like(high)], axis=0)


def loss_kernel(
    builds, tiles, half, chunk, block,
    meta, log_alpha, obs, nxt, act, misc_wide, noise_own, misc_own,
    own_actor, other_actor, own_critic, other_critic,
    keep, send,
    flat_ta, flat_oa, flat_tc, flat_oc,
    w1_t, w1a, w1c, wa_t, wa_o, wa_back, w2_ta, w2_tc, w2a, w2c, w2a_back, w2c_back, w2q_back,
    bias2, w3_ta, w3_oa, w3_tc, w3_oc, w3a_back, w3c_back, bias3_ta, bias3_oa, bias3_tc, bias3_oc,
    square,
    g1a, g1c, g2a, g2c, g3a, g3c, gb2a, gb2c, gb3a, gb3c, sums, total,
    z1_t, z1_a, z1_c, h1c, h2c, dz1c, dz2c, doc, h1a, h2a, dz1a, dz2a, doa,
    table, got, wide, states_before, states, states_after, nexts_after, aux, aux_after,
    gathered, listed, chosen, count, peaks, done, raw_ta, raw_oa, raw_tc, raw_oc, arrived,
):
    grid_step = pl.program_id(0)
    step = grid_step - builds

    def first_products(rows, next_rows, which=(0, 1, 2)):
        x = rows[...]
        x3 = x[:, 0:384]
        if 0 in which:
            z1_c[...] = nt(w1c[...], jnp.concatenate([x3, x], axis=1))
        if 1 in which:
            z1_a[...] = nt(w1a[...], jnp.concatenate([x3, x3], axis=1))
        if 2 in which:
            z1_t[...] = nt(w1_t[...], next_rows[...])

    def gradients(rows, which=range(6)):
        x = rows[...]
        if 0 in which:
            g2c[...] += nt(h1c[...], dz2c[...])
        if 1 in which:
            g3c[...] += nt(doc[...], h2c[...])
        if 2 in which:
            g1c[...] += nn(dz1c[...], x)
        if 3 in which:
            g2a[...] += nt(h1a[...], dz2a[...])
        if 4 in which:
            g3a[...] += nt(doa[...], h2a[...])
        if 5 in which:
            g1a[...] += nn(dz1a[...], x[:, 0:384])

    raws = (raw_ta, raw_oa, raw_tc, raw_oc)

    def parameter_copies(first):
        sources = (own_actor, other_actor, own_critic, other_critic)
        if not first:
            sources = (other_actor, own_actor, other_critic, own_critic)
        return [
            pltpu.make_async_copy(source, raw, arrived.at[k])
            for k, (source, raw) in enumerate(zip(sources, raws))
        ]

    @pl.when((grid_step == 0) & (meta[0] == 0))
    def _():
        for copy in parameter_copies(True):
            copy.start()

    @pl.when((grid_step == 0) & (meta[0] != 0))
    def _():
        for copy in parameter_copies(False):
            copy.start()

    @pl.when(grid_step == 0)
    def _():
        wide[...] = jnp.zeros_like(wide)
        gathered[...] = jnp.zeros_like(gathered)
        peaks[...] = jnp.zeros_like(peaks)
        listed[...] = jnp.zeros_like(listed)
        count[0] = 0

    @pl.when(grid_step < builds)
    def _():
        build_table(grid_step, block, obs, nxt, act, misc_wide, table, wide)
        choose(half // builds, noise_own, misc_own, listed, gathered, count)
        for k in range(0, half // builds, LANES):
            peaks[0:1, :] = jnp.maximum(peaks[0:1, :], misc_own[MISC_WEIGHT : MISC_WEIGHT + 1, k : k + LANES])

    @pl.when(grid_step == builds - 1)
    def _():
        for copy in parameter_copies(True):
            copy.wait()
        for flat, raw in zip((flat_ta, flat_oa, flat_tc, flat_oc), raws):
            copy_flat(flat, raw)
        copy = pltpu.make_async_copy(listed, chosen, done)
        copy.start()
        eye = square_eye()
        running = [
            actor_head(flat_ta, A_ROWS, w3_ta, bias3_ta, None),
            actor_head(flat_oa, A_ROWS, w3_oa, bias3_oa, w3a_back),
            critic_head(flat_tc, C_ROWS, eye, w3_tc, bias3_tc, None),
            critic_head(
                flat_oc, C_ROWS, eye, w3_oc, bias3_oc, w3c_back,
                lambda row: second_layer(flat_oc, C_ROWS, eye, w2c, w2c_back, w2q_back, row),
            ),
        ]
        flats = ((flat_ta, A_ROWS), (flat_tc, C_ROWS), (flat_oa, A_ROWS), (flat_oc, C_ROWS))
        beside = [
            lambda: first_layer(flat_oc, C_ROWS, eye, w1c, 2, 0),
            lambda: first_layer(flat_oa, A_ROWS, eye, w1a, 2, 0),
            lambda: first_layer(flat_ta, A_ROWS, eye, w1_t, 1, 0),
            lambda: first_layer(flat_tc, C_ROWS, eye, w1_t, 1, HID),
            lambda: action_layer(flat_oc, eye, square, wa_o, w1c, wa_back),
            lambda: action_layer(flat_tc, eye, square, wa_t, None, None),
            lambda: second_layer(flat_oa, A_ROWS, eye, w2a, w2a_back),
            lambda: second_layer(flat_ta, A_ROWS, eye, w2_ta, None),
            lambda: second_layer(flat_tc, C_ROWS, eye, w2_tc, None),
            lambda: second_biases(flats, eye, bias2),
            copy.wait,
        ]
        zeros = [g1a, g1c, g2a, g2c, g3a, g3c, gb2a, gb2c, gb3a, gb3c, sums]
        zeros += [h1c, h2c, dz1c, dz2c, doc, h1a, h2a, dz1a, dz2a, doa]
        fetched = 0
        while running or beside:
            running = [piece for piece in running if next(piece, True) is None]
            if beside:
                task = beside.pop(0)
                task()
                waited = task == copy.wait or fetched > 0
            for ref in zeros[:2]:
                ref[...] = jnp.zeros_like(ref)
            zeros = zeros[2:]
            if waited and fetched < TILE:
                fetch_rows(chosen, 0, table, got, fetched, fetched + 64)
                fetched += 64
        for ref in zeros:
            ref[...] = jnp.zeros_like(ref)
        fetch_rows(chosen, 0, table, got, fetched, TILE)
        turn_rows(got, states, nexts_after, aux)
        first_products(states, nexts_after)
        states_before[...] = states[...]

    @pl.when((grid_step >= builds) & (step * TILE < count[0]))
    def _():
        alpha = jnp.exp(jnp.full((1, SUB), log_alpha[0], F32))
        col0 = spread_lanes(w3c_back[:, 0:LANES])
        col1 = spread_lanes(w3c_back[:, LANES : 2 * LANES])
        pad = jnp.zeros((32 - ACT, SUB), F32)
        gap = jnp.zeros((24 - ACT, SUB), F32)
        row16 = lax.broadcasted_iota(jnp.int32, (16, SUB), 0)

        def head(weights, hidden, bias, size):
            tick()
            both = nn(weights[...], hidden)
            return both[0:size, :] + both[size : 2 * size, :] + spread_lanes(bias)

        def tick():
            task = beside.pop(0) if beside else None
            if task is not None:
                task()

        def gelu_t(t):
            tick()
            return gelu(t)

        def pair_t(t):
            tick()
            return gelu_pair(t)

        def nn_t(left, right):
            tick()
            return nn(left, right)

        def part(sub):
            lanes = slice(sub * SUB, (sub + 1) * SUB)
            per = SUB // LANES
            blocks = [gathered[step * (TILE // LANES) + sub * per + k] for k in range(per)]
            own = jnp.concatenate(blocks, axis=1)
            noise = own[0 : 2 * ACT + 1, :]
            place = step * TILE + sub * SUB + lax.broadcasted_iota(jnp.int32, (1, SUB), 1)
            counted = (place < count[0]).astype(F32)
            importance = own[OWN_WEIGHT + MISC_WEIGHT : OWN_WEIGHT + MISC_WEIGHT + 1, :]
            weight = counted * importance
            h1 = gelu_t(z1_t[0:HID, lanes])
            z2_t = nn_t(w2_ta[...], h1) + spread_lanes(bias2[:, 0 * LANES : 1 * LANES])
            hidden_a, s1a = pair_t(z1_a[:, lanes])
            z2_a = nn_t(w2a[...], twice(hidden_a)) + spread_lanes(bias2[:, 2 * LANES : 3 * LANES])
            hidden_c, s1c = pair_t(z1_c[:, lanes])
            z2_c = nn_t(w2c[...], twice(hidden_c)) + spread_lanes(bias2[:, 3 * LANES : 4 * LANES])
            yield
            h2 = gelu_t(z2_t)
            out = head(w3_ta, h2, bias3_ta[...], 48)
            last_a, s2a = pair_t(z2_a)
            out_a = head(w3_oa, last_a, bias3_oa[...], 48)
            last_c, s2c = pair_t(z2_c)
            both = nn_t(w3_oc[...], last_c)
            out_c = both[0:8, :] + both[16:24, :] + spread_lanes(bias3_oc[...])
            yield
            next_action, next_logp, _, _ = policy_parts(out, noise[0:ACT, :])
            z1_n = z1_t[HID:, lanes] + nn_t(wa_t[...], stacked_action(next_action, pad))
            shocks = noise[ACT : 2 * ACT, :]
            action, logp, spread_a, slope_a = policy_parts(out_a, shocks)
            old_action = aux[0:ACT, lanes] + aux[AUX_LOW : AUX_LOW + ACT, lanes]
            z1_q = z1_c[:, lanes] + nn_t(wa_o[...], stacked_action(action - old_action, pad))
            yield
            h1 = gelu_t(z1_n)
            z2_n = nn_t(w2_tc[...], h1) + spread_lanes(bias2[:, 1 * LANES : 2 * LANES])
            h1q, s1q = pair_t(z1_q)
            z2_q = nn_t(w2c[...], twice(h1q)) + spread_lanes(bias2[:, 3 * LANES : 4 * LANES])
            yield
            h2 = gelu_t(z2_n)
            both = nn_t(w3_tc[...], h2)
            out_t = both[0:8, :] + both[16:24, :] + spread_lanes(bias3_tc[...])
            h2q, s2q = pair_t(z2_q)
            both = nn_t(w3_oc[...], h2q)
            value_now = both[0:1, :] + both[16:17, :] + spread_lanes(bias3_oc[0:1, :])
            dz1q = nn_t(w2q_back[...], twice(s2q.astype(BF16))) * s1q
            yield
            both = nn_t(wa_back[...], dz1q.astype(BF16))
            value_back = both[0:ACT, :] + both[32 : 32 + ACT, :]
            next_spread = softplus(out_t[1:2, :]) + 0.1
            reward = aux[AUX_REWARD : AUX_REWARD + 1, lanes]
            goal = reward + DISCOUNT * (
                out_t[0:1, :] + next_spread * noise[2 * ACT : 2 * ACT + 1, :] - alpha * next_logp
            )
            q_value = out_c[0:1, :]
            soft, slope = softplus_pair(out_c[1:2, :])
            spread = soft + 0.1
            inverse = 1.0 / spread
            square_inverse = inverse * inverse
            miss = goal - q_value
            bound = jnp.minimum(jnp.maximum(miss, -3.0 * spread), 3.0 * spread)
            critic_loss = weight * (
                0.5 * miss * miss * square_inverse
                + 0.5 * bound * bound * square_inverse
                + jnp.log(spread)
            )
            mean_back = -weight * miss * square_inverse
            spread_back = weight * (1.0 - bound * bound * square_inverse) * inverse * slope
            dz2 = (col0 * mean_back + col1 * spread_back) * s2c
            back = dz2.astype(BF16)
            gb2c[...] += fold(dz2)
            dz1 = nn_t(w2c_back[...], twice(back)) * s1c
            do_c = jnp.where(
                row16 == 0,
                jnp.broadcast_to(mean_back, (16, SUB)),
                jnp.where(row16 == 1, jnp.broadcast_to(spread_back, (16, SUB)), 0.0),
            )
            gb3c[...] += fold(do_c)
            dz2c[:, lanes] = back
            dz1c[:, lanes] = dz1.astype(BF16)
            doc[:, lanes] = do_c.astype(BF16)
            h1c[:, lanes] = hidden_c
            h2c[:, lanes] = last_c
            yield
            counted_alpha = counted * alpha
            d_pre = counted_alpha * 2.0 * action - counted * value_back * (1.0 - action * action)
            d_raw = (d_pre * shocks - counted_alpha / spread_a) * slope_a
            do_a = jnp.concatenate([d_pre, gap, d_raw, gap], axis=0)
            high, low = split(ROOT_TWO * do_a)
            dz2 = nn_t(w3a_back[...], jnp.concatenate([high, low, high], axis=0)) * s2a
            back = dz2.astype(BF16)
            gb2a[...] += fold(dz2)
            gb3a[...] += fold(do_a)
            sums[0:1, :] += fold(counted)
            sums[1:2, :] += fold(counted * logp)
            sums[2:3, :] += fold(critic_loss)
            sums[3:4, :] += fold(counted * (alpha * logp - value_now))
            yield
            dz1 = nn_t(w2a_back[...], twice(back)) * s1a
            dz2a[:, lanes] = back
            dz1a[:, lanes] = dz1.astype(BF16)
            doa[:, lanes] = high
            h1a[:, lanes] = hidden_a
            h2a[:, lanes] = last_a

        first_pick = jnp.minimum(step + 1, tiles - 1) * (TILE // LANES)

        fetches = [
            lambda k=k: fetch_rows(chosen, first_pick, table, got, k, k + 16)
            for k in range(0, TILE, 16)
        ]
        sums_before = [
            lambda which=which: gradients(states_before, (which,)) for which in range(6)
        ]
        products_after = [
            lambda: turn_rows(got, states_after, nexts_after, aux_after),
            lambda: first_products(states_after, nexts_after, (0,)),
            lambda: first_products(states_after, nexts_after, (1,)),
            lambda: first_products(states_after, nexts_after, (2,)),
        ]
        beside = []
        for k, fetch in enumerate(fetches):
            beside.append(fetch)
            if k % 5 == 2 and sums_before:
                beside.append(sums_before.pop(0))
        for product in products_after:
            beside += [product, None, None, None, None]

        running = [part(sub) for sub in range(TILE // SUB)]
        while running:
            running = [piece for piece in running if next(piece, True) is None]
        while beside:
            tick()
        states_before[...] = states[...]
        states[...] = states_after[...]
        aux[...] = aux_after[...]

    @pl.when(step == tiles - 1)
    def _():
        gradients(states_before)
        total[...] = jnp.zeros_like(total)

        def sum_row(block):
            return jnp.sum(block.T, axis=0, keepdims=True)

        for side in (0, 1):
            at = side * LANES
            turned = 0.5 * g1a[at : at + LANES, :].T
            total[A_W1[side] : A_W1[side] + OBS, :] = turned[0:OBS, :]
            total[A_B + side : A_B + side + 1, :] = turned[ONE_LANE : ONE_LANE + 1, :]
            total[A_W2[side] : A_W2[side] + HID, :] = (0.5 * ROOT_HALF) * g2a[:, at : at + LANES]
            total[A_W3[side] : A_W3[side] + ACT, :] = 0.5 * g3a[0:ACT, at : at + LANES]
            total[A_W3[side] + ACT : A_W3[side] + 2 * ACT, :] = (
                0.5 * g3a[24 : 24 + ACT, at : at + LANES]
            )
            total[A_B + 2 + side : A_B + 3 + side, :] = 0.5 * sum_row(gb2a[at : at + LANES, :])
            turned = 0.5 * g1c[at : at + LANES, :].T
            total[C_W1[side] : C_W1[side] + OBS, :] = turned[0:OBS, :]
            total[C_W1[side] + OBS : C_W1[side] + OBS + ACT, :] = (
                turned[384 : 384 + ACT, :] + turned[384 + AUX_LOW : 384 + AUX_LOW + ACT, :]
            )
            total[C_B + side : C_B + side + 1, :] = turned[ONE_LANE : ONE_LANE + 1, :]
            total[C_W2[side] : C_W2[side] + HID, :] = (0.5 * ROOT_HALF) * g2c[:, at : at + LANES]
            total[C_W3[side] : C_W3[side] + 2, :] = ROOT_HALF * g3c[0:2, at : at + LANES]
            total[C_B + 2 + side : C_B + 3 + side, :] = 0.5 * sum_row(gb2c[at : at + LANES, :])
        none = jnp.zeros((LANES - 2 * ACT, LANES), F32)
        total[A_B + 4 : A_B + 5, :] = sum_row(
            jnp.concatenate([gb3a[0:ACT, :], gb3a[24 : 24 + ACT, :], none], axis=0)
        )
        none = jnp.zeros((LANES - 16, LANES), F32)
        total[C_B + 4 : C_B + 5, :] = sum_row(jnp.concatenate([gb3c[...], none], axis=0))
        total[EXTRA : EXTRA + 4, :] = sums[0:4, :]
        peak = jnp.max(peaks[0:1, :], axis=1, keepdims=True)
        for k in range(EXTRA + 8 - EXTRA_SLOTS):
            total[EXTRA_SLOTS + k : EXTRA_SLOTS + k + 1, :] = jnp.where(
                lanes_of(1) + k * LANES == meta[1], jnp.broadcast_to(peak, (1, LANES)), 0.0
            )
        count = keep.shape[0] // chunk
        for p in range(count):
            at = pl.multiple_of((meta[1] ^ p) * chunk, 8)
            keep[p * chunk : (p + 1) * chunk, :] = total[pl.ds(at, chunk), :]
            at = pl.multiple_of((meta[2] ^ p) * chunk, 8)
            send[p * chunk : (p + 1) * chunk, :] = total[pl.ds(at, chunk), :]


def losses(
    meta, log_alpha, obs, nxt, act, noise, misc, own_a, other_a, own_c, other_c, devices
):
    rows = obs.shape[1]
    half = noise.shape[1] // 2
    tiles = -(-half // TILE)
    block = next(size for size in (1280, 640, 512, 256, 128) if rows % size == 0)
    builds = rows // block
    own = half // builds
    list_rows = -(-(tiles * (TILE // LANES) + 1) // 8) * 8
    chunk = chunk_rows(devices)
    buffer_rows = chunk * devices

    def fixed(i, meta):
        return (0, 0)

    def source(i, meta):
        return (0, jnp.minimum(i, builds - 1))

    def own_source(i, meta):
        return (0, meta[0] * builds + jnp.minimum(i, builds - 1))

    def body(*refs):
        loss_kernel(builds, tiles, half, chunk, block, *refs)

    def bf(*shape):
        return pltpu.VMEM(shape, BF16)

    def f32(*shape):
        return pltpu.VMEM(shape, F32)

    features = noise.shape[0]
    return pl.pallas_call(
        body,
        out_shape=(
            jax.ShapeDtypeStruct((buffer_rows // 2, LANES), F32),
            jax.ShapeDtypeStruct((buffer_rows // 2, LANES), F32),
        ),
        grid_spec=pltpu.PrefetchScalarGridSpec(
            num_scalar_prefetch=1,
            grid=(builds + tiles,),
            in_specs=[
                pl.BlockSpec(memory_space=pltpu.SMEM),
                pl.BlockSpec((OBS, block), source),
                pl.BlockSpec((OBS, block), source),
                pl.BlockSpec((ACT, block), source),
                pl.BlockSpec((8, block), source),
                pl.BlockSpec((features, own), own_source),
                pl.BlockSpec((8, own), own_source),
                pl.BlockSpec(memory_space=pl.ANY),
                pl.BlockSpec(memory_space=pl.ANY),
                pl.BlockSpec(memory_space=pl.ANY),
                pl.BlockSpec(memory_space=pl.ANY),
            ],
            out_specs=(
                pl.BlockSpec((buffer_rows // 2, LANES), fixed),
                pl.BlockSpec((buffer_rows // 2, LANES), fixed),
            ),
            scratch_shapes=[
                f32(A_FLAT, LANES), f32(A_FLAT, LANES), f32(C_FLAT, LANES), f32(C_FLAT, LANES),
                bf(512, 384), bf(HID, 768), bf(HID, 896),
                bf(HID, LANES), bf(HID, LANES), bf(64, HID),
                bf(HID, HID), bf(HID, HID),
                bf(HID, 512), bf(HID, 512), bf(HID, 512), bf(HID, 512), bf(HID, 512),
                f32(HID, 4 * LANES), bf(96, HID), bf(96, HID), bf(32, HID), bf(32, HID),
                bf(HID, 144), f32(HID, 2 * LANES),
                f32(48, LANES), f32(48, LANES), f32(8, LANES), f32(8, LANES),
                f32(32, HID),
                f32(HID, 384), f32(HID, 512), f32(HID, HID), f32(HID, HID),
                f32(48, HID), f32(16, HID), f32(HID, LANES), f32(HID, LANES),
                f32(48, LANES), f32(16, LANES), f32(8, LANES), f32(buffer_rows, LANES),
                f32(2 * HID, TILE), f32(HID, TILE), f32(HID, TILE),
                bf(HID, TILE), bf(HID, TILE), bf(HID, TILE), bf(HID, TILE), bf(16, TILE),
                bf(HID, TILE), bf(HID, TILE), bf(HID, TILE), bf(HID, TILE), bf(48, TILE),
                f32((rows + 8) * CHUNKS, LANES), f32(TILE * 8, LANES), f32(LANES, block),
                bf(TILE, 512), bf(TILE, 512), bf(TILE, 512), bf(TILE, 384),
                f32(AUX_ROWS, TILE), f32(AUX_ROWS, TILE),
                f32(list_rows, OWN_ROWS, LANES),
                pltpu.VMEM((list_rows, LANES), jnp.int32),
                pltpu.SMEM((list_rows, LANES), jnp.int32),
                pltpu.SMEM((1,), jnp.int32), f32(8, LANES), pltpu.SemaphoreType.DMA,
                f32(1, A_SIZE), f32(1, A_SIZE), f32(1, C_SIZE), f32(1, C_SIZE),
                pltpu.SemaphoreType.DMA((4,)),
            ],
        ),
        compiler_params=pltpu.CompilerParams(
            dimension_semantics=("arbitrary",), vmem_limit_bytes=VMEM_BYTES
        ),
        name="losses",
    )(meta, log_alpha, obs, nxt, act, misc, noise, misc, own_a, other_a, own_c, other_c)


def stat_pieces(width_in, width_out):
    sizes = [width_in, HID, HID, HID, HID, width_out, HID, HID, width_out]
    starts = [sum(sizes[:k]) for k in range(len(sizes))]
    rows = [-(-size // LANES) for size in sizes]
    return sizes, starts, [sum(rows[:k]) for k in range(len(rows))], sum(rows)


def aligned_stats(statistics, width_in, width_out):
    sizes, starts, _, rows = stat_pieces(width_in, width_out)
    pieces = [
        jnp.pad(statistics[start : start + size], (0, -size % LANES))
        for size, start in zip(sizes, starts)
    ]
    pieces.append(jnp.zeros((-rows % 8 * LANES,), F32))
    return jnp.concatenate(pieces).reshape(-1, LANES)


def blend(old, new):
    return DECAY_RATE * old + (1.0 - DECAY_RATE) * new


def clip_scale(square_sum, number):
    return 1.0 / jnp.maximum(1.0, jnp.sqrt(square_sum / number) / CLIP_LEVEL)


def whole_sum(value):
    return jnp.sum(jnp.sum(value, axis=0, keepdims=True), axis=1, keepdims=True)


def large_layers(total, scale, old_row, width_in, places, rows, fg, fu, lines):
    for layer, (height, flat_at) in enumerate(((width_in, 0), (HID, rows[0]))):
        parts = [total[at : at + height, :] * scale for at in places[layer]]
        squares = [g * g + TINY_TERM for g in parts]
        yield
        blocks = -(-height // LANES)
        old = jnp.concatenate([column(old_row(layer, k)) for k in range(blocks)], axis=0)
        old = old[0:height, :]
        mean = jnp.sum(squares[0] + squares[1], axis=1, keepdims=True) * (1.0 / HID)
        row_stat = blend(old, jnp.broadcast_to(mean, (height, LANES)))
        yield
        for k in range(blocks):
            block = row_stat[k * LANES : min(height, (k + 1) * LANES), :]
            if block.shape[0] < LANES:
                block = jnp.concatenate(
                    [block, jnp.zeros((LANES - block.shape[0], LANES), F32)], axis=0
                )
            lines[layer].append(block.T[0:1, :])
        mean_row = jnp.sum(row_stat, axis=0, keepdims=True) * (1.0 / height)
        row_root = lax.rsqrt(row_stat)
        yield
        steps = []
        square_sum = 0.0
        for side in (0, 1):
            col_stat = blend(
                old_row(3 + layer, side),
                jnp.sum(squares[side], axis=0, keepdims=True) * (1.0 / height),
            )
            lines[3 + layer].append(col_stat)
            step = (parts[side] * row_root) * (lax.rsqrt(col_stat) * jnp.sqrt(mean_row))
            square_sum = square_sum + jnp.sum(step * step, axis=0, keepdims=True)
            steps.append(step)
            fg[pl.ds(flat_at + side, height, stride=2), :] = parts[side]
            yield
        square_sum = jnp.sum(square_sum, axis=1, keepdims=True)
        factor = clip_scale(square_sum, float(height * HID))
        for side in (0, 1):
            fu[pl.ds(flat_at + side, height, stride=2), :] = steps[side] * factor
            yield


def last_layer(total, scale, old_row, width_out, place, rows, fg, fu, lines):
    tall = -(-width_out // 8) * 8
    parts = [total[at : at + tall, :] * scale for at in place]
    real = rows_of(tall) < width_out
    squares = [jnp.where(real, g * g + TINY_TERM, 0.0) for g in parts]
    old = column(old_row(5, 0))[0:tall, :]
    mean = jnp.sum(squares[0] + squares[1], axis=1, keepdims=True) * (1.0 / HID)
    col_stat = blend(old, jnp.broadcast_to(mean, (tall, LANES)))
    pad = jnp.zeros((LANES - tall, LANES), F32)
    lines[5].append(jnp.concatenate([col_stat, pad], axis=0).T[0:1, :])
    yield
    row_stats = []
    for side in (0, 1):
        row_stats.append(
            blend(
                old_row(2, side),
                jnp.sum(squares[side], axis=0, keepdims=True) * (1.0 / width_out),
            )
        )
        lines[2].append(row_stats[side])
    mean_row = jnp.sum(row_stats[0] + row_stats[1], axis=1, keepdims=True) * (1.0 / HID)
    col_root = jnp.where(real, lax.rsqrt(col_stat), 0.0)
    steps = [
        (parts[side] * lax.rsqrt(row_stats[side])) * (col_root * jnp.sqrt(mean_row))
        for side in (0, 1)
    ]
    factor = clip_scale(
        whole_sum(steps[0] * steps[0] + steps[1] * steps[1]), float(HID * width_out)
    )
    yield
    size = rows[2] - rows[1]
    turned = [
        jnp.concatenate(
            [jnp.concatenate([jnp.where(real, part, 0.0), pad], axis=0).T for part in pair], axis=0
        )
        for pair in (parts, [u * factor for u in steps])
    ]
    yield
    flat_parts = yield from flatten(turned, width_out, -(-size // 8) * 8)
    for flat, part in zip((fg, fu), flat_parts):
        flat[rows[1] : rows[1] + size, :] = part[0:size, :]


def biases(total, scale, old, width_out, bias_at, rows, fg, fu, lines):
    grad = total[bias_at : bias_at + 8, :] * scale
    line = rows_of(8)
    lane = lanes_of(8)
    real = (line < 4) | ((line == 4) & (lane < width_out))
    grad = jnp.where(real, grad, 0.0)
    stat = blend(old, grad[0:5, :] * grad[0:5, :] + TINY_TERM)
    step = jnp.where(real[0:5, :], grad[0:5, :] * lax.rsqrt(stat), 0.0)
    yield
    factor = clip_scale(whole_sum(step * step), float(2 * HID + width_out))
    fg[rows[2] : rows[2] + 5, :] = grad[0:5, :]
    fu[rows[2] : rows[2] + 5, :] = step * factor
    for k in range(5):
        lines[6 + k // 2].append(stat[k : k + 1, :])


def store_statistics(lines, width_in, width_out, stats_out):
    sizes, starts, _, _ = stat_pieces(width_in, width_out)
    size = stats_out.shape[0]
    count = -(-size // LANES)
    made = [jnp.zeros((1, LANES), F32) for _ in range(count + 1)]
    lane = lanes_of(1)
    for piece, pieces in enumerate(lines):
        for k, value in enumerate(pieces):
            start = starts[piece] + k * LANES
            width = min(LANES, sizes[piece] - k * LANES)
            value = jnp.where(lane < width, value, 0.0)
            shift = start % LANES
            at = start // LANES
            if shift:
                value = pltpu.roll(value, shift, 1)
            made[at] = made[at] + jnp.where(lane >= shift, value, 0.0)
            if shift:
                made[at + 1] = made[at + 1] + jnp.where(lane < shift, value, 0.0)
    for k in range(count):
        width = min(LANES, size - k * LANES)
        stats_out[pl.ds(k * LANES, width)] = made[k][:, 0:width].reshape(width)


def in_turn(stages):
    while stages:
        stages = [stage for stage in stages if next(stage, True) is None]


def net_update(total, scale, old_stats, width_in, width_out, places, rows, fg, fu):
    sizes, _, first, _ = stat_pieces(width_in, width_out)
    lines = [[] for _ in sizes]

    def old_row(piece, k):
        return old_stats[first[piece] + k : first[piece] + k + 1, :]

    old_bias = old_stats[first[6] : first[6] + 5, :]
    large = large_layers(total, scale, old_row, width_in, places, rows, fg, fu, lines)
    small = [
        last_layer(total, scale, old_row, width_out, places[2], rows, fg, fu, lines),
        biases(total, scale, old_bias, width_out, places[3], rows, fg, fu, lines),
    ]
    return large, small, lines


def write_net(side, own, other, fg, fu, slot, copy, grad):
    size = own.shape[1]
    whole = size // 2048

    def piece(at, row, width, count):
        mine = own[0:1, pl.ds(at, width)].reshape(count, width // count)
        theirs = other[0:1, pl.ds(at, width)].reshape(count, width // count)
        wide = width // count
        step = fu[pl.ds(row, count), 0:wide]
        online = jnp.where(side == 0, theirs, mine)
        new = online - LEARN_RATE * step
        held = jnp.where(side == 0, POLYAK_RATE * new + (1.0 - POLYAK_RATE) * mine, new)
        slot[0:1, pl.ds(at, width)] = held.reshape(1, width)
        copy[0:1, pl.ds(at, width)] = held.astype(BF16).reshape(1, width)
        grad[pl.ds(at, width)] = fg[pl.ds(row, count), 0:wide].reshape(width)

    for k in range(whole):
        piece(k * 2048, k * 16, 2048, 16)
    full = size // LANES
    for row in range(whole * 16, full):
        piece(row * LANES, row, LANES, 1)
    piece(full * LANES, full, size - full * LANES, 1)


def update_kernel(
    chunk, devices,
    meta, log_alpha, mine, theirs, own_a, other_a, own_c, other_c, stats_a, stats_c,
    slot_a, slot_c, copy_a, copy_c, grad_a, grad_c, new_a, new_c, summary, alpha_out,
    total, fg_a, fu_a, fg_c, fu_c,
):
    count = devices // 2
    for p in range(count):
        at = pl.multiple_of((meta[1] ^ p) * chunk, 8)
        total[pl.ds(at, chunk), :] = mine[p * chunk : (p + 1) * chunk, :]
        at = pl.multiple_of((meta[2] ^ p) * chunk, 8)
        total[pl.ds(at, chunk), :] = theirs[p * chunk : (p + 1) * chunk, :]

    sums = jnp.sum(total[EXTRA : EXTRA + 8, :], axis=1, keepdims=True)
    peak = jnp.max(total[EXTRA_SLOTS : EXTRA + 8, :], axis=1, keepdims=True)
    peak = jnp.max(peak, axis=0, keepdims=True)
    counted = sums[0:1, :]
    scale_a = 1.0 / counted
    scale_c = scale_a / peak
    lane = lanes_of(1)
    line = jnp.where(
        lane == 0,
        jnp.broadcast_to(sums[2:3, :] / peak, (1, LANES)),
        jnp.where(
            lane == 1,
            jnp.broadcast_to(sums[3:4, :], (1, LANES)),
            jnp.broadcast_to(counted, (1, LANES)),
        ),
    )
    summary[...] = line[:, 0:3].reshape(3)
    new_alpha = log_alpha[0] + ALPHA_STEP * (
        jnp.broadcast_to(sums[1:2, :] / counted, (1, LANES)) - ACT
    )
    alpha_out[...] = new_alpha[:, 0:1].reshape(1)
    large_a, small_a, lines_a = net_update(
        total, scale_a, stats_a, OBS, 2 * ACT, (A_W1, A_W2, A_W3, A_B), A_ROWS, fg_a, fu_a
    )
    large_c, small_c, lines_c = net_update(
        total, scale_c, stats_c, OBS + ACT, 2, (C_W1, C_W2, C_W3, C_B), C_ROWS, fg_c, fu_c
    )
    in_turn([large_a] + small_a)
    in_turn([large_c] + small_c)
    store_statistics(lines_a, OBS, 2 * ACT, new_a)
    store_statistics(lines_c, OBS + ACT, 2, new_c)
    write_net(meta[0], own_a, other_a, fg_a, fu_a, slot_a, copy_a, grad_a)
    write_net(meta[0], own_c, other_c, fg_c, fu_c, slot_c, copy_c, grad_c)


def update(meta, log_alpha, mine, theirs, own_a, other_a, own_c, other_c, stats_a, stats_c, sizes, devices):
    chunk = chunk_rows(devices)

    def body(*refs):
        update_kernel(chunk, devices, *refs)

    def f32(*shape):
        return jax.ShapeDtypeStruct(shape, F32)

    smem = pl.BlockSpec(memory_space=pltpu.SMEM)
    vmem = pl.BlockSpec(memory_space=pltpu.VMEM)
    return pl.pallas_call(
        body,
        out_shape=(
            f32(1, A_SIZE), f32(1, C_SIZE),
            jax.ShapeDtypeStruct((1, A_SIZE), BF16), jax.ShapeDtypeStruct((1, C_SIZE), BF16),
            f32(A_SIZE), f32(C_SIZE), f32(sizes[0]), f32(sizes[1]), f32(3), f32(1),
        ),
        in_specs=[smem, smem] + [vmem] * 8,
        out_specs=tuple([vmem] * 10),
        scratch_shapes=[
            pltpu.VMEM((chunk * devices, LANES), F32),
            pltpu.VMEM((A_FLAT, LANES), F32), pltpu.VMEM((A_FLAT, LANES), F32),
            pltpu.VMEM((C_FLAT, LANES), F32), pltpu.VMEM((C_FLAT, LANES), F32),
        ],
        compiler_params=pltpu.CompilerParams(vmem_limit_bytes=UPDATE_VMEM_BYTES),
        name="optimizer",
    )(meta, log_alpha, mine, theirs, own_a, other_a, own_c, other_c, stats_a, stats_c)


def chunk_rows(devices):
    return -(-DATA_ROWS // (8 * devices)) * 8


def stage_bits(count, group):
    number = count.bit_length() - 1
    bits = [(bit + 2 * group) % number for bit in range(number)]
    return [bits[k : k + 2] for k in range(0, number, 2)]


def swap_groups(value):
    return lax.ppermute(value, "grp", [(0, 1), (1, 0)])


def exchange(value, stage, digit):
    count = lax.axis_size("dp")
    pairs = []
    for group in (0, 1):
        bits = stage_bits(count, group)[stage]
        mask = sum(1 << bit for k, bit in enumerate(bits) if digit >> k & 1)
        pairs += [(group * count + i, group * count + (i ^ mask)) for i in range(count)]
    return lax.ppermute(value, ("grp", "dp"), pairs)


def buffer_place(group, count):
    index = lax.axis_index("dp")
    place = group
    for bits in stage_bits(count, group):
        for bit in reversed(bits):
            place = place * 2 + (index >> bit & 1)
    return place


def all_sum(keep, send):
    count = lax.axis_size("dp")
    sizes = [1 << len(bits) for bits in stage_bits(count, 0)]
    value = keep + swap_groups(send)
    for stage, size in enumerate(sizes):
        rows = value.shape[0] // size
        parts = [value[k * rows : (k + 1) * rows] for k in range(size)]
        came = [exchange(parts[k], stage, k) for k in range(1, size)]
        value = parts[0]
        for part in came:
            value = value + part
    for stage, size in reversed(list(enumerate(sizes))):
        value = jnp.concatenate(
            [value] + [exchange(value, stage, k) for k in range(1, size)], axis=0
        )
    return value, swap_groups(value)


def shards(
    obs_rows,
    next_rows,
    action_rows,
    reward_rows,
    batch_index,
    valid_mask,
    noise,
    importance,
    actor_params,
    critic_params,
    actor_stats,
    critic_stats,
    log_alpha,
):
    devices = lax.axis_size("dp") * lax.axis_size("grp")
    group_side = lax.axis_index("grp")
    other_a = swap_groups(actor_params)
    other_c = swap_groups(critic_params)
    places = [buffer_place(group, lax.axis_size("dp")) for group in (0, 1)]
    other_c, turn = lax.optimization_barrier((other_c, group_side))
    number = jnp.arange(3)
    meta = jnp.where((number == 1) == (turn == 0), places[0], places[1])
    meta = jnp.where(number == 0, turn, meta).astype(jnp.int32)
    row = lax.broadcasted_iota(jnp.int32, (8, batch_index.shape[0]), 0)
    misc = jnp.where(row == MISC_VALID, valid_mask[None], batch_index[None]).astype(F32)
    misc = jnp.where(row == MISC_WEIGHT, importance[None], misc)
    misc = jnp.where(row == 0, reward_rows[None], misc)
    keep, send = losses(
        meta, log_alpha, obs_rows.T, next_rows.T, action_rows.T, noise.T, misc,
        actor_params, other_a, critic_params, other_c, devices,
    )
    keep, send, actor_stats, critic_stats = lax.optimization_barrier(
        (keep, send, actor_stats, critic_stats)
    )
    mine, theirs = all_sum(keep, send)
    (
        slot_a, slot_c, copy_a, copy_c, grad_a, grad_c, new_a, new_c, summary, alpha
    ) = update(
        meta, log_alpha, mine, theirs, actor_params, other_a, critic_params, other_c,
        aligned_stats(actor_stats, OBS, 2 * ACT), aligned_stats(critic_stats, OBS + ACT, 2),
        (actor_stats.shape[0], critic_stats.shape[0]), devices,
    )
    return (
        slot_a, slot_c, copy_a, copy_c, grad_a, grad_c, new_a, new_c,
        summary, alpha,
    )


def solution(mesh):
    return jax.shard_map(
        shards,
        mesh=mesh,
        in_specs=(
            P("dp", None),
            P("dp", None),
            P("dp", None),
            P("dp"),
            P("dp"),
            P("dp"),
            P("dp", None),
            P("dp"),
            P("grp", None),
            P("grp", None),
            P(),
            P(),
            P(),
        ),
        out_specs=(
            P("grp", None),
            P("grp", None),
            P("grp", None),
            P("grp", None),
            P(),
            P(),
            P(),
            P(),
            P(),
            P(),
        ),
        check_vma=False,
    )
```
